32 devices in a mesh: dp: 32 (over z, y, x, core).
Axes of the slice: x: 2, y: 2, z: 4, core: 2. Of those that a mesh axis runs over, the one named last changes fastest.
Arguments:
- tokens: bfloat16 [32768, 768], P('dp'), may hold values from -6 to 6
- lengths: int32 [64], P('dp'), may hold values from 65 to 512, as said below
- partners: int32 [64], replicated, may hold values from 0 to 63, each once
- targets: float32 [64], P('dp'), may hold values from 0 to 1
- query_proj: bfloat16 [768, 768], replicated, may hold values from -0.21875 to 0.21875
- query_bias: float32 [768], replicated, may hold values from -0.6 to 0.6
- key_proj: bfloat16 [768, 768], replicated, may hold values from -0.21875 to 0.21875
- value_proj: bfloat16 [768, 768], replicated, may hold values from -0.21875 to 0.21875
- value_bias: float32 [768], replicated, may hold values from -0.6 to 0.6
- mixer_proj: bfloat16 [768, 768], replicated, may hold values from -0.875 to 0.875
- mixer_bias: float32 [768], replicated, may hold values from -0.3 to 0.3
- first_gain: float32 [768], replicated, may hold values from 0.5 to 1.5
- first_shift: float32 [768], replicated, may hold values from -0.3 to 0.3
- expand_proj: bfloat16 [768, 3072], replicated, may hold values from -0.21875 to 0.21875
- expand_bias: float32 [3072], replicated, may hold values from -0.6 to 0.6
- shrink_proj: bfloat16 [3072, 768], replicated, may hold values from -0.109375 to 0.109375
- shrink_bias: float32 [768], replicated, may hold values from -0.3 to 0.3
- second_gain: float32 [768], replicated, may hold values from 0.5 to 1.5
- second_shift: float32 [768], replicated, may hold values from -0.3 to 0.3
Outputs:
- pair_scores: float32 [64], P('dp')
- tokens_grad: float32 [32768, 768], P('dp')
- query_proj_grad: float32 [768, 768], replicated
- query_bias_grad: float32 [768], replicated
- key_proj_grad: float32 [768, 768], replicated
- value_proj_grad: float32 [768, 768], replicated
- value_bias_grad: float32 [768], replicated
- mixer_proj_grad: float32 [768, 768], replicated
- mixer_bias_grad: float32 [768], replicated
- first_gain_grad: float32 [768], replicated
- first_shift_grad: float32 [768], replicated
- expand_proj_grad: float32 [768, 3072], replicated
- expand_bias_grad: float32 [3072], replicated
- shrink_proj_grad: float32 [3072, 768], replicated
- shrink_bias_grad: float32 [768], replicated
- second_gain_grad: float32 [768], replicated
- second_shift_grad: float32 [768], replicated
The draws below stay inside these ranges and needn't reach their ends.
Inputs may be any that keep to these rules, and one draw needn't show every extreme that they name: `lengths`: the 2 sentences of one device share one bucket with most 128, 256 or 512, and each length is above half of its bucket's most; some sentence is exactly 512 long. `partners`: every sentence is the partner of exactly one sentence.
All inputs are finite; a program needn't handle non-finite values.
Results may differ from the reference program's by a relative error of at most 0.012.
Values sent between devices are 32-bit elements; how exact they have to be, the bound alone decides.
A program may use at most 192 MiB of HBM per device.

```python
import math
from functools import partial
import jax
import jax.numpy as jnp
from jax import lax

D = 768
H = 12
HD = 64
FF = 3072
SLOT = 512
SENT_DEV = 2
SENTS = 64
TOKENS = 32768


def draw_lengths(key, part):
    key = jax.random.fold_in(key, 11)
    first, second, third = jax.random.split(key, 3)
    owners = SENTS // SENT_DEV
    tier_dev = jax.random.randint(first, (owners,), 0, 4)
    tier = jnp.repeat(tier_dev, SENT_DEV)
    level = jnp.maximum(tier - 1, 0)
    most = jnp.where(level == 0, SLOT // 4, jnp.where(level == 1, SLOT // 2, SLOT))
    spread = jax.random.randint(second, (SENTS,), 0, 65536)
    lengths = most // 2 + 1 + spread % (most // 2)
    chosen_dev = jax.random.randint(third, (), 0, owners)
    in_chosen = jnp.arange(SENTS) // SENT_DEV == chosen_dev
    lengths = jnp.where(in_chosen, SLOT // 2 + 1 + spread % (SLOT // 2), lengths)
    lengths = jnp.where(jnp.arange(SENTS) == chosen_dev * SENT_DEV, SLOT, lengths)
    return lengths.astype(jnp.int32)


def levels(rng, shape, shards, smallest, largest):
    loudness, own = 1.0, jax.random.fold_in(rng, 6)
    for dim, shards_of in shards:
        draws = jnp.exp(jax.random.uniform(jax.random.fold_in(own, dim), (shards_of,), jnp.float32, smallest / len(shards), largest / len(shards)))
        loudness = loudness * jnp.repeat(draws, shape[dim] // shards_of).reshape([-1 if axis == dim else 1 for axis in range(len(shape))])
    return loudness


def bell_draw(own_key, extent, scale, reach, pieces=(), kind=jnp.bfloat16):
    array = scale * jax.random.normal(own_key, extent, jnp.float32)
    if pieces:
        array = array * levels(own_key, extent, pieces, -0.22, 0.18)
    return jnp.clip(array, -reach, reach).astype(kind)


def setup_inputs(seed: int = 0) -> dict:
    key_list = jax.random.split(jax.random.key(seed), 20)
    return {
        "tokens": bell_draw(key_list[0], (TOKENS, D), 1.0, 6.0, ((0, 32),)),
        "lengths": draw_lengths(jax.random.fold_in(key_list[19], 71), 0),
        "partners": jax.random.permutation(key_list[2], SENTS).astype(jnp.int32),
        "targets": jnp.clip(1.0 * jax.random.uniform(key_list[3], (SENTS,), jnp.float32) ** levels(key_list[3], (SENTS,), ((0, 32),), -0.2, 0.2), 0.0, 1.0),
        "query_proj": bell_draw(key_list[4], (D, D), D ** -0.5, 0.21875),
        "query_bias": bell_draw(key_list[5], (D,), 0.1, 0.6, (), jnp.float32),
        "key_proj": bell_draw(key_list[6], (D, D), D ** -0.5, 0.21875),
        "value_proj": bell_draw(key_list[7], (D, D), D ** -0.5, 0.21875),
        "value_bias": bell_draw(key_list[8], (D,), 0.1, 0.6, (), jnp.float32),
        "mixer_proj": bell_draw(key_list[9], (D, D), (D // 16) ** -0.5, 0.875),
        "mixer_bias": bell_draw(key_list[10], (D,), 0.05, 0.3, (), jnp.float32),
        "first_gain": jnp.clip(1.0 + 0.1 * jax.random.normal(key_list[11], (D,), jnp.float32), 0.5, 1.5),
        "first_shift": bell_draw(key_list[12], (D,), 0.05, 0.3, (), jnp.float32),
        "expand_proj": bell_draw(key_list[13], (D, FF), D ** -0.5, 0.21875),
        "expand_bias": bell_draw(key_list[14], (FF,), 0.1, 0.6, (), jnp.float32),
        "shrink_proj": bell_draw(key_list[15], (FF, D), FF ** -0.5, 0.109375),
        "shrink_bias": bell_draw(key_list[16], (D,), 0.05, 0.3, (), jnp.float32),
        "second_gain": jnp.clip(1.0 + 0.1 * jax.random.normal(key_list[17], (D,), jnp.float32), 0.5, 1.5),
        "second_shift": bell_draw(key_list[18], (D,), 0.05, 0.3, (), jnp.float32),
    }


@jax.custom_vjp
def low(v):
    return lax.optimization_barrier(v.astype(jnp.bfloat16)).astype(jnp.float32)

@jax.custom_vjp
def low_back(v):
    return v

def low_keep(v):
    return (low(v), None)

def low_pass(kept, grad):
    return (grad,)

def back_keep(v):
    return (v, None)

def back_low(kept, grad):
    return (low(grad),)
low.defvjp(low_keep, low_pass)
low_back.defvjp(back_keep, back_low)

def both(v):
    return low(low_back(v))

def norm_rows(rows, gain, shift):
    mean = lax.optimization_barrier(jnp.mean(rows, axis=-1, keepdims=True))
    centred = rows - mean
    spread = lax.optimization_barrier(jnp.mean(centred * centred, axis=-1, keepdims=True))
    return centred * lax.rsqrt(spread + 1e-06) * gain + shift

def encode_group(weights, item):
    query_proj, query_bias, key_proj, value_proj, value_bias, mixer_proj, mixer_bias, first_gain, first_shift, expand_proj, expand_bias, shrink_proj, shrink_bias, second_gain, second_shift = weights
    block, counts = item
    group = block.shape[0]
    highest = lax.Precision.HIGHEST
    rows = block.reshape(group * SLOT, D)
    queries = both(jnp.dot(rows, query_proj, precision=highest) + query_bias).reshape(group, SLOT, H, HD)
    keys = both(jnp.dot(rows, key_proj, precision=highest)).reshape(group, SLOT, H, HD)
    values = both(jnp.dot(rows, value_proj, precision=highest) + value_bias).reshape(group, SLOT, H, HD)
    scale = 1.0 / math.sqrt(HD)
    valid = jnp.arange(SLOT, dtype=jnp.int32)[None, :] < counts[:, None]
    scores = low_back(jnp.einsum('gqhd,gkhd->ghqk', queries, keys, precision=highest) * scale)
    scores = jnp.where(valid[:, None, None, :], scores, -1000000000.0)
    probs = low(jax.nn.softmax(scores, axis=-1))
    mixed = both(jnp.einsum('ghqk,gkhd->gqhd', probs, values, precision=highest).reshape(group * SLOT, D))
    branch = low_back(jnp.dot(mixed, mixer_proj, precision=highest) + mixer_bias)
    first_out = norm_rows(rows + branch, first_gain, first_shift)
    pre = low_back(jnp.dot(low(first_out), expand_proj, precision=highest) + expand_bias)
    act = low(jax.nn.gelu(pre, approximate=False))
    shrink = low_back(jnp.dot(act, shrink_proj, precision=highest) + shrink_bias)
    outputs = norm_rows(first_out + shrink, second_gain, second_shift).reshape(group, SLOT, D)
    masked = jnp.where(valid[:, :, None], outputs, 0.0)
    return lax.optimization_barrier(jnp.sum(masked, axis=1)) / counts[:, None].astype(jnp.float32)

def pair_scores_of(rows, lengths, partners, weights):
    group = 8 if SENTS % 8 == 0 else 1
    blocks = rows.reshape(SENTS // group, group, SLOT, D)
    counts = lengths.reshape(SENTS // group, group)
    step = jax.checkpoint(partial(encode_group, weights))
    pooled = lax.map(step, (blocks, counts)).reshape(SENTS, D)
    partner_vec = pooled[partners]
    inner = lax.optimization_barrier(jnp.sum(pooled * partner_vec, axis=-1))
    own_len = jnp.sqrt(lax.optimization_barrier(jnp.sum(pooled * pooled, axis=-1)) + 1e-06)
    far_len = jnp.sqrt(lax.optimization_barrier(jnp.sum(partner_vec * partner_vec, axis=-1)) + 1e-06)
    return inner / (own_len * far_len)

def reference(tokens, lengths, partners, targets, query_proj, query_bias, key_proj, value_proj, value_bias, mixer_proj, mixer_bias, first_gain, first_shift, expand_proj, expand_bias, shrink_proj, shrink_bias, second_gain, second_shift):
    weights = tuple((w.astype(jnp.float32) for w in (query_proj, query_bias, key_proj, value_proj, value_bias, mixer_proj, mixer_bias, first_gain, first_shift, expand_proj, expand_bias, shrink_proj, shrink_bias, second_gain, second_shift)))

    def forward(rows, *params):
        return pair_scores_of(rows, lengths, partners, params)
    scores, pull = jax.vjp(forward, tokens.astype(jnp.float32), *weights)
    grads = pull(scores - targets)
    return (scores, grads[0], grads[1], grads[2], grads[3], grads[4], grads[5], grads[6], grads[7], grads[8], grads[9], grads[10], grads[11], grads[12], grads[13], grads[14], grads[15])
```

```python
from functools import partial
import math

import jax
import jax.numpy as jnp
from jax import lax
from jax.sharding import PartitionSpec as P

from jax.experimental import pallas as pl
from jax.experimental.pallas import tpu as pltpu

H = 12

MESH = pl.DeviceIdType.MESH
F32 = jnp.float32
BF = jnp.bfloat16


def rows16(index):
    return pl.ds(pl.multiple_of(index * 16, 16), 16)


def rows_at(start, size):
    return pl.ds(pl.multiple_of(start, 8), size)


def lanes_at(start, size):
    return pl.ds(pl.multiple_of(start, 128), size)


class Place:
    def __init__(self):
        me = lax.axis_index("dp")
        self.me = me
        self.c = me % 2
        self.x = (me // 2) % 2
        self.y = (me // 4) % 2
        self.z = me // 8
        self.sibling = me + 1 - 2 * self.c
        self.to_x = me + 2 - 4 * self.x
        self.to_y = me + 4 - 8 * self.y
        self.up = me + 8
        self.down = me - 8


def stream_scratch():
    return [
        pltpu.VMEM((2, 64, 768), F32),
        pltpu.VMEM((144, 128), F32),
        pltpu.VMEM((2, 144, 128), F32),
        pltpu.VMEM((144, 128), F32),
        pltpu.VMEM((2, 144, 128), F32),
        pltpu.VMEM((72, 128), F32),
        pltpu.VMEM((2, 72, 128), F32),
        pltpu.VMEM((72, 128), F32),
        pltpu.VMEM((2, 72, 128), F32),
        pltpu.VMEM((2, 192, 128), F32),
        pltpu.VMEM((2, 2, 192, 128), F32),
        pltpu.VMEM((128, 128), F32),
        pltpu.VMEM((64, 128), F32),
        pltpu.VMEM((4, 64, 128), F32),
        pltpu.VMEM((4, 128, 128), F32),
        pltpu.VMEM((16, 128), F32),
        pltpu.VMEM((8, 128), F32),
        pltpu.VMEM((8, 64, 768), F32),
        pltpu.SemaphoreType.DMA((10, 2)),
        pltpu.SemaphoreType.DMA((10, 2)),
        pltpu.SemaphoreType.DMA((2,)),
    ]


N_STREAM_SCRATCH = 21


class Stream:
    def __init__(self, place, which, count, refs, grad_ref, grad_rows, out_ref, out_rows):
        (self.sib_in, self.a_rs_out, self.a_rs_in, self.a_ag_out, self.a_ag_in, self.b_rs_out, self.b_rs_in,
         self.b_ag_out, self.b_ag_in, self.z_out, self.z_in, self.p1, self.p2, self.p3, self.q1, self.q2, self.q3,
         self.full, self.sent, self.came, self.kept) = refs
        self.place = place
        self.count = count
        self.grad_ref = grad_ref
        self.grad_rows = grad_rows
        self.out_ref = out_ref
        self.out_rows = out_rows
        if which == 0:
            self.d1, self.d2, self.to_a, self.to_b = place.x, place.y, place.to_x, place.to_y
        else:
            self.d1, self.d2, self.to_a, self.to_b = place.y, place.x, place.to_y, place.to_x

    def prepare(self):
        zero = jnp.zeros((192, 128), F32)
        for side in range(2):
            for parity in range(2):
                self.z_in[side, parity] = zero

    def copies(self, t):
        place, n = self.place, self.count
        par = t % 2
        never = t < 0

        def remote(i, src, dst, target):
            return pltpu.make_async_remote_copy(
                src_ref=src, dst_ref=dst, send_sem=self.sent.at[i, par], recv_sem=self.came.at[i, par],
                device_id=(target,), device_id_type=MESH)

        slot, row = self.grad_rows(t)
        other = rows_at(row + 64 * (1 - place.c), 64)
        m = t - 11
        ring = lax.rem(t + 5, 8)
        out_row = self.out_rows(m)
        mine = rows_at(out_row + 64 * place.c, 64)
        lead = (place.z, 3 - place.z)
        zs = []
        for side, device in ((0, place.up), (1, place.down)):
            for half, when in ((0, (t >= 1) & (t < n + 5)), (1, (t >= 6) & (t < n + 10))):
                for k in range(3):
                    at, size = (0, 144 - 48 * k) if half == 0 else (144 - 48 * k, 48 + 48 * k)
                    spot = pl.ds(at, size)
                    copy = remote(5 + 2 * side + half, self.z_out.at[side, spot], self.z_in.at[side, par, spot], device)
                    zs.append((copy, when, lead[side] == k, lead[side] == k + 1))
        return [
            (remote(0, self.grad_ref.at[slot, other], self.sib_in.at[par], place.sibling), (t >= 0) & (t < n), True, True),
            (remote(1, self.a_rs_out, self.a_rs_in.at[par], self.to_a), (t >= 1) & (t < n + 4), True, True),
            (remote(2, self.a_ag_out, self.a_ag_in.at[par], self.to_a), (t >= 7) & (t < n + 10), True, True),
            (remote(3, self.b_rs_out, self.b_rs_in.at[par], self.to_b), (t >= 2) & (t < n + 5), True, True),
            (remote(4, self.b_ag_out, self.b_ag_in.at[par], self.to_b), (t >= 6) & (t < n + 9), True, True),
            (remote(9, self.full.at[ring], self.out_ref.at[mine], place.sibling), (t >= 11) & (t < n + 11), True, True),
        ] + zs, (pltpu.make_async_copy(self.full.at[ring], self.out_ref.at[mine], self.kept.at[par]), (t >= 11) & (t < n + 11))

    def start(self, t):
        remote, (local, live) = self.copies(t)
        for copy, when, sends, _ in remote:
            pl.when(when if sends is True else when & sends)(copy.start)
        pl.when(live)(local.start)

    def wait(self, t):
        remote, (local, live) = self.copies(t)
        for copy, when, sends, takes in remote:
            if sends is True:
                @pl.when(when)
                def _(copy=copy):
                    copy.wait_send()
                    copy.wait_recv()
            else:
                pl.when(when & sends)(copy.wait_send)
                pl.when(when & takes)(copy.wait_recv)
        pl.when(live)(local.wait)

    def work(self, t):
        place = self.place
        z, d1, d2 = place.z, self.d1, self.d2
        par = (t + 1) % 2
        z_in, z_out = self.z_in, self.z_out
        lead = (z, 3 - z)

        def far(side, k):
            return z - k if side == 0 else z + k

        def target(side, step):
            return z + 4 - step if side == 0 else z - 4 + step

        def ring4(stage):
            return lax.rem(t + 16 - stage, 4)

        def ring8(stage):
            return lax.rem(t + 16 - stage, 8)

        def got_p(side, pos):
            return z_in[side, par, 48 * pos:48 * pos + 16, :]

        def got_q(side, pos, panel):
            at = 48 * pos + 16 + 16 * panel
            return z_in[side, par, at:at + 16, :]

        def put_p(side, pos, value):
            z_out[side, 48 * pos:48 * pos + 16, :] = value

        def put_q(side, pos, panel, value):
            at = 48 * pos + 16 + 16 * panel
            z_out[side, at:at + 16, :] = value

        def full_p(ring, block, value):
            self.full[ring, rows16(block), lanes_at((2 * d1 + d2) * 128, 128)] = value

        def full_q(ring, block, panel, value):
            self.full[ring, rows16(block), 512 + 128 * panel:640 + 128 * panel] = value

        @pl.when((t >= 11) & (t < self.count + 11))
        def _stage11():
            ring = ring8(11)
            self.full[ring, :, lanes_at((1 - d1) * 256, 128)] = self.a_ag_in[par, 0:64, :]
            self.full[ring, :, lanes_at((1 - d1) * 256 + 128, 128)] = self.a_ag_in[par, 64:128, :]
            for side in range(2):
                @pl.when(lead[side] == 3)
                def _(side=side, ring=ring):
                    for panel in range(2):
                        full_q(ring, far(side, 3), panel, got_q(side, 1, panel))

        @pl.when((t >= 10) & (t < self.count + 10))
        def _stage10():
            ring = ring8(10)
            other = self.b_ag_in[par, 0:64, :]
            self.full[ring, :, lanes_at((2 * d1 + 1 - d2) * 128, 128)] = other
            self.a_ag_out[rows_at(64 * (1 - d2), 64), :] = other
            self.a_ag_out[rows_at(64 * d2, 64), :] = self.full[ring, :, lanes_at((2 * d1 + d2) * 128, 128)]
            for side in range(2):
                @pl.when(lead[side] >= 2)
                def _(side=side, ring=ring):
                    for panel in range(2):
                        value = got_q(side, 2, panel)
                        full_q(ring, far(side, 2), panel, value)
                        put_q(side, 1, panel, value)

        @pl.when((t >= 9) & (t < self.count + 9))
        def _stage9():
            ring = ring8(9)
            for side in range(2):
                @pl.when(lead[side] == 3)
                def _(side=side, ring=ring):
                    full_p(ring, far(side, 3), got_p(side, 1))

                @pl.when(lead[side] >= 1)
                def _(side=side, ring=ring):
                    for panel in range(2):
                        value = got_q(side, 3, panel)
                        full_q(ring, far(side, 1), panel, value)
                        put_q(side, 2, panel, value)
            self.b_ag_out[0:64, :] = self.full[ring, :, lanes_at((2 * d1 + d2) * 128, 128)]

        @pl.when((t >= 8) & (t < self.count + 8))
        def _stage8():
            ring = ring8(8)
            for side in range(2):
                @pl.when(lead[side] >= 2)
                def _(side=side, ring=ring):
                    value = got_p(side, 2)
                    full_p(ring, far(side, 2), value)
                    put_p(side, 1, value)
            self.full[ring, rows16(z), lanes_at(512 + 128 * (1 - d1), 128)] = self.a_ag_in[par, 128:144, :]
            for panel in range(2):
                value = self.full[ring, rows16(z), 512 + 128 * panel:640 + 128 * panel]
                for side in range(2):
                    put_q(side, 3, panel, value)

        @pl.when((t >= 7) & (t < self.count + 7))
        def _stage7():
            ring = ring8(7)
            for side in range(2):
                @pl.when(lead[side] >= 1)
                def _(side=side, ring=ring):
                    value = got_p(side, 3)
                    full_p(ring, far(side, 1), value)
                    put_p(side, 2, value)
            self.full[ring, rows_at(16 * z + 8 * (1 - d2), 8), lanes_at(512 + 128 * d1, 128)] = self.b_ag_in[par, 64:72, :]
            self.a_ag_out[128:144, :] = self.full[ring, rows16(z), lanes_at(512 + 128 * d1, 128)]

        @pl.when((t >= 6) & (t < self.count + 6))
        def _stage6():
            ring = ring8(6)
            value = self.p3[ring4(6), rows16(z), :] + got_p(0, 0) + got_p(1, 0)
            full_p(ring, z, value)
            put_p(0, 3, value)
            put_p(1, 3, value)
            value = self.q3[...] + self.b_rs_in[par, 64:72, :]
            self.full[ring, rows_at(16 * z + 8 * d2, 8), lanes_at(512 + 128 * d1, 128)] = value
            self.b_ag_out[64:72, :] = value

        @pl.when((t >= 5) & (t < self.count + 5))
        def _stage5():
            for side in range(2):
                @pl.when(lead[side] <= 2)
                def _(side=side):
                    put_p(side, 0, self.p3[ring4(5), rows16(target(side, 3)), :] + got_p(side, 1))
            self.q3[...] = self.q2[rows_at(8 * d2, 8), :] + self.a_rs_in[par, rows_at(128 + 8 * d2, 8), :]
            self.b_rs_out[64:72, :] = self.q2[rows_at(8 * (1 - d2), 8), :] + self.a_rs_in[par, rows_at(128 + 8 * (1 - d2), 8), :]

        @pl.when((t >= 4) & (t < self.count + 4))
        def _stage4():
            for side in range(2):
                @pl.when(lead[side] <= 1)
                def _(side=side):
                    put_p(side, 1, self.p3[ring4(4), rows16(target(side, 2)), :] + got_p(side, 2))
            ring = ring4(4)

            def own_q(panel):
                first = self.q1[ring, rows_at(64 * panel + 16 * z, 16), :]
                spot = rows_at(16 + 16 * panel, 16)
                return first + z_in[0, par, spot, :] + z_in[1, par, spot, :]

            self.q2[...] = own_q(d1)
            self.a_rs_out[128:144, :] = own_q(1 - d1)

        @pl.when((t >= 3) & (t < self.count + 3))
        def _stage3():
            for side in range(2):
                @pl.when(lead[side] <= 2)
                def _(side=side):
                    for panel in range(2):
                        own = self.q1[ring4(3), rows_at(64 * panel + 16 * target(side, 3), 16), :]
                        put_q(side, 0, panel, own + got_q(side, 1, panel))
            ring = ring4(3)
            self.p3[ring] = self.p2[...] + self.b_rs_in[par, 0:64, :]
            for side in range(2):
                @pl.when(lead[side] == 0)
                def _(side=side, ring=ring):
                    put_p(side, 2, self.p3[ring, rows16(target(side, 1)), :])

        @pl.when((t >= 2) & (t < self.count + 2))
        def _stage2():
            for side in range(2):
                @pl.when(lead[side] <= 1)
                def _(side=side):
                    for panel in range(2):
                        own = self.q1[ring4(2), rows_at(64 * panel + 16 * target(side, 2), 16), :]
                        put_q(side, 1, panel, own + got_q(side, 2, panel))
            self.p2[...] = self.p1[rows_at(64 * d2, 64), :] + self.a_rs_in[par, rows_at(64 * d2, 64), :]
            self.b_rs_out[0:64, :] = self.p1[rows_at(64 * (1 - d2), 64), :] + self.a_rs_in[par, rows_at(64 * (1 - d2), 64), :]

        @pl.when((t >= 1) & (t < self.count + 1))
        def _stage1():
            slot, row = self.grad_rows(t - 1)
            mine = rows_at(row + 64 * place.c, 64)

            def summed(lane):
                spot = lanes_at(lane, 128)
                return self.grad_ref[slot, mine, spot] + self.sib_in[par, :, spot]

            for half in range(2):
                self.p1[64 * half:64 * half + 64, :] = summed(256 * d1 + 128 * half)
                self.a_rs_out[64 * half:64 * half + 64, :] = summed(256 * (1 - d1) + 128 * half)
            ring = ring4(1)
            for panel in range(2):
                self.q1[ring, 64 * panel:64 * panel + 64, :] = summed(512 + 128 * panel)
            for side in range(2):
                @pl.when(lead[side] == 0)
                def _(side=side, ring=ring):
                    for panel in range(2):
                        put_q(side, 2, panel, self.q1[ring, rows_at(64 * panel + 16 * target(side, 1), 16), :])


def greet_neighbours(place):
    bar = pltpu.get_barrier_semaphore()

    def hail(device):
        pl.semaphore_signal(bar, 1, device_id=(device,), device_id_type=MESH)

    hail(place.sibling)
    hail(place.to_x)
    hail(place.to_y)
    pl.when(place.z < 3)(lambda: hail(place.up))
    pl.when(place.z > 0)(lambda: hail(place.down))
    ends = jnp.where(place.z == 0, 1, 0) + jnp.where(place.z == 3, 1, 0)
    pl.semaphore_wait(bar, 5 - ends)


def sum_kernel(g_ref, s_ref, o_ref, ring, loaded, *rest):
    place = Place()
    first, second = rest[:N_STREAM_SCRATCH], rest[N_STREAM_SCRATCH:]

    def load(b):
        slot = lax.rem(b, 2)
        return pltpu.make_async_copy(g_ref.at[b], ring.at[slot], loaded.at[slot])

    def chunk_rows(t, shift):
        t = jnp.clip(t, 0, 36)
        return lax.rem(t // 3, 2), lax.rem(t, 3) * 256 + shift

    def out_rows(t, shift):
        return jnp.clip(t, 0, 36) * 256 + shift

    one = Stream(place, 0, 37, first, ring, lambda t: chunk_rows(t, 0), o_ref, lambda t: out_rows(t, 0))
    two = Stream(place, 1, 36, second, ring, lambda t: chunk_rows(t, 128), o_ref, lambda t: out_rows(t, 128))
    one.prepare()
    two.prepare()
    greet_neighbours(place)
    load(jnp.int32(0)).start()

    def step(t, carry):
        b = t // 3

        @pl.when((lax.rem(t, 3) == 0) & (b < 12))
        def _():
            load(b).wait()

        @pl.when(t == 36)
        def _():
            ring[0, 0:128, :] = s_ref[...]

        for stream in (one, two):
            stream.wait(t - 1)
            stream.work(t)
            stream.start(t)

        @pl.when((lax.rem(t, 3) == 1) & (b + 1 < 12))
        def _():
            load(b + 1).start()

        return carry

    lax.fori_loop(0, 49, step, 0)


def sum_over_all(matrices, vectors):
    small = jnp.pad(vectors, ((0, 116), (0, 0)))
    return pl.pallas_call(
        sum_kernel,
        out_shape=jax.ShapeDtypeStruct((37 * 256 - 128, 768), F32),
        in_specs=[pl.BlockSpec(memory_space=pl.ANY), pl.BlockSpec(memory_space=pltpu.VMEM)],
        out_specs=pl.BlockSpec(memory_space=pl.ANY),
        scratch_shapes=[pltpu.VMEM((2, 768, 768), F32), pltpu.SemaphoreType.DMA((2,))]
        + stream_scratch() + stream_scratch(),
        compiler_params=pltpu.CompilerParams(
            collective_id=0, has_side_effects=True, vmem_limit_bytes=48 << 20),
    )(matrices, small)


def to_low(value):
    return value.astype(jnp.bfloat16)


def tdot(left, right):
    return lax.dot_general(
        left, right, (((0,), (0,)), ((), ())), preferred_element_type=jnp.float32
    )


def ndot(left, right):
    return lax.dot_general(
        left, right, (((1,), (1,)), ((), ())), preferred_element_type=jnp.float32
    )


def norm_rows(rows, gain, shift):
    mean = jnp.mean(rows, axis=-1, keepdims=True)
    centred = rows - mean
    spread = jnp.mean(centred * centred, axis=-1, keepdims=True)
    inverse = lax.rsqrt(spread + 1e-06)
    normed = centred * inverse
    return (normed * gain + shift, normed, inverse)


def norm_back(upstream, normed, inverse, gain):
    gain_grad = jnp.sum(upstream * normed, axis=0)
    shift_grad = jnp.sum(upstream, axis=0)
    dnormed = upstream * gain
    first_mean = jnp.mean(dnormed, axis=-1, keepdims=True)
    second_mean = jnp.mean(dnormed * normed, axis=-1, keepdims=True)
    return (inverse * (dnormed - first_mean - normed * second_mean), gain_grad, shift_grad)


def per_device(
    tokens,
    lengths,
    partners,
    targets,
    query_proj,
    query_bias,
    key_proj,
    value_proj,
    value_bias,
    mixer_proj,
    mixer_bias,
    first_gain,
    first_shift,
    expand_proj,
    expand_bias,
    shrink_proj,
    shrink_bias,
    second_gain,
    second_shift,
    devices,
):
    sents = lengths.shape[0]
    rows_all = tokens.shape[0]
    slot = rows_all // sents
    width = tokens.shape[1]
    heads = H
    depth = width // heads
    scale = 1.0 / math.sqrt(depth)
    total = partners.shape[0]
    base = lax.axis_index("dp") * sents
    highest = lax.Precision.HIGHEST
    places = jnp.arange(slot, dtype=jnp.int32)
    valid = places[None, :] < lengths[:, None]
    row_mask = valid.reshape(rows_all, 1).astype(jnp.float32)
    shape4 = (sents, slot, heads, depth)
    queries = to_low(jnp.dot(tokens, query_proj, preferred_element_type=jnp.float32) + query_bias)
    keys = to_low(jnp.dot(tokens, key_proj, preferred_element_type=jnp.float32))
    values = to_low(jnp.dot(tokens, value_proj, preferred_element_type=jnp.float32) + value_bias)
    queries4 = queries.reshape(shape4)
    keys4 = keys.reshape(shape4)
    values4 = values.reshape(shape4)

    def masked_scores(query_rows, key_rows, live):
        raw = (
            jnp.einsum("qhd,khd->hqk", query_rows, key_rows, preferred_element_type=jnp.float32)
            * scale
        )
        return jnp.where(live[None, None, :], raw, -1000000000.0)

    def attend(item):
        query_rows, key_rows, value_rows, live = item
        raw = masked_scores(query_rows, key_rows, live)
        top = jnp.max(raw, axis=-1, keepdims=True)
        expd = jnp.exp(raw - top)
        summed = jnp.sum(expd, axis=-1, keepdims=True)
        probs = to_low(expd / summed)
        mixed = jnp.einsum("hqk,khd->qhd", probs, value_rows, preferred_element_type=jnp.float32)
        return (mixed, (top + jnp.log(summed))[..., 0])

    mixed, logsum = lax.map(attend, (queries4, keys4, values4, valid))
    mixed_low = to_low(mixed.reshape(rows_all, width))
    branch = jnp.dot(mixed_low, mixer_proj, preferred_element_type=jnp.float32) + mixer_bias
    first_out, first_normed, first_inverse = norm_rows(
        tokens.astype(jnp.float32) + branch, first_gain, first_shift
    )
    first_low = to_low(first_out)
    pre = jnp.dot(first_low, expand_proj, preferred_element_type=jnp.float32) + expand_bias
    act, gelu_back = jax.vjp(partial(jax.nn.gelu, approximate=False), pre)
    act_low = to_low(act)
    shrink = jnp.dot(act_low, shrink_proj, preferred_element_type=jnp.float32) + shrink_bias
    outputs, second_normed, second_inverse = norm_rows(
        first_out + shrink, second_gain, second_shift
    )
    counts = lengths.astype(jnp.float32)
    pooled = jnp.sum((outputs * row_mask).reshape(sents, slot, width), axis=1) / counts[:, None]
    mine = lax.dynamic_slice_in_dim(partners, base, sents)
    every = lax.all_gather(pooled, "dp", axis=0, tiled=True)
    partner_vec = jnp.take(every, mine, axis=0)
    inner = jnp.sum(pooled * partner_vec, axis=-1)
    own_len = jnp.sqrt(jnp.sum(pooled * pooled, axis=-1) + 1e-06)
    far_len = jnp.sqrt(jnp.sum(partner_vec * partner_vec, axis=-1) + 1e-06)
    pair_scores = inner / (own_len * far_len)
    miss = pair_scores - targets
    joint = (own_len * far_len)[:, None]
    dpooled = miss[:, None] * (
        partner_vec / joint - (pair_scores / (own_len * own_len))[:, None] * pooled
    )
    dpartner = miss[:, None] * (
        pooled / joint - (pair_scores / (far_len * far_len))[:, None] * partner_vec
    )
    owners = (mine[:, None] == jnp.arange(total, dtype=jnp.int32)[None, :]).astype(jnp.float32)
    spread = lax.dot_general(owners, dpartner, (((0,), (0,)), ((), ())), precision=highest)
    returned = lax.psum_scatter(spread, "dp", scatter_dimension=0, tiled=True)
    dpool_all = (dpooled + returned) / counts[:, None]
    doutputs = (dpool_all[:, None, :] * valid[:, :, None].astype(jnp.float32)).reshape(
        rows_all, width
    )
    dsecond, second_gain_grad, second_shift_grad = norm_back(
        doutputs, second_normed, second_inverse, second_gain
    )
    dshrink = to_low(dsecond)
    shrink_proj_grad = tdot(act_low, dshrink)
    shrink_bias_grad = jnp.sum(dshrink.astype(jnp.float32), axis=0)
    dact = ndot(dshrink, shrink_proj)
    dpre = to_low(gelu_back(dact)[0])
    expand_proj_grad = tdot(first_low, dpre)
    expand_bias_grad = jnp.sum(dpre.astype(jnp.float32), axis=0)
    dfirst_out = ndot(dpre, expand_proj) + dsecond
    dfirst, first_gain_grad, first_shift_grad = norm_back(
        dfirst_out, first_normed, first_inverse, first_gain
    )
    dbranch = to_low(dfirst)
    mixer_proj_grad = tdot(mixed_low, dbranch)
    mixer_bias_grad = jnp.sum(dbranch.astype(jnp.float32), axis=0)
    dmixed = to_low(ndot(dbranch, mixer_proj)).reshape(shape4)

    def attend_back(item):
        query_rows, key_rows, value_rows, live, row_logsum, dmix = item
        raw = masked_scores(query_rows, key_rows, live)
        probs = jnp.exp(raw - row_logsum[..., None])
        probs_low = to_low(probs)
        dprob = jnp.einsum("qhd,khd->hqk", dmix, value_rows, preferred_element_type=jnp.float32)
        delta = jnp.sum(dprob * probs, axis=-1, keepdims=True)
        dscore = to_low(probs * (dprob - delta))
        dquery = (
            jnp.einsum("hqk,khd->qhd", dscore, key_rows, preferred_element_type=jnp.float32) * scale
        )
        dkey = (
            jnp.einsum("hqk,qhd->khd", dscore, query_rows, preferred_element_type=jnp.float32)
            * scale
        )
        dvalue = jnp.einsum("hqk,qhd->khd", probs_low, dmix, preferred_element_type=jnp.float32)
        return (to_low(dquery), to_low(dkey), to_low(dvalue))

    dquery, dkey, dvalue = lax.map(attend_back, (queries4, keys4, values4, valid, logsum, dmixed))
    dquery = dquery.reshape(rows_all, width)
    dkey = dkey.reshape(rows_all, width)
    dvalue = dvalue.reshape(rows_all, width)
    query_proj_grad = tdot(tokens, dquery)
    query_bias_grad = jnp.sum(dquery.astype(jnp.float32), axis=0)
    key_proj_grad = tdot(tokens, dkey)
    value_proj_grad = tdot(tokens, dvalue)
    value_bias_grad = jnp.sum(dvalue.astype(jnp.float32), axis=0)
    tokens_grad = (
        ndot(dquery, query_proj) + ndot(dkey, key_proj) + ndot(dvalue, value_proj) + dfirst
    )
    if devices == 32 and width == 768 and expand_proj.shape[1] == 4 * width:
        matrices = jnp.concatenate([
            shrink_proj_grad.reshape(4, width, width),
            expand_proj_grad.reshape(width, 4, width).transpose(1, 0, 2),
            mixer_proj_grad[None], query_proj_grad[None], key_proj_grad[None], value_proj_grad[None]])
        vectors = jnp.concatenate([
            query_bias_grad, value_bias_grad, mixer_bias_grad, first_gain_grad, first_shift_grad,
            shrink_bias_grad, second_gain_grad, second_shift_grad, expand_bias_grad]).reshape(12, width)
        summed = sum_over_all(matrices, vectors)
        blocks = summed[:12 * width].reshape(12, width, width)
        small = summed[12 * width:12 * width + 12]
        shrink_proj_grad = summed[:4 * width]
        expand_proj_grad = blocks[4:8].transpose(1, 0, 2).reshape(width, 4 * width)
        mixer_proj_grad, query_proj_grad, key_proj_grad, value_proj_grad = blocks[8], blocks[9], blocks[10], blocks[11]
        (query_bias_grad, value_bias_grad, mixer_bias_grad, first_gain_grad, first_shift_grad,
         shrink_bias_grad, second_gain_grad, second_shift_grad) = [small[i] for i in range(8)]
        expand_bias_grad = small[8:].reshape(4 * width)
    else:
        (
            query_proj_grad,
            query_bias_grad,
            key_proj_grad,
            value_proj_grad,
            value_bias_grad,
            mixer_proj_grad,
            mixer_bias_grad,
            first_gain_grad,
            first_shift_grad,
            expand_proj_grad,
            expand_bias_grad,
            shrink_proj_grad,
            shrink_bias_grad,
            second_gain_grad,
            second_shift_grad,
        ) = lax.psum(
            (
                query_proj_grad,
                query_bias_grad,
                key_proj_grad,
                value_proj_grad,
                value_bias_grad,
                mixer_proj_grad,
                mixer_bias_grad,
                first_gain_grad,
                first_shift_grad,
                expand_proj_grad,
                expand_bias_grad,
                shrink_proj_grad,
                shrink_bias_grad,
                second_gain_grad,
                second_shift_grad,
            ),
            "dp",
        )
    return (
        pair_scores,
        tokens_grad,
        query_proj_grad,
        query_bias_grad,
        key_proj_grad,
        value_proj_grad,
        value_bias_grad,
        mixer_proj_grad,
        mixer_bias_grad,
        first_gain_grad,
        first_shift_grad,
        expand_proj_grad,
        expand_bias_grad,
        shrink_proj_grad,
        shrink_bias_grad,
        second_gain_grad,
        second_shift_grad,
    )


def solution(mesh):
    in_specs = (
        P("dp", None),
        P("dp"),
        P(),
        P("dp"),
        P(),
        P(),
        P(),
        P(),
        P(),
        P(),
        P(),
        P(),
        P(),
        P(),
        P(),
        P(),
        P(),
        P(),
        P(),
    )
    out_specs = (
        P("dp"),
        P("dp", None),
        P(),
        P(),
        P(),
        P(),
        P(),
        P(),
        P(),
        P(),
        P(),
        P(),
        P(),
        P(),
        P(),
        P(),
        P(),
    )
    return jax.shard_map(
        partial(per_device, devices=mesh.shape["dp"]), mesh=mesh, in_specs=in_specs, out_specs=out_specs, check_vma=False
    )
```

```python
from functools import partial
import math

import jax
import jax.numpy as jnp
from jax import lax
from jax.sharding import PartitionSpec as P

from jax.experimental import pallas as pl
from jax.experimental.pallas import tpu as pltpu

H = 12

MESH = pl.DeviceIdType.MESH
F32 = jnp.float32
BF = jnp.bfloat16


def rows16(index):
    return pl.ds(pl.multiple_of(index * 16, 16), 16)


def rows_at(start, size):
    return pl.ds(pl.multiple_of(start, 8), size)


def lanes_at(start, size):
    return pl.ds(pl.multiple_of(start, 128), size)


class Place:
    def __init__(self):
        me = lax.axis_index("dp")
        self.me = me
        self.c = me % 2
        self.x = (me // 2) % 2
        self.y = (me // 4) % 2
        self.z = me // 8
        self.sibling = me + 1 - 2 * self.c
        self.to_x = me + 2 - 4 * self.x
        self.to_y = me + 4 - 8 * self.y
        self.up = me + 8
        self.down = me - 8


def stream_scratch():
    return [
        pltpu.VMEM((2, 64, 768), F32),
        pltpu.VMEM((144, 128), F32),
        pltpu.VMEM((2, 144, 128), F32),
        pltpu.VMEM((144, 128), F32),
        pltpu.VMEM((2, 144, 128), F32),
        pltpu.VMEM((72, 128), F32),
        pltpu.VMEM((2, 72, 128), F32),
        pltpu.VMEM((72, 128), F32),
        pltpu.VMEM((2, 72, 128), F32),
        pltpu.VMEM((2, 192, 128), F32),
        pltpu.VMEM((2, 2, 192, 128), F32),
        pltpu.VMEM((128, 128), F32),
        pltpu.VMEM((64, 128), F32),
        pltpu.VMEM((4, 64, 128), F32),
        pltpu.VMEM((4, 128, 128), F32),
        pltpu.VMEM((16, 128), F32),
        pltpu.VMEM((8, 128), F32),
        pltpu.VMEM((8, 64, 768), F32),
        pltpu.SemaphoreType.DMA((10, 2)),
        pltpu.SemaphoreType.DMA((10, 2)),
        pltpu.SemaphoreType.DMA((2,)),
    ]


N_STREAM_SCRATCH = 21


class Stream:
    def __init__(self, place, which, count, refs, grad_ref, grad_rows, out_ref, out_rows):
        (self.sib_in, self.a_rs_out, self.a_rs_in, self.a_ag_out, self.a_ag_in, self.b_rs_out, self.b_rs_in,
         self.b_ag_out, self.b_ag_in, self.z_out, self.z_in, self.p1, self.p2, self.p3, self.q1, self.q2, self.q3,
         self.full, self.sent, self.came, self.kept) = refs
        self.place = place
        self.count = count
        self.grad_ref = grad_ref
        self.grad_rows = grad_rows
        self.out_ref = out_ref
        self.out_rows = out_rows
        if which == 0:
            self.d1, self.d2, self.to_a, self.to_b = place.x, place.y, place.to_x, place.to_y
        else:
            self.d1, self.d2, self.to_a, self.to_b = place.y, place.x, place.to_y, place.to_x

    def prepare(self):
        zero = jnp.zeros((192, 128), F32)
        for side in range(2):
            for parity in range(2):
                self.z_in[side, parity] = zero

    def copies(self, t):
        place, n = self.place, self.count
        par = t % 2
        never = t < 0

        def remote(i, src, dst, target):
            return pltpu.make_async_remote_copy(
                src_ref=src, dst_ref=dst, send_sem=self.sent.at[i, par], recv_sem=self.came.at[i, par],
                device_id=(target,), device_id_type=MESH)

        slot, row = self.grad_rows(t)
        other = rows_at(row + 64 * (1 - place.c), 64)
        m = t - 11
        ring = lax.rem(t + 5, 8)
        out_row = self.out_rows(m)
        mine = rows_at(out_row + 64 * place.c, 64)
        lead = (place.z, 3 - place.z)
        zs = []
        for side, device in ((0, place.up), (1, place.down)):
            for half, when in ((0, (t >= 1) & (t < n + 5)), (1, (t >= 6) & (t < n + 10))):
                for k in range(3):
                    at, size = (0, 144 - 48 * k) if half == 0 else (144 - 48 * k, 48 + 48 * k)
                    spot = pl.ds(at, size)
                    copy = remote(5 + 2 * side + half, self.z_out.at[side, spot], self.z_in.at[side, par, spot], device)
                    zs.append((copy, when, lead[side] == k, lead[side] == k + 1))
        return [
            (remote(0, self.grad_ref.at[slot, other], self.sib_in.at[par], place.sibling), (t >= 0) & (t < n), True, True),
            (remote(1, self.a_rs_out, self.a_rs_in.at[par], self.to_a), (t >= 1) & (t < n + 4), True, True),
            (remote(2, self.a_ag_out, self.a_ag_in.at[par], self.to_a), (t >= 7) & (t < n + 10), True, True),
            (remote(3, self.b_rs_out, self.b_rs_in.at[par], self.to_b), (t >= 2) & (t < n + 5), True, True),
            (remote(4, self.b_ag_out, self.b_ag_in.at[par], self.to_b), (t >= 6) & (t < n + 9), True, True),
            (remote(9, self.full.at[ring], self.out_ref.at[mine], place.sibling), (t >= 11) & (t < n + 11), True, True),
        ] + zs, (pltpu.make_async_copy(self.full.at[ring], self.out_ref.at[mine], self.kept.at[par]), (t >= 11) & (t < n + 11))

    def start(self, t):
        remote, (local, live) = self.copies(t)
        for copy, when, sends, _ in remote:
            pl.when(when if sends is True else when & sends)(copy.start)
        pl.when(live)(local.start)

    def wait(self, t):
        remote, (local, live) = self.copies(t)
        for copy, when, sends, takes in remote:
            if sends is True:
                @pl.when(when)
                def _(copy=copy):
                    copy.wait_send()
                    copy.wait_recv()
            else:
                pl.when(when & sends)(copy.wait_send)
                pl.when(when & takes)(copy.wait_recv)
        pl.when(live)(local.wait)

    def work(self, t):
        place = self.place
        z, d1, d2 = place.z, self.d1, self.d2
        par = (t + 1) % 2
        z_in, z_out = self.z_in, self.z_out
        lead = (z, 3 - z)

        def far(side, k):
            return z - k if side == 0 else z + k

        def target(side, step):
            return z + 4 - step if side == 0 else z - 4 + step

        def ring4(stage):
            return lax.rem(t + 16 - stage, 4)

        def ring8(stage):
            return lax.rem(t + 16 - stage, 8)

        def got_p(side, pos):
            return z_in[side, par, 48 * pos:48 * pos + 16, :]

        def got_q(side, pos, panel):
            at = 48 * pos + 16 + 16 * panel
            return z_in[side, par, at:at + 16, :]

        def put_p(side, pos, value):
            z_out[side, 48 * pos:48 * pos + 16, :] = value

        def put_q(side, pos, panel, value):
            at = 48 * pos + 16 + 16 * panel
            z_out[side, at:at + 16, :] = value

        def full_p(ring, block, value):
            self.full[ring, rows16(block), lanes_at((2 * d1 + d2) * 128, 128)] = value

        def full_q(ring, block, panel, value):
            self.full[ring, rows16(block), 512 + 128 * panel:640 + 128 * panel] = value

        @pl.when((t >= 11) & (t < self.count + 11))
        def _stage11():
            ring = ring8(11)
            self.full[ring, :, lanes_at((1 - d1) * 256, 128)] = self.a_ag_in[par, 0:64, :]
            self.full[ring, :, lanes_at((1 - d1) * 256 + 128, 128)] = self.a_ag_in[par, 64:128, :]
            for side in range(2):
                @pl.when(lead[side] == 3)
                def _(side=side, ring=ring):
                    for panel in range(2):
                        full_q(ring, far(side, 3), panel, got_q(side, 1, panel))

        @pl.when((t >= 10) & (t < self.count + 10))
        def _stage10():
            ring = ring8(10)
            other = self.b_ag_in[par, 0:64, :]
            self.full[ring, :, lanes_at((2 * d1 + 1 - d2) * 128, 128)] = other
            self.a_ag_out[rows_at(64 * (1 - d2), 64), :] = other
            self.a_ag_out[rows_at(64 * d2, 64), :] = self.full[ring, :, lanes_at((2 * d1 + d2) * 128, 128)]
            for side in range(2):
                @pl.when(lead[side] >= 2)
                def _(side=side, ring=ring):
                    for panel in range(2):
                        value = got_q(side, 2, panel)
                        full_q(ring, far(side, 2), panel, value)
                        put_q(side, 1, panel, value)

        @pl.when((t >= 9) & (t < self.count + 9))
        def _stage9():
            ring = ring8(9)
            for side in range(2):
                @pl.when(lead[side] == 3)
                def _(side=side, ring=ring):
                    full_p(ring, far(side, 3), got_p(side, 1))

                @pl.when(lead[side] >= 1)
                def _(side=side, ring=ring):
                    for panel in range(2):
                        value = got_q(side, 3, panel)
                        full_q(ring, far(side, 1), panel, value)
                        put_q(side, 2, panel, value)
            self.b_ag_out[0:64, :] = self.full[ring, :, lanes_at((2 * d1 + d2) * 128, 128)]

        @pl.when((t >= 8) & (t < self.count + 8))
        def _stage8():
            ring = ring8(8)
            for side in range(2):
                @pl.when(lead[side] >= 2)
                def _(side=side, ring=ring):
                    value = got_p(side, 2)
                    full_p(ring, far(side, 2), value)
                    put_p(side, 1, value)
            self.full[ring, rows16(z), lanes_at(512 + 128 * (1 - d1), 128)] = self.a_ag_in[par, 128:144, :]
            for panel in range(2):
                value = self.full[ring, rows16(z), 512 + 128 * panel:640 + 128 * panel]
                for side in range(2):
                    put_q(side, 3, panel, value)

        @pl.when((t >= 7) & (t < self.count + 7))
        def _stage7():
            ring = ring8(7)
            for side in range(2):
                @pl.when(lead[side] >= 1)
                def _(side=side, ring=ring):
                    value = got_p(side, 3)
                    full_p(ring, far(side, 1), value)
                    put_p(side, 2, value)
            self.full[ring, rows_at(16 * z + 8 * (1 - d2), 8), lanes_at(512 + 128 * d1, 128)] = self.b_ag_in[par, 64:72, :]
            self.a_ag_out[128:144, :] = self.full[ring, rows16(z), lanes_at(512 + 128 * d1, 128)]

        @pl.when((t >= 6) & (t < self.count + 6))
        def _stage6():
            ring = ring8(6)
            value = self.p3[ring4(6), rows16(z), :] + got_p(0, 0) + got_p(1, 0)
            full_p(ring, z, value)
            put_p(0, 3, value)
            put_p(1, 3, value)
            value = self.q3[...] + self.b_rs_in[par, 64:72, :]
            self.full[ring, rows_at(16 * z + 8 * d2, 8), lanes_at(512 + 128 * d1, 128)] = value
            self.b_ag_out[64:72, :] = value

        @pl.when((t >= 5) & (t < self.count + 5))
        def _stage5():
            for side in range(2):
                @pl.when(lead[side] <= 2)
                def _(side=side):
                    put_p(side, 0, self.p3[ring4(5), rows16(target(side, 3)), :] + got_p(side, 1))
            self.q3[...] = self.q2[rows_at(8 * d2, 8), :] + self.a_rs_in[par, rows_at(128 + 8 * d2, 8), :]
            self.b_rs_out[64:72, :] = self.q2[rows_at(8 * (1 - d2), 8), :] + self.a_rs_in[par, rows_at(128 + 8 * (1 - d2), 8), :]

        @pl.when((t >= 4) & (t < self.count + 4))
        def _stage4():
            for side in range(2):
                @pl.when(lead[side] <= 1)
                def _(side=side):
                    put_p(side, 1, self.p3[ring4(4), rows16(target(side, 2)), :] + got_p(side, 2))
            ring = ring4(4)

            def own_q(panel):
                first = self.q1[ring, rows_at(64 * panel + 16 * z, 16), :]
                spot = rows_at(16 + 16 * panel, 16)
                return first + z_in[0, par, spot, :] + z_in[1, par, spot, :]

            self.q2[...] = own_q(d1)
            self.a_rs_out[128:144, :] = own_q(1 - d1)

        @pl.when((t >= 3) & (t < self.count + 3))
        def _stage3():
            for side in range(2):
                @pl.when(lead[side] <= 2)
                def _(side=side):
                    for panel in range(2):
                        own = self.q1[ring4(3), rows_at(64 * panel + 16 * target(side, 3), 16), :]
                        put_q(side, 0, panel, own + got_q(side, 1, panel))
            ring = ring4(3)
            self.p3[ring] = self.p2[...] + self.b_rs_in[par, 0:64, :]
            for side in range(2):
                @pl.when(lead[side] == 0)
                def _(side=side, ring=ring):
                    put_p(side, 2, self.p3[ring, rows16(target(side, 1)), :])

        @pl.when((t >= 2) & (t < self.count + 2))
        def _stage2():
            for side in range(2):
                @pl.when(lead[side] <= 1)
                def _(side=side):
                    for panel in range(2):
                        own = self.q1[ring4(2), rows_at(64 * panel + 16 * target(side, 2), 16), :]
                        put_q(side, 1, panel, own + got_q(side, 2, panel))
            self.p2[...] = self.p1[rows_at(64 * d2, 64), :] + self.a_rs_in[par, rows_at(64 * d2, 64), :]
            self.b_rs_out[0:64, :] = self.p1[rows_at(64 * (1 - d2), 64), :] + self.a_rs_in[par, rows_at(64 * (1 - d2), 64), :]

        @pl.when((t >= 1) & (t < self.count + 1))
        def _stage1():
            slot, row = self.grad_rows(t - 1)
            mine = rows_at(row + 64 * place.c, 64)

            def summed(lane):
                spot = lanes_at(lane, 128)
                return self.grad_ref[slot, mine, spot] + self.sib_in[par, :, spot]

            for half in range(2):
                self.p1[64 * half:64 * half + 64, :] = summed(256 * d1 + 128 * half)
                self.a_rs_out[64 * half:64 * half + 64, :] = summed(256 * (1 - d1) + 128 * half)
            ring = ring4(1)
            for panel in range(2):
                self.q1[ring, 64 * panel:64 * panel + 64, :] = summed(512 + 128 * panel)
            for side in range(2):
                @pl.when(lead[side] == 0)
                def _(side=side, ring=ring):
                    for panel in range(2):
                        put_q(side, 2, panel, self.q1[ring, rows_at(64 * panel + 16 * target(side, 1), 16), :])


T0 = (((0,), (0,)), ((), ()))
NT = (((1,), (1,)), ((), ()))


def mm(left, right):
    return jnp.dot(left, right, preferred_element_type=F32)


def mm_nt(left, right):
    return lax.dot_general(left, right, NT, preferred_element_type=F32)


def mm_t(left, right):
    return lax.dot_general(left, right, T0, preferred_element_type=F32)


def row_of(ref):
    return ref[...].reshape(1, -1)


def normal_cdf(pre):
    size = jnp.abs(pre)
    down = 1.0 + (0.3275911 / 1.4142135623730951) * size
    t = pl.reciprocal(down, approx=True)
    t = t * (2.0 - down * t)
    bell = jnp.exp(-0.5 * pre * pre)
    poly = t * (0.5 * 0.254829592 + t * (0.5 * -0.284496736 + t * (0.5 * 1.421413741 + t * (
        0.5 * -1.453152027 + t * (0.5 * 1.061405429)))))
    tail = poly * bell
    return jnp.where(pre >= 0, 1.0 - tail, tail), bell


G0, D0 = 0, 4
X, Q, K, V, O, Y1, DZ, DA, DO = 8, 9, 10, 11, 12, 13, 14, 15, 16
N_ACTS = 17


class Net:
    def __init__(self, **refs):
        self.__dict__.update(refs)

    def project(self, i):
        rows = pl.ds(pl.multiple_of(i * 256, 256), 256)
        acts = self.acts
        x = acts[X, rows, :]
        acts[Q, rows, :] = (mm(x, self.w_q[...]) + row_of(self.query_bias)).astype(BF) * BF(0.125)
        acts[K, rows, :] = mm(x, self.w_k[...]).astype(BF)
        acts[V, rows, :] = (mm(x, self.w_v[...]) + row_of(self.value_bias)).astype(BF)

    def masks(self):
        place = lax.broadcasted_iota(jnp.int32, (8, 512), 1)
        for s in range(2):
            self.key_row[s] = jnp.where(place < self.lengths[s], 0.0, -1e9)

    def attend(self, i):
        s, pair = i // 6, lax.rem(i, 6)
        rows = pl.ds(pl.multiple_of(s * 512, 512), 512)
        lanes = lanes_at(pair * 128, 128)
        acts = self.acts
        k = acts[K, rows, lanes]
        v = acts[V, rows, lanes]
        lane = lax.broadcasted_iota(jnp.int32, (1, 128), 1)
        v_ones = jnp.concatenate([v, jnp.ones((512, 128), BF)], axis=1)
        step = 256
        for part in range(512 // step):
            some = pl.ds(pl.multiple_of(s * 512 + part * step, step), step)
            q = acts[Q, some, lanes]
            outs = []
            tops = []
            for head in range(2):
                live = (lane >= 64) if head else (lane < 64)
                score = mm_nt(jnp.where(live, q, BF(0)), k) + self.key_row[s, 0:1, :]
                top = jnp.max(score, axis=1, keepdims=True)
                e = jnp.exp(score - top).astype(BF)
                both = mm(e, v_ones)
                total = both[:, 128:]
                outs.append(both[:, :128] / total)
                tops.append(top + jnp.log(total))
            acts[O, some, lanes] = jnp.where(lane < 64, outs[0], outs[1]).astype(BF)
            spot = pl.ds(part * step, step)
            old = self.logs[s, spot, :]
            old = jnp.where(lane == 2 * pair, tops[0], old)
            self.logs[s, spot, :] = jnp.where(lane == 2 * pair + 1, tops[1], old)

    def normed(self, rows):
        mean = jnp.sum(rows, axis=1, keepdims=True) * (1.0 / 768)
        centred = rows - mean
        spread = jnp.sum(centred * centred, axis=1, keepdims=True) * (1.0 / 768)
        inverse = lax.rsqrt(spread + 1e-6)
        return centred * inverse, inverse

    def feed(self, i):
        rows = pl.ds(pl.multiple_of(i * 256, 256), 256)
        acts = self.acts
        h1 = acts[X, rows, :].astype(F32) + mm(acts[O, rows, :], self.w_m[...]) + row_of(self.mixer_bias)
        n1, r1 = self.normed(h1)
        self.n1[rows, :] = n1.astype(self.n1.dtype)
        self.r1[rows, :] = jnp.broadcast_to(r1, (256, 128))
        y1 = n1 * row_of(self.first_gain) + row_of(self.first_shift)
        self.z[...] = y1 + row_of(self.shrink_bias)
        acts[Y1, rows, :] = y1.astype(BF)
        for j in range(4):
            self.feed_block(rows, j)
        n2, r2 = self.normed(self.z[...])
        self.n2[rows, :] = n2
        self.r2[rows, :] = jnp.broadcast_to(r2, (256, 128))
        s = i // 2
        at = lax.broadcasted_iota(jnp.int32, (256, 1), 0) + lax.rem(i, 2) * 256
        live = jnp.where(at < self.lengths[s], n2, 0.0)
        part = jnp.sum(live, axis=0, keepdims=True)
        first = lax.rem(i, 2) == 0
        self.n2_sum[s, 0:1, :] = jnp.where(first, part, self.n2_sum[s, 0:1, :] + part)

    def feed_block(self, rows, j):
        acts = self.acts
        cols = pl.ds(768 * j, 768)
        pre = mm(acts[Y1, rows, :], self.w_e[:, cols]) + self.expand_bias[cols].reshape(1, 768)
        cdf, bell = normal_cdf(pre)
        low = (pre * cdf).astype(BF)
        acts[G0 + j, rows, :] = low
        acts[D0 + j, rows, :] = (cdf + pre * bell * 0.3989422804014327).astype(BF)
        self.z[...] += mm(low, self.w_s[cols, :])

    def pool(self, s):
        count = self.lengths[s].astype(F32)
        return self.n2_sum[s, 0:1, :] * row_of(self.second_gain) / count + row_of(self.second_shift)


class Back(Net):
    def turn_logs(self):
        for s in range(2):
            self.logs_t[s] = jnp.transpose(self.logs[s])[0:16, :]

    def gather(self, place):
        c, chip = place.c, place.me // 2
        every = self.every
        for s in range(2):
            u = self.pool(s)
            for j in range(6):
                every[c, chip, 8 * s + j:8 * s + j + 1, :] = u[:, 128 * j:128 * j + 128]
            every[c, chip, 8 * s + 6:8 * s + 8, :] = jnp.full((2, 128), self.targets[s], F32)

        def copy(source, device):
            return pltpu.make_async_remote_copy(
                src_ref=every.at[c, source], dst_ref=every.at[c, source], send_sem=self.told.at[device // 2],
                recv_sem=self.heard.at[source], device_id=(device,), device_id_type=MESH)

        def out(k, carry):
            copy(chip, lax.rem(chip + k, 16) * 2 + c).start()
            return carry

        def done(k, carry):
            copy(chip, lax.rem(chip + k, 16) * 2 + c).wait_send()
            copy(lax.rem(chip + 16 - k, 16), place.me).wait_recv()
            return carry

        lax.fori_loop(1, 16, out, 0)
        lax.fori_loop(1, 16, done, 0)
        share = pltpu.make_async_remote_copy(
            src_ref=every.at[c], dst_ref=every.at[c], send_sem=self.told.at[chip],
            recv_sem=self.heard.at[chip], device_id=(place.sibling,), device_id_type=MESH)
        share.start()
        share.wait_send()
        share.wait_recv()

    def pair(self, place, s):
        here = place.me * 2 + s
        wanted = jnp.full((8, 128), self.partners[here], jnp.int32)
        mine = self.every[place.c, place.me // 2, 8 * s:8 * s + 8, :]

        def pick(i, found):
            far, near = found
            device = i // 2
            tile = self.every[lax.rem(device, 2), device // 2, rows_at(8 * lax.rem(i, 2), 8), :]
            far += jnp.where(wanted == i, tile, 0.0)
            near += jnp.where(jnp.full((8, 128), self.partners[i], jnp.int32) == here, tile, 0.0)
            return far, near

        nothing = jnp.zeros((8, 128), F32)
        far, near = lax.fori_loop(0, 64, pick, (nothing, nothing))
        live = lax.broadcasted_iota(jnp.int32, (8, 128), 0) < 6

        def inner(left, right):
            return jnp.sum(jnp.where(live, left * right, 0.0), axis=(0, 1), keepdims=True)

        length = jnp.sqrt(inner(mine, mine) + 1e-6)
        far_length = jnp.sqrt(inner(far, far) + 1e-6)
        near_length = jnp.sqrt(inner(near, near) + 1e-6)
        score = inner(mine, far) / (length * far_length)
        near_score = inner(near, mine) / (near_length * length)
        miss = score - mine[6:7, 0:1]
        near_miss = near_score - near[6:7, 0:1]
        own = mine / (length * length)
        grad = miss * (far / (length * far_length) - score * own)
        grad += near_miss * (near / (near_length * length) - near_score * own)
        for j in range(6):
            self.du[s, 0:1, 128 * j:128 * j + 128] = grad[j:j + 1, :]
        self.scores[s] = jnp.sum(score)

    def clear(self):
        self.vec[...] = jnp.zeros_like(self.vec)

    def add_vec(self, at, rows):
        self.vec[at:at + 1, :] += jnp.sum(rows.astype(F32), axis=0, keepdims=True)

    def second_vectors(self):
        gain = jnp.zeros((1, 768), F32)
        for s in range(2):
            gain += self.du[s, 0:1, :] * self.n2_sum[s, 0:1, :] / self.lengths[s].astype(F32)
        self.vec[6:7, :] = gain
        self.vec[7:8, :] = self.du[0, 0:1, :] + self.du[1, 0:1, :]

    def back_second(self, i):
        rows = pl.ds(pl.multiple_of(i * 256, 256), 256)
        s = i // 2
        up = self.du[s, 0:1, :] * row_of(self.second_gain) / self.lengths[s].astype(F32)
        mean = jnp.sum(up, axis=1, keepdims=True) * (1.0 / 768)
        n2 = self.n2[rows, :]
        along = jnp.sum(n2 * up, axis=1, keepdims=True) * (1.0 / 768)
        at = lax.broadcasted_iota(jnp.int32, (256, 1), 0) + lax.rem(i, 2) * 256
        dh2 = jnp.where(at < self.lengths[s], self.r2[rows, 0:1] * (up - mean - n2 * along), 0.0)
        self.n2[rows, :] = dh2
        dz = dh2.astype(BF)
        self.acts[DZ, rows, :] = dz
        self.add_vec(5, dz)

    def back_hidden(self, i):
        j, half = i // 2, lax.rem(i, 2)
        rows = pl.ds(pl.multiple_of(half * 512, 512), 512)
        units = pl.ds(pl.multiple_of(j * 768, 768), 768)
        df = (mm_nt(self.acts[DZ, rows, :], self.w_s[units, :]) * self.acts[D0 + j, rows, :].astype(F32)).astype(BF)
        self.acts[D0 + j, rows, :] = df
        part = jnp.sum(df.astype(F32), axis=0, keepdims=True)
        line = lax.broadcasted_iota(jnp.int32, (8, 768), 0) == j
        self.vec[8:16, :] += jnp.where(line, part, 0.0)

    def back_first(self, i):
        rows = pl.ds(pl.multiple_of(i * 256, 256), 256)
        acts = self.acts
        up = self.n2[rows, :]
        for j in range(4):
            up += mm_nt(acts[D0 + j, rows, :], self.w_e[:, 768 * j:768 * j + 768])
        n1 = self.n1[rows, :].astype(F32)
        self.add_vec(3, up * n1)
        self.add_vec(4, up)
        dn = up * row_of(self.first_gain)
        mean = jnp.sum(dn, axis=1, keepdims=True) * (1.0 / 768)
        along = jnp.sum(dn * n1, axis=1, keepdims=True) * (1.0 / 768)
        dh1 = self.r1[rows, 0:1] * (dn - mean - n1 * along)
        self.n2[rows, :] = dh1
        da = dh1.astype(BF)
        acts[DA, rows, :] = da
        self.add_vec(2, da)
        acts[DO, rows, :] = mm_nt(da, self.w_m[...]).astype(BF)

    def attend_back(self, i):
        s, head = i // 12, lax.rem(i, 12)
        rows = pl.ds(pl.multiple_of(s * 512, 512), 512)
        lanes = lanes_at((head // 2) * 128, 128)
        acts = self.acts
        lane = lax.broadcasted_iota(jnp.int32, (1, 128), 1)
        live = (lane // 64) == lax.rem(head, 2)
        q_all, k, v = acts[Q, rows, lanes], acts[K, rows, lanes], acts[V, rows, lanes]
        q = jnp.where(live, q_all, BF(0))
        up = jnp.where(live, acts[DO, rows, lanes], BF(0))
        place = lax.broadcasted_iota(jnp.int32, (512, 1), 0)
        off = jnp.where(place < self.lengths[s], 0.0, -1e9)
        probs = jnp.exp(mm_nt(k, q) + off - self.logs_t[s, pl.ds(head, 1), :])
        weighed = probs * mm_nt(v, up)
        delta = jnp.sum(weighed, axis=0, keepdims=True)
        ds = (weighed - probs * delta).astype(BF)
        dv = mm(probs.astype(BF), up)
        dk = mm(ds, q)
        dq = mm_t(ds, k) * 0.125
        acts[Q, rows, lanes] = jnp.where(live, dq.astype(BF), q_all)
        acts[K, rows, lanes] = jnp.where(live, dk.astype(BF), k)
        acts[V, rows, lanes] = jnp.where(live, dv.astype(BF), v)

    def token_copy(self, i):
        rows = pl.ds(pl.multiple_of(i * 256, 256), 256)
        return pltpu.make_async_copy(self.n2.at[rows], self.tokens_grad.at[rows], self.wrote.at[i])

    def back_tokens(self, i):
        rows = pl.ds(pl.multiple_of(i * 256, 256), 256)
        dq, dk, dv = self.acts[Q, rows, :], self.acts[K, rows, :], self.acts[V, rows, :]
        self.add_vec(0, dq)
        self.add_vec(1, dv)
        self.n2[rows, :] += mm_nt(dq, self.w_q[...]) + mm_nt(dk, self.w_k[...]) + mm_nt(dv, self.w_v[...])
        self.token_copy(i).start()

    def back_task(self, i):
        pl.when(i < 8)(lambda: self.back_hidden(i))
        pl.when((i >= 8) & (i < 12))(lambda: self.back_first(i - 8))
        pl.when((i >= 12) & (i < 36))(lambda: self.attend_back(i - 12))
        pl.when((i >= 36) & (i < 40))(lambda: self.back_tokens(i - 36))

    def grad_piece(self, i):
        b = i // 3
        cols = pl.ds(pl.multiple_of(lax.rem(i, 3) * 256, 256), 256)
        left = jnp.where(b < 4, G0 + b, jnp.where(b < 8, Y1, jnp.where(b < 9, O, X)))
        right = jnp.where(b < 4, DZ, jnp.where(b < 8, D0 + b - 4, jnp.where(b < 9, DA, b)))
        self.ring[lax.rem(b, 2), cols, :] = mm_t(self.acts[left, :, cols], self.acts[right])


N_IN = 19
VECTORS = ("query_bias", "value_bias", "mixer_bias", "first_gain", "first_shift", "shrink_bias", "second_gain",
           "second_shift")


def layer_kernel(*refs):
    (tokens, lengths, partners, targets, w_q, query_bias, w_k, w_v, value_bias, w_m, mixer_bias, first_gain,
     first_shift, w_e, expand_bias, w_s, shrink_bias, second_gain, second_shift) = refs[:N_IN]
    scores, tokens_grad, summed = refs[N_IN:N_IN + 3]
    rest = refs[N_IN + 3:]
    (acts, v_q, v_k, v_v, v_m, v_e, v_s, key_row, logs, logs_t, n1, r1, n2, r2, z, n2_sum, every, du, vec, ring,
     loaded, told, heard, wrote) = rest[:24]
    first, second = rest[24:24 + N_STREAM_SCRATCH], rest[24 + N_STREAM_SCRATCH:]
    place = Place()
    net = Back(
        acts=acts, w_q=v_q, w_k=v_k, w_v=v_v, w_m=v_m, w_e=v_e, w_s=v_s, query_bias=query_bias, value_bias=value_bias,
        mixer_bias=mixer_bias, first_gain=first_gain, first_shift=first_shift, expand_bias=expand_bias,
        shrink_bias=shrink_bias, second_gain=second_gain, second_shift=second_shift, lengths=lengths,
        partners=partners, targets=targets, scores=scores, tokens_grad=tokens_grad, key_row=key_row, logs=logs,
        logs_t=logs_t, n1=n1, r1=r1, n2=n2, r2=r2, z=z, n2_sum=n2_sum, every=every, du=du, vec=vec, ring=ring,
        told=told, heard=heard, wrote=wrote)
    loads = [pltpu.make_async_copy(src, dst, loaded.at[i]) for i, (src, dst) in enumerate([
        (tokens, acts.at[X]), (w_q, v_q), (w_k, v_k), (w_v, v_v), (w_m, v_m), (w_e, v_e), (w_s, v_s)])]
    for copy in loads:
        copy.start()

    def chunk_rows(t, shift):
        t = jnp.clip(t, 0, 36)
        return lax.rem(t // 3, 2), lax.rem(t, 3) * 256 + shift

    def out_rows(t, shift):
        return jnp.clip(t, 0, 36) * 256 + shift

    one = Stream(place, 0, 37, first, ring, lambda t: chunk_rows(t, 0), summed, lambda t: out_rows(t, 0))
    two = Stream(place, 1, 36, second, ring, lambda t: chunk_rows(t, 128), summed, lambda t: out_rows(t, 128))
    one.prepare()
    two.prepare()
    greet_all(place)

    def each(count, task):
        def step(i, carry):
            task(i)
            return carry

        lax.fori_loop(0, count, step, 0)

    net.masks()
    net.clear()
    for copy in loads[:4]:
        copy.wait()
    each(4, net.project)
    each(12, net.attend)
    net.turn_logs()
    for copy in loads[4:]:
        copy.wait()
    each(4, net.feed)
    await_all()
    net.gather(place)
    for s in range(2):
        net.pair(place, s)
    net.second_vectors()
    each(4, net.back_second)

    def step(turn, carry):
        t = turn - 3

        @pl.when(t >= 0)
        def _():
            @pl.when(t == 36)
            def _():
                ring[0, 0:128, :] = jnp.zeros((128, 768), F32)
                ring[0, 0:16, :] = vec[...]

            for stream in (one, two):
                stream.wait(t - 1)
                stream.work(t)
                stream.start(t)

        pl.when(turn < 36)(lambda: net.grad_piece(turn))

        @pl.when((t >= 0) & (t < 20))
        def _():
            def run(i, carry):
                net.back_task(2 * t + i)
                return carry

            lax.fori_loop(0, 2, run, 0)

        return carry

    lax.fori_loop(0, 52, step, 0)
    for i in range(4):
        net.token_copy(i).wait()


def greet_all(place):
    bar = pltpu.get_barrier_semaphore()
    chip = place.me // 2

    def hail(k, carry):
        pl.semaphore_signal(bar, 1, device_id=(lax.rem(chip + k, 16) * 2 + place.c,), device_id_type=MESH)
        return carry

    pl.semaphore_signal(bar, 1, device_id=(place.sibling,), device_id_type=MESH)
    lax.fori_loop(1, 16, hail, 0)


def await_all():
    pl.semaphore_wait(pltpu.get_barrier_semaphore(), 16)


def whole_layer(*args):
    anywhere = pl.BlockSpec(memory_space=pl.ANY)
    vector = pl.BlockSpec(memory_space=pltpu.VMEM)
    scalars = pl.BlockSpec(memory_space=pltpu.SMEM)
    specs = [anywhere if a.dtype == BF else vector if a.shape[0] >= 768 else scalars for a in args]

    def low(*shape):
        return pltpu.VMEM(shape, BF)

    def full(*shape):
        return pltpu.VMEM(shape, F32)

    return pl.pallas_call(
        layer_kernel,
        out_shape=(
            jax.ShapeDtypeStruct((2,), F32),
            jax.ShapeDtypeStruct((1024, 768), F32),
            jax.ShapeDtypeStruct((73 * 128, 768), F32),
        ),
        in_specs=specs,
        out_specs=(scalars, anywhere, anywhere),
        scratch_shapes=[
            low(N_ACTS, 1024, 768),
            low(768, 768), low(768, 768), low(768, 768), low(768, 768), low(768, 3072), low(3072, 768),
            full(2, 8, 512), full(2, 512, 128), full(2, 16, 512),
            full(1024, 768), full(1024, 128), full(1024, 768), full(1024, 128), full(256, 768), full(2, 8, 768),
            full(2, 16, 16, 128), full(2, 8, 768), full(16, 768), full(2, 768, 768),
            pltpu.SemaphoreType.DMA((7,)), pltpu.SemaphoreType.DMA((16,)), pltpu.SemaphoreType.DMA((16,)),
            pltpu.SemaphoreType.DMA((4,)),
        ] + stream_scratch() + stream_scratch(),
        compiler_params=pltpu.CompilerParams(
            collective_id=0, has_side_effects=True, vmem_limit_bytes=63 << 20),
    )(*args)


def fused(*args):
    pair_scores, tokens_grad, summed = whole_layer(*args)
    blocks = summed[:9216].reshape(12, 768, 768)
    small = summed[9216:9228]
    return (
        pair_scores, tokens_grad, blocks[9], small[0], blocks[10], blocks[11], small[1], blocks[8], small[2],
        small[3], small[4], jnp.concatenate([blocks[4], blocks[5], blocks[6], blocks[7]], axis=1),
        small[8:].reshape(3072), summed[:3072], small[5], small[6], small[7])


def to_low(value):
    return value.astype(jnp.bfloat16)


def tdot(left, right):
    return lax.dot_general(
        left, right, (((0,), (0,)), ((), ())), preferred_element_type=jnp.float32
    )


def ndot(left, right):
    return lax.dot_general(
        left, right, (((1,), (1,)), ((), ())), preferred_element_type=jnp.float32
    )


def norm_rows(rows, gain, shift):
    mean = jnp.mean(rows, axis=-1, keepdims=True)
    centred = rows - mean
    spread = jnp.mean(centred * centred, axis=-1, keepdims=True)
    inverse = lax.rsqrt(spread + 1e-06)
    normed = centred * inverse
    return (normed * gain + shift, normed, inverse)


def norm_back(upstream, normed, inverse, gain):
    gain_grad = jnp.sum(upstream * normed, axis=0)
    shift_grad = jnp.sum(upstream, axis=0)
    dnormed = upstream * gain
    first_mean = jnp.mean(dnormed, axis=-1, keepdims=True)
    second_mean = jnp.mean(dnormed * normed, axis=-1, keepdims=True)
    return (inverse * (dnormed - first_mean - normed * second_mean), gain_grad, shift_grad)


def per_device(
    tokens,
    lengths,
    partners,
    targets,
    query_proj,
    query_bias,
    key_proj,
    value_proj,
    value_bias,
    mixer_proj,
    mixer_bias,
    first_gain,
    first_shift,
    expand_proj,
    expand_bias,
    shrink_proj,
    shrink_bias,
    second_gain,
    second_shift,
):
    sents = lengths.shape[0]
    rows_all = tokens.shape[0]
    slot = rows_all // sents
    width = tokens.shape[1]
    heads = H
    depth = width // heads
    scale = 1.0 / math.sqrt(depth)
    total = partners.shape[0]
    base = lax.axis_index("dp") * sents
    highest = lax.Precision.HIGHEST
    places = jnp.arange(slot, dtype=jnp.int32)
    valid = places[None, :] < lengths[:, None]
    row_mask = valid.reshape(rows_all, 1).astype(jnp.float32)
    shape4 = (sents, slot, heads, depth)
    queries = to_low(jnp.dot(tokens, query_proj, preferred_element_type=jnp.float32) + query_bias)
    keys = to_low(jnp.dot(tokens, key_proj, preferred_element_type=jnp.float32))
    values = to_low(jnp.dot(tokens, value_proj, preferred_element_type=jnp.float32) + value_bias)
    queries4 = queries.reshape(shape4)
    keys4 = keys.reshape(shape4)
    values4 = values.reshape(shape4)

    def masked_scores(query_rows, key_rows, live):
        raw = (
            jnp.einsum("qhd,khd->hqk", query_rows, key_rows, preferred_element_type=jnp.float32)
            * scale
        )
        return jnp.where(live[None, None, :], raw, -1000000000.0)

    def attend(item):
        query_rows, key_rows, value_rows, live = item
        raw = masked_scores(query_rows, key_rows, live)
        top = jnp.max(raw, axis=-1, keepdims=True)
        expd = jnp.exp(raw - top)
        summed = jnp.sum(expd, axis=-1, keepdims=True)
        probs = to_low(expd / summed)
        mixed = jnp.einsum("hqk,khd->qhd", probs, value_rows, preferred_element_type=jnp.float32)
        return (mixed, (top + jnp.log(summed))[..., 0])

    mixed, logsum = lax.map(attend, (queries4, keys4, values4, valid))
    mixed_low = to_low(mixed.reshape(rows_all, width))
    branch = jnp.dot(mixed_low, mixer_proj, preferred_element_type=jnp.float32) + mixer_bias
    first_out, first_normed, first_inverse = norm_rows(
        tokens.astype(jnp.float32) + branch, first_gain, first_shift
    )
    first_low = to_low(first_out)
    pre = jnp.dot(first_low, expand_proj, preferred_element_type=jnp.float32) + expand_bias
    act, gelu_back = jax.vjp(partial(jax.nn.gelu, approximate=False), pre)
    act_low = to_low(act)
    shrink = jnp.dot(act_low, shrink_proj, preferred_element_type=jnp.float32) + shrink_bias
    outputs, second_normed, second_inverse = norm_rows(
        first_out + shrink, second_gain, second_shift
    )
    counts = lengths.astype(jnp.float32)
    pooled = jnp.sum((outputs * row_mask).reshape(sents, slot, width), axis=1) / counts[:, None]
    mine = lax.dynamic_slice_in_dim(partners, base, sents)
    every = lax.all_gather(pooled, "dp", axis=0, tiled=True)
    partner_vec = jnp.take(every, mine, axis=0)
    inner = jnp.sum(pooled * partner_vec, axis=-1)
    own_len = jnp.sqrt(jnp.sum(pooled * pooled, axis=-1) + 1e-06)
    far_len = jnp.sqrt(jnp.sum(partner_vec * partner_vec, axis=-1) + 1e-06)
    pair_scores = inner / (own_len * far_len)
    miss = pair_scores - targets
    joint = (own_len * far_len)[:, None]
    dpooled = miss[:, None] * (
        partner_vec / joint - (pair_scores / (own_len * own_len))[:, None] * pooled
    )
    dpartner = miss[:, None] * (
        pooled / joint - (pair_scores / (far_len * far_len))[:, None] * partner_vec
    )
    owners = (mine[:, None] == jnp.arange(total, dtype=jnp.int32)[None, :]).astype(jnp.float32)
    spread = lax.dot_general(owners, dpartner, (((0,), (0,)), ((), ())), precision=highest)
    returned = lax.psum_scatter(spread, "dp", scatter_dimension=0, tiled=True)
    dpool_all = (dpooled + returned) / counts[:, None]
    doutputs = (dpool_all[:, None, :] * valid[:, :, None].astype(jnp.float32)).reshape(
        rows_all, width
    )
    dsecond, second_gain_grad, second_shift_grad = norm_back(
        doutputs, second_normed, second_inverse, second_gain
    )
    dshrink = to_low(dsecond)
    shrink_proj_grad = tdot(act_low, dshrink)
    shrink_bias_grad = jnp.sum(dshrink.astype(jnp.float32), axis=0)
    dact = ndot(dshrink, shrink_proj)
    dpre = to_low(gelu_back(dact)[0])
    expand_proj_grad = tdot(first_low, dpre)
    expand_bias_grad = jnp.sum(dpre.astype(jnp.float32), axis=0)
    dfirst_out = ndot(dpre, expand_proj) + dsecond
    dfirst, first_gain_grad, first_shift_grad = norm_back(
        dfirst_out, first_normed, first_inverse, first_gain
    )
    dbranch = to_low(dfirst)
    mixer_proj_grad = tdot(mixed_low, dbranch)
    mixer_bias_grad = jnp.sum(dbranch.astype(jnp.float32), axis=0)
    dmixed = to_low(ndot(dbranch, mixer_proj)).reshape(shape4)

    def attend_back(item):
        query_rows, key_rows, value_rows, live, row_logsum, dmix = item
        raw = masked_scores(query_rows, key_rows, live)
        probs = jnp.exp(raw - row_logsum[..., None])
        probs_low = to_low(probs)
        dprob = jnp.einsum("qhd,khd->hqk", dmix, value_rows, preferred_element_type=jnp.float32)
        delta = jnp.sum(dprob * probs, axis=-1, keepdims=True)
        dscore = to_low(probs * (dprob - delta))
        dquery = (
            jnp.einsum("hqk,khd->qhd", dscore, key_rows, preferred_element_type=jnp.float32) * scale
        )
        dkey = (
            jnp.einsum("hqk,qhd->khd", dscore, query_rows, preferred_element_type=jnp.float32)
            * scale
        )
        dvalue = jnp.einsum("hqk,qhd->khd", probs_low, dmix, preferred_element_type=jnp.float32)
        return (to_low(dquery), to_low(dkey), to_low(dvalue))

    dquery, dkey, dvalue = lax.map(attend_back, (queries4, keys4, values4, valid, logsum, dmixed))
    dquery = dquery.reshape(rows_all, width)
    dkey = dkey.reshape(rows_all, width)
    dvalue = dvalue.reshape(rows_all, width)
    query_proj_grad = tdot(tokens, dquery)
    query_bias_grad = jnp.sum(dquery.astype(jnp.float32), axis=0)
    key_proj_grad = tdot(tokens, dkey)
    value_proj_grad = tdot(tokens, dvalue)
    value_bias_grad = jnp.sum(dvalue.astype(jnp.float32), axis=0)
    tokens_grad = (
        ndot(dquery, query_proj) + ndot(dkey, key_proj) + ndot(dvalue, value_proj) + dfirst
    )
    (
        query_proj_grad,
        query_bias_grad,
        key_proj_grad,
        value_proj_grad,
        value_bias_grad,
        mixer_proj_grad,
        mixer_bias_grad,
        first_gain_grad,
        first_shift_grad,
        expand_proj_grad,
        expand_bias_grad,
        shrink_proj_grad,
        shrink_bias_grad,
        second_gain_grad,
        second_shift_grad,
    ) = lax.psum(
        (
            query_proj_grad,
            query_bias_grad,
            key_proj_grad,
            value_proj_grad,
            value_bias_grad,
            mixer_proj_grad,
            mixer_bias_grad,
            first_gain_grad,
            first_shift_grad,
            expand_proj_grad,
            expand_bias_grad,
            shrink_proj_grad,
            shrink_bias_grad,
            second_gain_grad,
            second_shift_grad,
        ),
        "dp",
    )
    return (
        pair_scores,
        tokens_grad,
        query_proj_grad,
        query_bias_grad,
        key_proj_grad,
        value_proj_grad,
        value_bias_grad,
        mixer_proj_grad,
        mixer_bias_grad,
        first_gain_grad,
        first_shift_grad,
        expand_proj_grad,
        expand_bias_grad,
        shrink_proj_grad,
        shrink_bias_grad,
        second_gain_grad,
        second_shift_grad,
    )


def solution(mesh):
    in_specs = (
        P("dp", None),
        P("dp"),
        P(),
        P("dp"),
        P(),
        P(),
        P(),
        P(),
        P(),
        P(),
        P(),
        P(),
        P(),
        P(),
        P(),
        P(),
        P(),
        P(),
        P(),
    )
    out_specs = (
        P("dp"),
        P("dp", None),
        P(),
        P(),
        P(),
        P(),
        P(),
        P(),
        P(),
        P(),
        P(),
        P(),
        P(),
        P(),
        P(),
        P(),
        P(),
    )
    plain = mesh.shape["dp"] != 32
    return jax.shard_map(
        per_device if plain else fused, mesh=mesh, in_specs=in_specs, out_specs=out_specs, check_vma=False
    )
```

```python
from functools import partial
import math

import jax
import jax.numpy as jnp
from jax import lax
from jax.sharding import PartitionSpec as P

from jax.experimental import pallas as pl
from jax.experimental.pallas import tpu as pltpu

H = 12

MESH = pl.DeviceIdType.MESH
F32 = jnp.float32
BF = jnp.bfloat16


def rows16(index):
    return pl.ds(pl.multiple_of(index * 16, 16), 16)


def rows_at(start, size):
    return pl.ds(pl.multiple_of(start, 8), size)


def lanes_at(start, size):
    return pl.ds(pl.multiple_of(start, 128), size)


class Place:
    def __init__(self):
        me = lax.axis_index("dp")
        self.me = me
        self.c = me % 2
        self.x = (me // 2) % 2
        self.y = (me // 4) % 2
        self.z = me // 8
        self.sibling = me + 1 - 2 * self.c
        self.to_x = me + 2 - 4 * self.x
        self.to_y = me + 4 - 8 * self.y
        self.up = me + 8
        self.down = me - 8


def stream_scratch():
    return [
        pltpu.VMEM((2, 64, 768), F32),
        pltpu.VMEM((144, 128), F32),
        pltpu.VMEM((2, 144, 128), F32),
        pltpu.VMEM((144, 128), F32),
        pltpu.VMEM((2, 144, 128), F32),
        pltpu.VMEM((72, 128), F32),
        pltpu.VMEM((2, 72, 128), F32),
        pltpu.VMEM((72, 128), F32),
        pltpu.VMEM((2, 72, 128), F32),
        pltpu.VMEM((2, 192, 128), F32),
        pltpu.VMEM((2, 2, 192, 128), F32),
        pltpu.VMEM((128, 128), F32),
        pltpu.VMEM((64, 128), F32),
        pltpu.VMEM((4, 64, 128), F32),
        pltpu.VMEM((4, 128, 128), F32),
        pltpu.VMEM((16, 128), F32),
        pltpu.VMEM((8, 128), F32),
        pltpu.VMEM((8, 64, 768), F32),
        pltpu.SemaphoreType.DMA((10, 2)),
        pltpu.SemaphoreType.DMA((10, 2)),
        pltpu.SemaphoreType.DMA((2,)),
    ]


N_STREAM_SCRATCH = 21


class Stream:
    def __init__(self, place, which, count, refs, grad_ref, grad_rows, out_ref, out_rows):
        (self.sib_in, self.a_rs_out, self.a_rs_in, self.a_ag_out, self.a_ag_in, self.b_rs_out, self.b_rs_in,
         self.b_ag_out, self.b_ag_in, self.z_out, self.z_in, self.p1, self.p2, self.p3, self.q1, self.q2, self.q3,
         self.full, self.sent, self.came, self.kept) = refs
        self.place = place
        self.count = count
        self.grad_ref = grad_ref
        self.grad_rows = grad_rows
        self.out_ref = out_ref
        self.out_rows = out_rows
        if which == 0:
            self.d1, self.d2, self.to_a, self.to_b = place.x, place.y, place.to_x, place.to_y
        else:
            self.d1, self.d2, self.to_a, self.to_b = place.y, place.x, place.to_y, place.to_x

    def prepare(self):
        zero = jnp.zeros((192, 128), F32)
        for side in range(2):
            for parity in range(2):
                self.z_in[side, parity] = zero

    def copies(self, t):
        place, n = self.place, self.count
        par = t % 2

        def remote(i, src, dst, target):
            return pltpu.make_async_remote_copy(
                src_ref=src, dst_ref=dst, send_sem=self.sent.at[i, par], recv_sem=self.came.at[i, par],
                device_id=(target,), device_id_type=MESH)

        def tail(i, src, dst, at, size, target):
            return remote(i, src.at[pl.ds(at, size)], dst.at[par, pl.ds(at, size)], target)

        slot, row = self.grad_rows(t)
        other = rows_at(row + 64 * (1 - place.c), 64)
        m = t - 11
        ring = lax.rem(t + 5, 8)
        out_row = self.out_rows(m)
        mine = rows_at(out_row + 64 * place.c, 64)
        lead = (place.z, 3 - place.z)
        zs = []
        for side, device in ((0, place.up), (1, place.down)):
            for half, when in ((0, (t >= 1) & (t < n + 5)), (1, (t >= 6) & (t < n + 10))):
                for k in range(3):
                    at, size = (0, 144 - 48 * k) if half == 0 else (144 - 48 * k, 48 + 48 * k)
                    spot = pl.ds(at, size)
                    copy = remote(5 + 2 * side + half, self.z_out.at[side, spot], self.z_in.at[side, par, spot], device)
                    zs.append((copy, when, lead[side] == k, lead[side] == k + 1))
        return [
            (remote(0, self.grad_ref.at[slot, other], self.sib_in.at[par], place.sibling), (t >= 0) & (t < n), True, True),
            (remote(1, self.a_rs_out, self.a_rs_in.at[par], self.to_a), (t >= 1) & (t < n + 1), True, True),
            (tail(1, self.a_rs_out, self.a_rs_in, 128, 16, self.to_a), (t >= n + 1) & (t < n + 4), True, True),
            (tail(2, self.a_ag_out, self.a_ag_in, 128, 16, self.to_a), (t >= 7) & (t < 10), True, True),
            (remote(2, self.a_ag_out, self.a_ag_in.at[par], self.to_a), (t >= 10) & (t < n + 10), True, True),
            (remote(3, self.b_rs_out, self.b_rs_in.at[par], self.to_b), (t >= 2) & (t < n + 2), True, True),
            (tail(3, self.b_rs_out, self.b_rs_in, 64, 8, self.to_b), (t >= n + 2) & (t < n + 5), True, True),
            (tail(4, self.b_ag_out, self.b_ag_in, 64, 8, self.to_b), (t >= 6) & (t < 9), True, True),
            (remote(4, self.b_ag_out, self.b_ag_in.at[par], self.to_b), (t >= 9) & (t < n + 9), True, True),
            (remote(9, self.full.at[ring], self.out_ref.at[mine], place.sibling), (t >= 11) & (t < n + 11), True, True),
        ] + zs, (pltpu.make_async_copy(self.full.at[ring], self.out_ref.at[mine], self.kept.at[par]), (t >= 11) & (t < n + 11))

    def start(self, t):
        remote, (local, live) = self.copies(t)
        for copy, when, sends, _ in remote:
            pl.when(when if sends is True else when & sends)(copy.start)
        pl.when(live)(local.start)

    def wait(self, t):
        remote, (local, live) = self.copies(t)
        for copy, when, sends, takes in remote:
            if sends is True:
                @pl.when(when)
                def _(copy=copy):
                    copy.wait_send()
                    copy.wait_recv()
            else:
                pl.when(when & sends)(copy.wait_send)
                pl.when(when & takes)(copy.wait_recv)
        pl.when(live)(local.wait)

    def work(self, t):
        place = self.place
        z, d1, d2 = place.z, self.d1, self.d2
        par = (t + 1) % 2
        z_in, z_out = self.z_in, self.z_out
        lead = (z, 3 - z)

        def far(side, k):
            return z - k if side == 0 else z + k

        def target(side, step):
            return z + 4 - step if side == 0 else z - 4 + step

        def ring4(stage):
            return lax.rem(t + 16 - stage, 4)

        def ring8(stage):
            return lax.rem(t + 16 - stage, 8)

        def got_p(side, pos):
            return z_in[side, par, 48 * pos:48 * pos + 16, :]

        def got_q(side, pos, panel):
            at = 48 * pos + 16 + 16 * panel
            return z_in[side, par, at:at + 16, :]

        def put_p(side, pos, value):
            z_out[side, 48 * pos:48 * pos + 16, :] = value

        def put_q(side, pos, panel, value):
            at = 48 * pos + 16 + 16 * panel
            z_out[side, at:at + 16, :] = value

        def full_p(ring, block, value):
            self.full[ring, rows16(block), lanes_at((2 * d1 + d2) * 128, 128)] = value

        def full_q(ring, block, panel, value):
            self.full[ring, rows16(block), 512 + 128 * panel:640 + 128 * panel] = value

        @pl.when((t >= 11) & (t < self.count + 11))
        def _stage11():
            ring = ring8(11)
            self.full[ring, :, lanes_at((1 - d1) * 256, 128)] = self.a_ag_in[par, 0:64, :]
            self.full[ring, :, lanes_at((1 - d1) * 256 + 128, 128)] = self.a_ag_in[par, 64:128, :]
            for side in range(2):
                @pl.when(lead[side] == 3)
                def _(side=side, ring=ring):
                    for panel in range(2):
                        full_q(ring, far(side, 3), panel, got_q(side, 1, panel))

        @pl.when((t >= 10) & (t < self.count + 10))
        def _stage10():
            ring = ring8(10)
            other = self.b_ag_in[par, 0:64, :]
            self.full[ring, :, lanes_at((2 * d1 + 1 - d2) * 128, 128)] = other
            self.a_ag_out[rows_at(64 * (1 - d2), 64), :] = other
            self.a_ag_out[rows_at(64 * d2, 64), :] = self.full[ring, :, lanes_at((2 * d1 + d2) * 128, 128)]
            for side in range(2):
                @pl.when(lead[side] >= 2)
                def _(side=side, ring=ring):
                    for panel in range(2):
                        value = got_q(side, 2, panel)
                        full_q(ring, far(side, 2), panel, value)
                        put_q(side, 1, panel, value)

        @pl.when((t >= 9) & (t < self.count + 9))
        def _stage9():
            ring = ring8(9)
            for side in range(2):
                @pl.when(lead[side] == 3)
                def _(side=side, ring=ring):
                    full_p(ring, far(side, 3), got_p(side, 1))

                @pl.when(lead[side] >= 1)
                def _(side=side, ring=ring):
                    for panel in range(2):
                        value = got_q(side, 3, panel)
                        full_q(ring, far(side, 1), panel, value)
                        put_q(side, 2, panel, value)
            self.b_ag_out[0:64, :] = self.full[ring, :, lanes_at((2 * d1 + d2) * 128, 128)]

        @pl.when((t >= 8) & (t < self.count + 8))
        def _stage8():
            ring = ring8(8)
            for side in range(2):
                @pl.when(lead[side] >= 2)
                def _(side=side, ring=ring):
                    value = got_p(side, 2)
                    full_p(ring, far(side, 2), value)
                    put_p(side, 1, value)
            self.full[ring, rows16(z), lanes_at(512 + 128 * (1 - d1), 128)] = self.a_ag_in[par, 128:144, :]
            for panel in range(2):
                value = self.full[ring, rows16(z), 512 + 128 * panel:640 + 128 * panel]
                for side in range(2):
                    put_q(side, 3, panel, value)

        @pl.when((t >= 7) & (t < self.count + 7))
        def _stage7():
            ring = ring8(7)
            for side in range(2):
                @pl.when(lead[side] >= 1)
                def _(side=side, ring=ring):
                    value = got_p(side, 3)
                    full_p(ring, far(side, 1), value)
                    put_p(side, 2, value)
            self.full[ring, rows_at(16 * z + 8 * (1 - d2), 8), lanes_at(512 + 128 * d1, 128)] = self.b_ag_in[par, 64:72, :]
            self.a_ag_out[128:144, :] = self.full[ring, rows16(z), lanes_at(512 + 128 * d1, 128)]

        @pl.when((t >= 6) & (t < self.count + 6))
        def _stage6():
            ring = ring8(6)
            value = self.p3[ring4(6), rows16(z), :] + got_p(0, 0) + got_p(1, 0)
            full_p(ring, z, value)
            put_p(0, 3, value)
            put_p(1, 3, value)
            value = self.q3[...] + self.b_rs_in[par, 64:72, :]
            self.full[ring, rows_at(16 * z + 8 * d2, 8), lanes_at(512 + 128 * d1, 128)] = value
            self.b_ag_out[64:72, :] = value

        @pl.when((t >= 5) & (t < self.count + 5))
        def _stage5():
            for side in range(2):
                @pl.when(lead[side] <= 2)
                def _(side=side):
                    put_p(side, 0, self.p3[ring4(5), rows16(target(side, 3)), :] + got_p(side, 1))
            self.q3[...] = self.q2[rows_at(8 * d2, 8), :] + self.a_rs_in[par, rows_at(128 + 8 * d2, 8), :]
            self.b_rs_out[64:72, :] = self.q2[rows_at(8 * (1 - d2), 8), :] + self.a_rs_in[par, rows_at(128 + 8 * (1 - d2), 8), :]

        @pl.when((t >= 4) & (t < self.count + 4))
        def _stage4():
            for side in range(2):
                @pl.when(lead[side] <= 1)
                def _(side=side):
                    put_p(side, 1, self.p3[ring4(4), rows16(target(side, 2)), :] + got_p(side, 2))
            ring = ring4(4)

            def own_q(panel):
                first = self.q1[ring, rows_at(64 * panel + 16 * z, 16), :]
                spot = rows_at(16 + 16 * panel, 16)
                return first + z_in[0, par, spot, :] + z_in[1, par, spot, :]

            self.q2[...] = own_q(d1)
            self.a_rs_out[128:144, :] = own_q(1 - d1)

        @pl.when((t >= 3) & (t < self.count + 3))
        def _stage3():
            for side in range(2):
                @pl.when(lead[side] <= 2)
                def _(side=side):
                    for panel in range(2):
                        own = self.q1[ring4(3), rows_at(64 * panel + 16 * target(side, 3), 16), :]
                        put_q(side, 0, panel, own + got_q(side, 1, panel))
            ring = ring4(3)
            self.p3[ring] = self.p2[...] + self.b_rs_in[par, 0:64, :]
            for side in range(2):
                @pl.when(lead[side] == 0)
                def _(side=side, ring=ring):
                    put_p(side, 2, self.p3[ring, rows16(target(side, 1)), :])

        @pl.when((t >= 2) & (t < self.count + 2))
        def _stage2():
            for side in range(2):
                @pl.when(lead[side] <= 1)
                def _(side=side):
                    for panel in range(2):
                        own = self.q1[ring4(2), rows_at(64 * panel + 16 * target(side, 2), 16), :]
                        put_q(side, 1, panel, own + got_q(side, 2, panel))
            self.p2[...] = self.p1[rows_at(64 * d2, 64), :] + self.a_rs_in[par, rows_at(64 * d2, 64), :]
            self.b_rs_out[0:64, :] = self.p1[rows_at(64 * (1 - d2), 64), :] + self.a_rs_in[par, rows_at(64 * (1 - d2), 64), :]

        @pl.when((t >= 1) & (t < self.count + 1))
        def _stage1():
            slot, row = self.grad_rows(t - 1)
            mine = rows_at(row + 64 * place.c, 64)

            def summed(lane):
                spot = lanes_at(lane, 128)
                return self.grad_ref[slot, mine, spot] + self.sib_in[par, :, spot]

            for half in range(2):
                self.p1[64 * half:64 * half + 64, :] = summed(256 * d1 + 128 * half)
                self.a_rs_out[64 * half:64 * half + 64, :] = summed(256 * (1 - d1) + 128 * half)
            ring = ring4(1)
            for panel in range(2):
                self.q1[ring, 64 * panel:64 * panel + 64, :] = summed(512 + 128 * panel)
            for side in range(2):
                @pl.when(lead[side] == 0)
                def _(side=side, ring=ring):
                    for panel in range(2):
                        put_q(side, 2, panel, self.q1[ring, rows_at(64 * panel + 16 * target(side, 1), 16), :])


T0 = (((0,), (0,)), ((), ()))
NT = (((1,), (1,)), ((), ()))


def mm(left, right):
    return jnp.dot(left, right, preferred_element_type=F32)


def mm_nt(left, right):
    return lax.dot_general(left, right, NT, preferred_element_type=F32)


def mm_t(left, right):
    return lax.dot_general(left, right, T0, preferred_element_type=F32)


def row_of(ref):
    return ref[...].reshape(1, -1)


def normal_cdf(pre):
    return 0.5 + 0.5 * lax.erf(pre * 0.7071067811865476), jnp.exp(-0.5 * pre * pre)


G0, D0 = 0, 4
X, Q, K, V, O, Y1, DZ, DA, DO = 8, 9, 10, 11, 12, 13, 14, 15, 16
N_ACTS = 17
ROWS = 512


class Net:
    def __init__(self, **refs):
        self.__dict__.update(refs)

    def project(self, i):
        rows = pl.ds(pl.multiple_of(i * ROWS, ROWS), ROWS)
        acts = self.acts
        x = acts[X, rows, :]
        acts[Q, rows, :] = (mm(x, self.w_q[...]) + row_of(self.query_bias)).astype(BF) * BF(0.125)
        acts[K, rows, :] = mm(x, self.w_k[...]).astype(BF)
        acts[V, rows, :] = (mm(x, self.w_v[...]) + row_of(self.value_bias)).astype(BF)

    def masks(self):
        place = lax.broadcasted_iota(jnp.int32, (8, 512), 1)
        for s in range(2):
            self.key_row[s] = jnp.where(place < self.lengths[s], 0.0, -1e9)

    def attend(self, i):
        s, pair = i // 6, lax.rem(i, 6)
        rows = pl.ds(pl.multiple_of(s * 512, 512), 512)
        lanes = lanes_at(pair * 128, 128)
        acts = self.acts
        k = acts[K, rows, lanes]
        v = acts[V, rows, lanes]
        lane = lax.broadcasted_iota(jnp.int32, (1, 128), 1)
        v_ones = jnp.concatenate([v, jnp.ones((512, 128), BF)], axis=1)
        q = acts[Q, rows, lanes]
        boths, tops = [], []
        for head in range(2):
            live = (lane >= 64) if head else (lane < 64)
            score = mm_nt(jnp.where(live, q, BF(0)), k) + self.key_row[s, 0:1, :]
            top = jnp.max(score, axis=1, keepdims=True)
            boths.append(mm(jnp.exp(score - top).astype(BF), v_ones))
            tops.append(top)
        pick = lane < 64
        mixed = jnp.where(pick, boths[0][:, :128], boths[1][:, :128])
        total = jnp.where(pick, boths[0][:, 128:], boths[1][:, 128:])
        acts[O, rows, lanes] = (mixed * pl.reciprocal(total, approx=False)).astype(BF)
        one, two = lane == 2 * pair, lane == 2 * pair + 1
        self.logs[s] = jnp.where(one, tops[0], jnp.where(two, tops[1], self.logs[s]))
        self.sums[s] = jnp.where(one, boths[0][:, 128:], jnp.where(two, boths[1][:, 128:], self.sums[s]))

    def normed(self, rows):
        mean = jnp.sum(rows, axis=1, keepdims=True) * (1.0 / 768)
        centred = rows - mean
        spread = jnp.sum(centred * centred, axis=1, keepdims=True) * (1.0 / 768)
        inverse = lax.rsqrt(spread + 1e-6)
        return centred * inverse, inverse

    def feed(self, i):
        rows = pl.ds(pl.multiple_of(i * ROWS, ROWS), ROWS)
        acts = self.acts
        h1 = acts[X, rows, :].astype(F32) + mm(acts[O, rows, :], self.w_m[...]) + row_of(self.mixer_bias)
        n1, r1 = self.normed(h1)
        self.n1[rows, :] = n1.astype(self.n1.dtype)
        self.r1[rows, :] = jnp.broadcast_to(r1, (ROWS, 128))
        y1 = n1 * row_of(self.first_gain) + row_of(self.first_shift)
        self.z[...] = y1 + row_of(self.shrink_bias)
        acts[Y1, rows, :] = y1.astype(BF)
        for j in range(4):
            self.feed_block(rows, j)
        n2, r2 = self.normed(self.z[...])
        self.n2[rows, :] = n2
        self.r2[rows, :] = jnp.broadcast_to(r2, (ROWS, 128))
        each = 512 // ROWS
        s, part = i // each, lax.rem(i, each)
        at = lax.broadcasted_iota(jnp.int32, (ROWS, 1), 0) + part * ROWS
        live = jnp.where(at < self.lengths[s], n2, 0.0)
        some = jnp.sum(live, axis=0, keepdims=True)
        self.n2_sum[s, 0:1, :] = jnp.where(part == 0, some, self.n2_sum[s, 0:1, :] + some)

    def feed_block(self, rows, j):
        acts = self.acts
        cols = pl.ds(768 * j, 768)
        pre = mm(acts[Y1, rows, :], self.w_e[:, cols]) + self.expand_bias[cols].reshape(1, 768)
        cdf, bell = normal_cdf(pre)
        low = (pre * cdf).astype(BF)
        acts[G0 + j, rows, :] = low
        acts[D0 + j, rows, :] = (cdf + pre * bell * 0.3989422804014327).astype(BF)
        self.z[...] += mm(low, self.w_s[cols, :])

    def pool(self, s):
        count = self.lengths[s].astype(F32)
        return self.n2_sum[s, 0:1, :] * row_of(self.second_gain) / count + row_of(self.second_shift)


class Back(Net):
    def turn_logs(self):
        for s in range(2):
            self.logs_t[s] = jnp.transpose(self.logs[s] + jnp.log(self.sums[s]))[0:16, :]

    def gather(self, place):
        c, chip = place.c, place.me // 2
        every = self.every
        for s in range(2):
            u = self.pool(s)
            for j in range(6):
                every[c, chip, 8 * s + j:8 * s + j + 1, :] = u[:, 128 * j:128 * j + 128]
            every[c, chip, 8 * s + 6:8 * s + 8, :] = jnp.full((2, 128), self.targets[s], F32)

        def copy(source, device):
            return pltpu.make_async_remote_copy(
                src_ref=every.at[c, source], dst_ref=every.at[c, source], send_sem=self.told.at[device // 2],
                recv_sem=self.heard.at[source], device_id=(device,), device_id_type=MESH)

        order = (12, 4, 13, 11, 3, 5, 14, 10, 2, 6, 15, 9, 1, 7, 8)
        for k in order:
            copy(chip, lax.rem(chip + k, 16) * 2 + c).start()
        for k in order:
            copy(lax.rem(chip + 16 - k, 16), place.me).wait_recv()
        share = pltpu.make_async_remote_copy(
            src_ref=every.at[c], dst_ref=every.at[c], send_sem=self.told.at[chip],
            recv_sem=self.heard.at[chip], device_id=(place.sibling,), device_id_type=MESH)
        share.start()
        for k in order:
            copy(chip, lax.rem(chip + k, 16) * 2 + c).wait_send()
        share.wait_send()
        share.wait_recv()

    def pair(self, place, s):
        here = place.me * 2 + s
        wanted = jnp.full((8, 128), self.partners[here], jnp.int32)
        mine = self.every[place.c, place.me // 2, 8 * s:8 * s + 8, :]

        def pick(i, found):
            far, near = found
            device = i // 2
            tile = self.every[lax.rem(device, 2), device // 2, rows_at(8 * lax.rem(i, 2), 8), :]
            far += jnp.where(wanted == i, tile, 0.0)
            near += jnp.where(jnp.full((8, 128), self.partners[i], jnp.int32) == here, tile, 0.0)
            return far, near

        nothing = jnp.zeros((8, 128), F32)
        far, near = lax.fori_loop(0, 64, pick, (nothing, nothing), unroll=8)
        live = lax.broadcasted_iota(jnp.int32, (8, 128), 0) < 6

        def inner(left, right):
            return jnp.sum(jnp.where(live, left * right, 0.0), axis=(0, 1), keepdims=True)

        length = jnp.sqrt(inner(mine, mine) + 1e-6)
        far_length = jnp.sqrt(inner(far, far) + 1e-6)
        near_length = jnp.sqrt(inner(near, near) + 1e-6)
        score = inner(mine, far) / (length * far_length)
        near_score = inner(near, mine) / (near_length * length)
        miss = score - mine[6:7, 0:1]
        near_miss = near_score - near[6:7, 0:1]
        own = mine / (length * length)
        grad = miss * (far / (length * far_length) - score * own)
        grad += near_miss * (near / (near_length * length) - near_score * own)
        for j in range(6):
            self.du[s, 0:1, 128 * j:128 * j + 128] = grad[j:j + 1, :]
        self.scores[s] = jnp.sum(score)

    def clear(self):
        self.vec[...] = jnp.zeros_like(self.vec)
        self.logs[...] = jnp.zeros_like(self.logs)
        self.sums[...] = jnp.ones_like(self.sums)

    def add_vec(self, at, rows):
        self.vec[at:at + 1, :] += jnp.sum(rows.astype(F32), axis=0, keepdims=True)

    def second_vectors(self):
        gain = jnp.zeros((1, 768), F32)
        for s in range(2):
            gain += self.du[s, 0:1, :] * self.n2_sum[s, 0:1, :] / self.lengths[s].astype(F32)
        self.vec[6:7, :] = gain
        self.vec[7:8, :] = self.du[0, 0:1, :] + self.du[1, 0:1, :]

    def back_second(self, i):
        rows = pl.ds(pl.multiple_of(i * 256, 256), 256)
        s = i // 2
        up = self.du[s, 0:1, :] * row_of(self.second_gain) / self.lengths[s].astype(F32)
        mean = jnp.sum(up, axis=1, keepdims=True) * (1.0 / 768)
        n2 = self.n2[rows, :]
        along = jnp.sum(n2 * up, axis=1, keepdims=True) * (1.0 / 768)
        at = lax.broadcasted_iota(jnp.int32, (256, 1), 0) + lax.rem(i, 2) * 256
        dh2 = jnp.where(at < self.lengths[s], self.r2[rows, 0:1] * (up - mean - n2 * along), 0.0)
        self.n2[rows, :] = dh2
        dz = dh2.astype(BF)
        self.acts[DZ, rows, :] = dz
        self.add_vec(5, dz)

    def back_hidden(self, i):
        j, half = i // 2, lax.rem(i, 2)
        rows = pl.ds(pl.multiple_of(half * 512, 512), 512)
        units = pl.ds(pl.multiple_of(j * 768, 768), 768)
        df = (mm_nt(self.acts[DZ, rows, :], self.w_s[units, :]) * self.acts[D0 + j, rows, :].astype(F32)).astype(BF)
        self.acts[D0 + j, rows, :] = df
        part = jnp.sum(df.astype(F32), axis=0, keepdims=True)
        line = lax.broadcasted_iota(jnp.int32, (8, 768), 0) == j
        self.vec[8:16, :] += jnp.where(line, part, 0.0)

    def back_first(self, i):
        rows = pl.ds(pl.multiple_of(i * 256, 256), 256)
        acts = self.acts
        up = self.n2[rows, :]
        for j in range(4):
            up += mm_nt(acts[D0 + j, rows, :], self.w_e[:, 768 * j:768 * j + 768])
        n1 = self.n1[rows, :].astype(F32)
        self.add_vec(3, up * n1)
        self.add_vec(4, up)
        dn = up * row_of(self.first_gain)
        mean = jnp.sum(dn, axis=1, keepdims=True) * (1.0 / 768)
        along = jnp.sum(dn * n1, axis=1, keepdims=True) * (1.0 / 768)
        dh1 = self.r1[rows, 0:1] * (dn - mean - n1 * along)
        self.n2[rows, :] = dh1
        da = dh1.astype(BF)
        acts[DA, rows, :] = da
        self.add_vec(2, da)
        acts[DO, rows, :] = mm_nt(da, self.w_m[...]).astype(BF)

    def attend_back(self, i):
        s, head = i // 12, lax.rem(i, 12)
        rows = pl.ds(pl.multiple_of(s * 512, 512), 512)
        lanes = lanes_at((head // 2) * 128, 128)
        acts = self.acts
        lane = lax.broadcasted_iota(jnp.int32, (1, 128), 1)
        live = (lane // 64) == lax.rem(head, 2)
        q_all, k, v = acts[Q, rows, lanes], acts[K, rows, lanes], acts[V, rows, lanes]
        q = jnp.where(live, q_all, BF(0))
        up = jnp.where(live, acts[DO, rows, lanes], BF(0))
        place = lax.broadcasted_iota(jnp.int32, (512, 1), 0)
        off = jnp.where(place < self.lengths[s], 0.0, -1e9)
        probs = jnp.exp(mm_nt(k, q) + off - self.logs_t[s, pl.ds(head, 1), :])
        weighed = probs * mm_nt(v, up)
        delta = jnp.sum(weighed, axis=0, keepdims=True)
        ds = (weighed - probs * delta).astype(BF)
        dv = mm(probs.astype(BF), up)
        dk = mm(ds, q)
        dq = mm_t(ds, k) * 0.125
        acts[Q, rows, lanes] = jnp.where(live, dq.astype(BF), q_all)
        acts[K, rows, lanes] = jnp.where(live, dk.astype(BF), k)
        acts[V, rows, lanes] = jnp.where(live, dv.astype(BF), v)

    def token_copy(self, i):
        rows = pl.ds(pl.multiple_of(i * 256, 256), 256)
        return pltpu.make_async_copy(self.n2.at[rows], self.tokens_grad.at[rows], self.wrote.at[i])

    def back_tokens(self, i):
        rows = pl.ds(pl.multiple_of(i * 256, 256), 256)
        dq, dk, dv = self.acts[Q, rows, :], self.acts[K, rows, :], self.acts[V, rows, :]
        self.add_vec(0, dq)
        self.add_vec(1, dv)
        self.n2[rows, :] += mm_nt(dq, self.w_q[...]) + mm_nt(dk, self.w_k[...]) + mm_nt(dv, self.w_v[...])
        self.token_copy(i).start()

    def back_task(self, i):
        pl.when(i < 8)(lambda: self.back_hidden(i))
        pl.when((i >= 8) & (i < 12))(lambda: self.back_first(i - 8))
        pl.when((i >= 12) & (i < 36))(lambda: self.attend_back(i - 12))
        pl.when((i >= 36) & (i < 40))(lambda: self.back_tokens(i - 36))

    def grad_piece(self, i):
        b = i // 3
        slot = lax.rem(i, 2)
        cols = pl.ds(pl.multiple_of(lax.rem(i, 3) * 256, 256), 256)
        left = jnp.where(b < 4, G0 + b, jnp.where(b < 8, Y1, jnp.where(b < 9, O, X)))
        right = jnp.where(b < 4, DZ, jnp.where(b < 8, D0 + b - 4, jnp.where(b < 9, DA, b)))
        self.ring[slot] = mm_t(self.acts[left, :, cols], self.acts[right])


N_IN = 19
VECTORS = ("query_bias", "value_bias", "mixer_bias", "first_gain", "first_shift", "shrink_bias", "second_gain",
           "second_shift")


def layer_kernel(*refs):
    (tokens, lengths, partners, targets, w_q, query_bias, w_k, w_v, value_bias, w_m, mixer_bias, first_gain,
     first_shift, w_e, expand_bias, w_s, shrink_bias, second_gain, second_shift) = refs[:N_IN]
    scores, tokens_grad, summed = refs[N_IN:N_IN + 3]
    rest = refs[N_IN + 3:]
    (acts, v_q, v_k, v_v, v_m, v_e, v_s, key_row, logs, sums, logs_t, n1, r1, n2, r2, z, n2_sum, every, du, vec, ring,
     loaded, told, heard, wrote) = rest[:25]
    first, second = rest[25:25 + N_STREAM_SCRATCH], rest[25 + N_STREAM_SCRATCH:]
    place = Place()
    net = Back(
        acts=acts, w_q=v_q, w_k=v_k, w_v=v_v, w_m=v_m, w_e=v_e, w_s=v_s, query_bias=query_bias, value_bias=value_bias,
        mixer_bias=mixer_bias, first_gain=first_gain, first_shift=first_shift, expand_bias=expand_bias,
        shrink_bias=shrink_bias, second_gain=second_gain, second_shift=second_shift, lengths=lengths,
        partners=partners, targets=targets, scores=scores, tokens_grad=tokens_grad, key_row=key_row, logs=logs, sums=sums,
        logs_t=logs_t, n1=n1, r1=r1, n2=n2, r2=r2, z=z, n2_sum=n2_sum, every=every, du=du, vec=vec, ring=ring,
        told=told, heard=heard, wrote=wrote)
    loads = [pltpu.make_async_copy(src, dst, loaded.at[i]) for i, (src, dst) in enumerate([
        (tokens, acts.at[X]), (w_q, v_q), (w_k, v_k), (w_v, v_v), (w_m, v_m), (w_e, v_e), (w_s, v_s)])]
    for copy in loads[:4]:
        copy.start()

    def chunk_rows(t, shift):
        t = jnp.clip(t, 0, 36)
        return lax.rem(t, 2), shift

    def out_rows(t, shift):
        return jnp.clip(t, 0, 36) * 256 + shift

    one = Stream(place, 0, 37, first, ring, lambda t: chunk_rows(t, 0), summed, lambda t: out_rows(t, 0))
    two = Stream(place, 1, 36, second, ring, lambda t: chunk_rows(t, 128), summed, lambda t: out_rows(t, 128))
    one.prepare()
    two.prepare()
    greet_all(place)

    def each(count, task):
        def step(i, carry):
            task(i)
            return carry

        lax.fori_loop(0, count, step, 0)

    net.masks()
    net.clear()
    for copy in loads[:4]:
        copy.wait()
    for copy in loads[4:]:
        copy.start()
    each(1024 // ROWS, net.project)
    each(12, net.attend)
    net.turn_logs()
    for copy in loads[4:]:
        copy.wait()
    each(1024 // ROWS, net.feed)
    await_all()
    net.gather(place)
    for s in range(2):
        net.pair(place, s)
    net.second_vectors()
    each(4, net.back_second)

    first_task = 12

    def step(turn, carry):
        t = turn // 2 - 1
        side = lax.rem(turn, 2)

        @pl.when(turn == 74)
        def _():
            ring[0, 0:128, :] = jnp.zeros((128, 768), F32)
            ring[0, 0:16, :] = vec[...]

        for i, stream in enumerate((one, two)):
            @pl.when((side == i) & (t >= 0))
            def _(stream=stream):
                stream.wait(t - 1)
                stream.work(t)
                stream.start(t)

        pl.when((side == 1) & (t + 1 < 36))(lambda: net.grad_piece(t + 1))
        task = turn - 2 - first_task
        pl.when((task >= 0) & (task < 40))(lambda: net.back_task(task))
        return carry

    lax.fori_loop(1, 2 * 49 + 2, step, 0)
    for i in range(4):
        net.token_copy(i).wait()


def greet_all(place):
    bar = pltpu.get_barrier_semaphore()
    chip = place.me // 2

    def hail(k, carry):
        pl.semaphore_signal(bar, 1, device_id=(lax.rem(chip + k, 16) * 2 + place.c,), device_id_type=MESH)
        return carry

    pl.semaphore_signal(bar, 1, device_id=(place.sibling,), device_id_type=MESH)
    lax.fori_loop(1, 16, hail, 0)


def await_all():
    pl.semaphore_wait(pltpu.get_barrier_semaphore(), 16)


def whole_layer(*args):
    anywhere = pl.BlockSpec(memory_space=pl.ANY)
    vector = pl.BlockSpec(memory_space=pltpu.VMEM)
    scalars = pl.BlockSpec(memory_space=pltpu.SMEM)
    specs = [anywhere if a.dtype == BF else vector if a.shape[0] >= 768 else scalars for a in args]

    def low(*shape):
        return pltpu.VMEM(shape, BF)

    def full(*shape):
        return pltpu.VMEM(shape, F32)

    return pl.pallas_call(
        layer_kernel,
        out_shape=(
            jax.ShapeDtypeStruct((2,), F32),
            jax.ShapeDtypeStruct((1024, 768), F32),
            jax.ShapeDtypeStruct((73 * 128, 768), F32),
        ),
        in_specs=specs,
        out_specs=(scalars, anywhere, anywhere),
        scratch_shapes=[
            low(N_ACTS, 1024, 768),
            low(768, 768), low(768, 768), low(768, 768), low(768, 768), low(768, 3072), low(3072, 768),
            full(2, 8, 512), full(2, 512, 128), full(2, 512, 128), full(2, 16, 512),
            full(1024, 768), full(1024, 128), full(1024, 768), full(1024, 128), full(ROWS, 768), full(2, 8, 768),
            full(2, 16, 16, 128), full(2, 8, 768), full(16, 768), full(2, 256, 768),
            pltpu.SemaphoreType.DMA((7,)), pltpu.SemaphoreType.DMA((16,)), pltpu.SemaphoreType.DMA((16,)),
            pltpu.SemaphoreType.DMA((4,)),
        ] + stream_scratch() + stream_scratch(),
        compiler_params=pltpu.CompilerParams(
            collective_id=0, has_side_effects=True, vmem_limit_bytes=63 << 20),
    )(*args)


def deliver_kernel(count, height, summed, tokens_sum, scores, *refs):
    (scores_out, tokens_out, w_q, query_bias, w_k, w_v, value_bias, w_m, mixer_bias, first_gain, first_shift, w_e,
     expand_bias, w_s, shrink_bias, second_gain, second_shift) = refs[:17]
    buffer, small, came, left, small_came = refs[17:]
    jobs = []
    for row in range(0, 3072, height):
        jobs.append((summed.at[pl.ds(row, height)], w_s.at[pl.ds(row, height)]))
    for row in range(0, 3072, height):
        block, at = row // 768, row % 768
        jobs.append((summed.at[pl.ds(3072 + row, height)], w_e.at[pl.ds(at, height), pl.ds(768 * block, 768)]))
    for row in range(0, 3072, height):
        block, at = row // 768, row % 768
        jobs.append((summed.at[pl.ds(6144 + row, height)], (w_m, w_q, w_k, w_v)[block].at[pl.ds(at, height)]))
    rows = tokens_sum.shape[0]
    for row in range(0, rows, height):
        size = min(height, rows - row)
        jobs.append((tokens_sum.at[pl.ds(row, size)], tokens_out.at[pl.ds(row, size)]))

    def copies(i):
        src, dst = jobs[i]
        spot = buffer.at[i % count, pl.ds(0, src.shape[0])]
        return (pltpu.make_async_copy(src, spot, came.at[i % count]),
                pltpu.make_async_copy(spot, dst, left.at[i % count]))

    total = len(jobs)
    ahead = count // 2
    vectors = pltpu.make_async_copy(summed.at[pl.ds(9216, 16)], small, small_came)
    vectors.start()
    for i in range(min(ahead, total)):
        copies(i)[0].start()
    for i in range(total):
        copies(i)[0].wait()
        copies(i)[1].start()
        later = i + ahead
        if later < total:
            if later >= count:
                copies(later - count)[1].wait()
            copies(later)[0].start()
        if i == 0:
            vectors.wait()
            for j, ref in enumerate((query_bias, value_bias, mixer_bias, first_gain, first_shift, shrink_bias,
                                     second_gain, second_shift)):
                ref[...] = small[j, :]
            for j in range(4):
                expand_bias[768 * j:768 * j + 768] = small[8 + j, :]
            for s in range(2):
                scores_out[s] = scores[s]
    for i in range(max(0, total - count), total):
        copies(i)[1].wait()


def fused(*args):
    pair_scores, tokens_grad, summed = whole_layer(*args)
    anywhere = pl.BlockSpec(memory_space=pl.ANY)
    vector = pl.BlockSpec(memory_space=pltpu.VMEM)
    scalars = pl.BlockSpec(memory_space=pltpu.SMEM)
    shapes = [(2,), (1024, 768), (768, 768), (768,), (768, 768), (768, 768), (768,), (768, 768), (768,), (768,), (768,),
              (768, 3072), (3072,), (3072, 768), (768,), (768,), (768,)]
    count, height = 16, 384
    return tuple(pl.pallas_call(
        partial(deliver_kernel, count, height),
        out_shape=[jax.ShapeDtypeStruct(shape, F32) for shape in shapes],
        in_specs=[anywhere, pl.BlockSpec(memory_space=pltpu.HBM), scalars],
        out_specs=[anywhere if len(shape) == 2 else vector if shape[0] > 2 else scalars for shape in shapes],
        scratch_shapes=[pltpu.VMEM((count, height, 768), F32), pltpu.VMEM((16, 768), F32),
                        pltpu.SemaphoreType.DMA((count,)), pltpu.SemaphoreType.DMA((count,)),
                        pltpu.SemaphoreType.DMA],
        compiler_params=pltpu.CompilerParams(vmem_limit_bytes=60 << 20),
    )(summed, tokens_grad, pair_scores))


def to_low(value):
    return value.astype(jnp.bfloat16)


def tdot(left, right):
    return lax.dot_general(
        left, right, (((0,), (0,)), ((), ())), preferred_element_type=jnp.float32
    )


def ndot(left, right):
    return lax.dot_general(
        left, right, (((1,), (1,)), ((), ())), preferred_element_type=jnp.float32
    )


def norm_rows(rows, gain, shift):
    mean = jnp.mean(rows, axis=-1, keepdims=True)
    centred = rows - mean
    spread = jnp.mean(centred * centred, axis=-1, keepdims=True)
    inverse = lax.rsqrt(spread + 1e-06)
    normed = centred * inverse
    return (normed * gain + shift, normed, inverse)


def norm_back(upstream, normed, inverse, gain):
    gain_grad = jnp.sum(upstream * normed, axis=0)
    shift_grad = jnp.sum(upstream, axis=0)
    dnormed = upstream * gain
    first_mean = jnp.mean(dnormed, axis=-1, keepdims=True)
    second_mean = jnp.mean(dnormed * normed, axis=-1, keepdims=True)
    return (inverse * (dnormed - first_mean - normed * second_mean), gain_grad, shift_grad)


def per_device(
    tokens,
    lengths,
    partners,
    targets,
    query_proj,
    query_bias,
    key_proj,
    value_proj,
    value_bias,
    mixer_proj,
    mixer_bias,
    first_gain,
    first_shift,
    expand_proj,
    expand_bias,
    shrink_proj,
    shrink_bias,
    second_gain,
    second_shift,
):
    sents = lengths.shape[0]
    rows_all = tokens.shape[0]
    slot = rows_all // sents
    width = tokens.shape[1]
    heads = H
    depth = width // heads
    scale = 1.0 / math.sqrt(depth)
    total = partners.shape[0]
    base = lax.axis_index("dp") * sents
    highest = lax.Precision.HIGHEST
    places = jnp.arange(slot, dtype=jnp.int32)
    valid = places[None, :] < lengths[:, None]
    row_mask = valid.reshape(rows_all, 1).astype(jnp.float32)
    shape4 = (sents, slot, heads, depth)
    queries = to_low(jnp.dot(tokens, query_proj, preferred_element_type=jnp.float32) + query_bias)
    keys = to_low(jnp.dot(tokens, key_proj, preferred_element_type=jnp.float32))
    values = to_low(jnp.dot(tokens, value_proj, preferred_element_type=jnp.float32) + value_bias)
    queries4 = queries.reshape(shape4)
    keys4 = keys.reshape(shape4)
    values4 = values.reshape(shape4)

    def masked_scores(query_rows, key_rows, live):
        raw = (
            jnp.einsum("qhd,khd->hqk", query_rows, key_rows, preferred_element_type=jnp.float32)
            * scale
        )
        return jnp.where(live[None, None, :], raw, -1000000000.0)

    def attend(item):
        query_rows, key_rows, value_rows, live = item
        raw = masked_scores(query_rows, key_rows, live)
        top = jnp.max(raw, axis=-1, keepdims=True)
        expd = jnp.exp(raw - top)
        summed = jnp.sum(expd, axis=-1, keepdims=True)
        probs = to_low(expd / summed)
        mixed = jnp.einsum("hqk,khd->qhd", probs, value_rows, preferred_element_type=jnp.float32)
        return (mixed, (top + jnp.log(summed))[..., 0])

    mixed, logsum = lax.map(attend, (queries4, keys4, values4, valid))
    mixed_low = to_low(mixed.reshape(rows_all, width))
    branch = jnp.dot(mixed_low, mixer_proj, preferred_element_type=jnp.float32) + mixer_bias
    first_out, first_normed, first_inverse = norm_rows(
        tokens.astype(jnp.float32) + branch, first_gain, first_shift
    )
    first_low = to_low(first_out)
    pre = jnp.dot(first_low, expand_proj, preferred_element_type=jnp.float32) + expand_bias
    act, gelu_back = jax.vjp(partial(jax.nn.gelu, approximate=False), pre)
    act_low = to_low(act)
    shrink = jnp.dot(act_low, shrink_proj, preferred_element_type=jnp.float32) + shrink_bias
    outputs, second_normed, second_inverse = norm_rows(
        first_out + shrink, second_gain, second_shift
    )
    counts = lengths.astype(jnp.float32)
    pooled = jnp.sum((outputs * row_mask).reshape(sents, slot, width), axis=1) / counts[:, None]
    mine = lax.dynamic_slice_in_dim(partners, base, sents)
    every = lax.all_gather(pooled, "dp", axis=0, tiled=True)
    partner_vec = jnp.take(every, mine, axis=0)
    inner = jnp.sum(pooled * partner_vec, axis=-1)
    own_len = jnp.sqrt(jnp.sum(pooled * pooled, axis=-1) + 1e-06)
    far_len = jnp.sqrt(jnp.sum(partner_vec * partner_vec, axis=-1) + 1e-06)
    pair_scores = inner / (own_len * far_len)
    miss = pair_scores - targets
    joint = (own_len * far_len)[:, None]
    dpooled = miss[:, None] * (
        partner_vec / joint - (pair_scores / (own_len * own_len))[:, None] * pooled
    )
    dpartner = miss[:, None] * (
        pooled / joint - (pair_scores / (far_len * far_len))[:, None] * partner_vec
    )
    owners = (mine[:, None] == jnp.arange(total, dtype=jnp.int32)[None, :]).astype(jnp.float32)
    spread = lax.dot_general(owners, dpartner, (((0,), (0,)), ((), ())), precision=highest)
    returned = lax.psum_scatter(spread, "dp", scatter_dimension=0, tiled=True)
    dpool_all = (dpooled + returned) / counts[:, None]
    doutputs = (dpool_all[:, None, :] * valid[:, :, None].astype(jnp.float32)).reshape(
        rows_all, width
    )
    dsecond, second_gain_grad, second_shift_grad = norm_back(
        doutputs, second_normed, second_inverse, second_gain
    )
    dshrink = to_low(dsecond)
    shrink_proj_grad = tdot(act_low, dshrink)
    shrink_bias_grad = jnp.sum(dshrink.astype(jnp.float32), axis=0)
    dact = ndot(dshrink, shrink_proj)
    dpre = to_low(gelu_back(dact)[0])
    expand_proj_grad = tdot(first_low, dpre)
    expand_bias_grad = jnp.sum(dpre.astype(jnp.float32), axis=0)
    dfirst_out = ndot(dpre, expand_proj) + dsecond
    dfirst, first_gain_grad, first_shift_grad = norm_back(
        dfirst_out, first_normed, first_inverse, first_gain
    )
    dbranch = to_low(dfirst)
    mixer_proj_grad = tdot(mixed_low, dbranch)
    mixer_bias_grad = jnp.sum(dbranch.astype(jnp.float32), axis=0)
    dmixed = to_low(ndot(dbranch, mixer_proj)).reshape(shape4)

    def attend_back(item):
        query_rows, key_rows, value_rows, live, row_logsum, dmix = item
        raw = masked_scores(query_rows, key_rows, live)
        probs = jnp.exp(raw - row_logsum[..., None])
        probs_low = to_low(probs)
        dprob = jnp.einsum("qhd,khd->hqk", dmix, value_rows, preferred_element_type=jnp.float32)
        delta = jnp.sum(dprob * probs, axis=-1, keepdims=True)
        dscore = to_low(probs * (dprob - delta))
        dquery = (
            jnp.einsum("hqk,khd->qhd", dscore, key_rows, preferred_element_type=jnp.float32) * scale
        )
        dkey = (
            jnp.einsum("hqk,qhd->khd", dscore, query_rows, preferred_element_type=jnp.float32)
            * scale
        )
        dvalue = jnp.einsum("hqk,qhd->khd", probs_low, dmix, preferred_element_type=jnp.float32)
        return (to_low(dquery), to_low(dkey), to_low(dvalue))

    dquery, dkey, dvalue = lax.map(attend_back, (queries4, keys4, values4, valid, logsum, dmixed))
    dquery = dquery.reshape(rows_all, width)
    dkey = dkey.reshape(rows_all, width)
    dvalue = dvalue.reshape(rows_all, width)
    query_proj_grad = tdot(tokens, dquery)
    query_bias_grad = jnp.sum(dquery.astype(jnp.float32), axis=0)
    key_proj_grad = tdot(tokens, dkey)
    value_proj_grad = tdot(tokens, dvalue)
    value_bias_grad = jnp.sum(dvalue.astype(jnp.float32), axis=0)
    tokens_grad = (
        ndot(dquery, query_proj) + ndot(dkey, key_proj) + ndot(dvalue, value_proj) + dfirst
    )
    (
        query_proj_grad,
        query_bias_grad,
        key_proj_grad,
        value_proj_grad,
        value_bias_grad,
        mixer_proj_grad,
        mixer_bias_grad,
        first_gain_grad,
        first_shift_grad,
        expand_proj_grad,
        expand_bias_grad,
        shrink_proj_grad,
        shrink_bias_grad,
        second_gain_grad,
        second_shift_grad,
    ) = lax.psum(
        (
            query_proj_grad,
            query_bias_grad,
            key_proj_grad,
            value_proj_grad,
            value_bias_grad,
            mixer_proj_grad,
            mixer_bias_grad,
            first_gain_grad,
            first_shift_grad,
            expand_proj_grad,
            expand_bias_grad,
            shrink_proj_grad,
            shrink_bias_grad,
            second_gain_grad,
            second_shift_grad,
        ),
        "dp",
    )
    return (
        pair_scores,
        tokens_grad,
        query_proj_grad,
        query_bias_grad,
        key_proj_grad,
        value_proj_grad,
        value_bias_grad,
        mixer_proj_grad,
        mixer_bias_grad,
        first_gain_grad,
        first_shift_grad,
        expand_proj_grad,
        expand_bias_grad,
        shrink_proj_grad,
        shrink_bias_grad,
        second_gain_grad,
        second_shift_grad,
    )


def solution(mesh):
    in_specs = (
        P("dp", None),
        P("dp"),
        P(),
        P("dp"),
        P(),
        P(),
        P(),
        P(),
        P(),
        P(),
        P(),
        P(),
        P(),
        P(),
        P(),
        P(),
        P(),
        P(),
        P(),
    )
    out_specs = (
        P("dp"),
        P("dp", None),
        P(),
        P(),
        P(),
        P(),
        P(),
        P(),
        P(),
        P(),
        P(),
        P(),
        P(),
        P(),
        P(),
        P(),
        P(),
    )
    plain = mesh.shape["dp"] != 32
    return jax.shard_map(
        per_device if plain else fused, mesh=mesh, in_specs=in_specs, out_specs=out_specs, check_vma=False
    )
```

```python
from functools import partial
import math

import jax
import jax.numpy as jnp
from jax import lax
from jax.sharding import PartitionSpec as P

from jax.experimental import pallas as pl
from jax.experimental.pallas import tpu as pltpu

H = 12

MESH = pl.DeviceIdType.MESH
F32 = jnp.float32
BF = jnp.bfloat16


def rows16(index):
    return pl.ds(pl.multiple_of(index * 16, 16), 16)


def rows_at(start, size):
    return pl.ds(pl.multiple_of(start, 8), size)


def lanes_at(start, size):
    return pl.ds(pl.multiple_of(start, 128), size)


class Place:
    def __init__(self):
        me = lax.axis_index("dp")
        self.me = me
        self.c = me % 2
        self.x = (me // 2) % 2
        self.y = (me // 4) % 2
        self.z = me // 8
        self.sibling = me + 1 - 2 * self.c
        self.to_x = me + 2 - 4 * self.x
        self.to_y = me + 4 - 8 * self.y
        self.up = me + 8
        self.down = me - 8


def stream_scratch():
    return [
        pltpu.VMEM((2, 64, 768), F32),
        pltpu.VMEM((144, 128), F32),
        pltpu.VMEM((2, 144, 128), F32),
        pltpu.VMEM((144, 128), F32),
        pltpu.VMEM((2, 144, 128), F32),
        pltpu.VMEM((72, 128), F32),
        pltpu.VMEM((2, 72, 128), F32),
        pltpu.VMEM((72, 128), F32),
        pltpu.VMEM((2, 72, 128), F32),
        pltpu.VMEM((2, 192, 128), F32),
        pltpu.VMEM((2, 2, 192, 128), F32),
        pltpu.VMEM((128, 128), F32),
        pltpu.VMEM((64, 128), F32),
        pltpu.VMEM((4, 64, 128), F32),
        pltpu.VMEM((4, 128, 128), F32),
        pltpu.VMEM((16, 128), F32),
        pltpu.VMEM((8, 128), F32),
        pltpu.VMEM((8, 64, 768), F32),
        pltpu.SemaphoreType.DMA((10, 2)),
        pltpu.SemaphoreType.DMA((10, 2)),
        pltpu.SemaphoreType.DMA((2,)),
    ]


N_STREAM_SCRATCH = 21


class Stream:
    def __init__(self, place, which, count, refs, grad_ref, grad_rows, outs):
        (self.sib_in, self.a_rs_out, self.a_rs_in, self.a_ag_out, self.a_ag_in, self.b_rs_out, self.b_rs_in,
         self.b_ag_out, self.b_ag_in, self.z_out, self.z_in, self.p1, self.p2, self.p3, self.q1, self.q2, self.q3,
         self.full, self.sent, self.came, self.kept) = refs
        self.place = place
        self.count = count
        self.grad_ref = grad_ref
        self.grad_rows = grad_rows
        self.outs = outs
        if which == 0:
            self.d1, self.d2, self.to_a, self.to_b = place.x, place.y, place.to_x, place.to_y
        else:
            self.d1, self.d2, self.to_a, self.to_b = place.y, place.x, place.to_y, place.to_x

    def prepare(self):
        zero = jnp.zeros((192, 128), F32)
        for side in range(2):
            for parity in range(2):
                self.z_in[side, parity] = zero

    def copies(self, t):
        place, n = self.place, self.count
        par = t % 2

        def remote(i, src, dst, target):
            return pltpu.make_async_remote_copy(
                src_ref=src, dst_ref=dst, send_sem=self.sent.at[i, par], recv_sem=self.came.at[i, par],
                device_id=(target,), device_id_type=MESH)

        def tail(i, src, dst, at, size, target):
            return remote(i, src.at[pl.ds(at, size)], dst.at[par, pl.ds(at, size)], target)

        slot, row = self.grad_rows(t)
        other = rows_at(row + 64 * (1 - place.c), 64)
        m = t - 11
        ring = lax.rem(t + 5, 8)
        outs = self.outs(m, 64 * place.c)
        lead = (place.z, 3 - place.z)
        zs = []
        for side, device in ((0, place.up), (1, place.down)):
            for half, when in ((0, (t >= 1) & (t < n + 5)), (1, (t >= 6) & (t < n + 10))):
                for k in range(3):
                    at, size = (0, 144 - 48 * k) if half == 0 else (144 - 48 * k, 48 + 48 * k)
                    spot = pl.ds(at, size)
                    copy = remote(5 + 2 * side + half, self.z_out.at[side, spot], self.z_in.at[side, par, spot], device)
                    zs.append((copy, when, lead[side] == k, lead[side] == k + 1))
        return [
            (remote(0, self.grad_ref.at[slot, other], self.sib_in.at[par], place.sibling), (t >= 0) & (t < n), True, True),
            (remote(1, self.a_rs_out, self.a_rs_in.at[par], self.to_a), (t >= 1) & (t < n + 1), True, True),
            (tail(1, self.a_rs_out, self.a_rs_in, 128, 16, self.to_a), (t >= n + 1) & (t < n + 4), True, True),
            (tail(2, self.a_ag_out, self.a_ag_in, 128, 16, self.to_a), (t >= 7) & (t < 10), True, True),
            (remote(2, self.a_ag_out, self.a_ag_in.at[par], self.to_a), (t >= 10) & (t < n + 10), True, True),
            (remote(3, self.b_rs_out, self.b_rs_in.at[par], self.to_b), (t >= 2) & (t < n + 2), True, True),
            (tail(3, self.b_rs_out, self.b_rs_in, 64, 8, self.to_b), (t >= n + 2) & (t < n + 5), True, True),
            (tail(4, self.b_ag_out, self.b_ag_in, 64, 8, self.to_b), (t >= 6) & (t < 9), True, True),
            (remote(4, self.b_ag_out, self.b_ag_in.at[par], self.to_b), (t >= 9) & (t < n + 9), True, True),
        ] + zs + [
            (remote(9, self.full.at[ring], spot, place.sibling), (t >= 11) & (t < n + 11) & when, True, True)
            for spot, when in outs
        ], [(pltpu.make_async_copy(self.full.at[ring], spot, self.kept.at[par]), (t >= 11) & (t < n + 11) & when)
            for spot, when in outs]

    def start(self, t):
        remote, local = self.copies(t)
        for copy, when, sends, _ in remote:
            pl.when(when if sends is True else when & sends)(copy.start)
        for copy, when in local:
            pl.when(when)(copy.start)

    def wait(self, t):
        remote, local = self.copies(t)
        for copy, when, sends, takes in remote:
            if sends is True:
                @pl.when(when)
                def _(copy=copy):
                    copy.wait_send()
                    copy.wait_recv()
            else:
                pl.when(when & sends)(copy.wait_send)
                pl.when(when & takes)(copy.wait_recv)
        for copy, when in local:
            pl.when(when)(copy.wait)

    def work(self, t):
        place = self.place
        z, d1, d2 = place.z, self.d1, self.d2
        par = (t + 1) % 2
        z_in, z_out = self.z_in, self.z_out
        lead = (z, 3 - z)

        def far(side, k):
            return z - k if side == 0 else z + k

        def target(side, step):
            return z + 4 - step if side == 0 else z - 4 + step

        def ring4(stage):
            return lax.rem(t + 16 - stage, 4)

        def ring8(stage):
            return lax.rem(t + 16 - stage, 8)

        def got_p(side, pos):
            return z_in[side, par, 48 * pos:48 * pos + 16, :]

        def got_q(side, pos, panel):
            at = 48 * pos + 16 + 16 * panel
            return z_in[side, par, at:at + 16, :]

        def put_p(side, pos, value):
            z_out[side, 48 * pos:48 * pos + 16, :] = value

        def put_q(side, pos, panel, value):
            at = 48 * pos + 16 + 16 * panel
            z_out[side, at:at + 16, :] = value

        def full_p(ring, block, value):
            self.full[ring, rows16(block), lanes_at((2 * d1 + d2) * 128, 128)] = value

        def full_q(ring, block, panel, value):
            self.full[ring, rows16(block), 512 + 128 * panel:640 + 128 * panel] = value

        @pl.when((t >= 11) & (t < self.count + 11))
        def _stage11():
            ring = ring8(11)
            self.full[ring, :, lanes_at((1 - d1) * 256, 128)] = self.a_ag_in[par, 0:64, :]
            self.full[ring, :, lanes_at((1 - d1) * 256 + 128, 128)] = self.a_ag_in[par, 64:128, :]
            for side in range(2):
                @pl.when(lead[side] == 3)
                def _(side=side, ring=ring):
                    for panel in range(2):
                        full_q(ring, far(side, 3), panel, got_q(side, 1, panel))

        @pl.when((t >= 10) & (t < self.count + 10))
        def _stage10():
            ring = ring8(10)
            other = self.b_ag_in[par, 0:64, :]
            self.full[ring, :, lanes_at((2 * d1 + 1 - d2) * 128, 128)] = other
            self.a_ag_out[rows_at(64 * (1 - d2), 64), :] = other
            self.a_ag_out[rows_at(64 * d2, 64), :] = self.full[ring, :, lanes_at((2 * d1 + d2) * 128, 128)]
            for side in range(2):
                @pl.when(lead[side] >= 2)
                def _(side=side, ring=ring):
                    for panel in range(2):
                        value = got_q(side, 2, panel)
                        full_q(ring, far(side, 2), panel, value)
                        put_q(side, 1, panel, value)

        @pl.when((t >= 9) & (t < self.count + 9))
        def _stage9():
            ring = ring8(9)
            for side in range(2):
                @pl.when(lead[side] == 3)
                def _(side=side, ring=ring):
                    full_p(ring, far(side, 3), got_p(side, 1))

                @pl.when(lead[side] >= 1)
                def _(side=side, ring=ring):
                    for panel in range(2):
                        value = got_q(side, 3, panel)
                        full_q(ring, far(side, 1), panel, value)
                        put_q(side, 2, panel, value)
            self.b_ag_out[0:64, :] = self.full[ring, :, lanes_at((2 * d1 + d2) * 128, 128)]

        @pl.when((t >= 8) & (t < self.count + 8))
        def _stage8():
            ring = ring8(8)
            for side in range(2):
                @pl.when(lead[side] >= 2)
                def _(side=side, ring=ring):
                    value = got_p(side, 2)
                    full_p(ring, far(side, 2), value)
                    put_p(side, 1, value)
            self.full[ring, rows16(z), lanes_at(512 + 128 * (1 - d1), 128)] = self.a_ag_in[par, 128:144, :]
            for panel in range(2):
                value = self.full[ring, rows16(z), 512 + 128 * panel:640 + 128 * panel]
                for side in range(2):
                    put_q(side, 3, panel, value)

        @pl.when((t >= 7) & (t < self.count + 7))
        def _stage7():
            ring = ring8(7)
            for side in range(2):
                @pl.when(lead[side] >= 1)
                def _(side=side, ring=ring):
                    value = got_p(side, 3)
                    full_p(ring, far(side, 1), value)
                    put_p(side, 2, value)
            self.full[ring, rows_at(16 * z + 8 * (1 - d2), 8), lanes_at(512 + 128 * d1, 128)] = self.b_ag_in[par, 64:72, :]
            self.a_ag_out[128:144, :] = self.full[ring, rows16(z), lanes_at(512 + 128 * d1, 128)]

        @pl.when((t >= 6) & (t < self.count + 6))
        def _stage6():
            ring = ring8(6)
            value = self.p3[ring4(6), rows16(z), :] + got_p(0, 0) + got_p(1, 0)
            full_p(ring, z, value)
            put_p(0, 3, value)
            put_p(1, 3, value)
            value = self.q3[...] + self.b_rs_in[par, 64:72, :]
            self.full[ring, rows_at(16 * z + 8 * d2, 8), lanes_at(512 + 128 * d1, 128)] = value
            self.b_ag_out[64:72, :] = value

        @pl.when((t >= 5) & (t < self.count + 5))
        def _stage5():
            for side in range(2):
                @pl.when(lead[side] <= 2)
                def _(side=side):
                    put_p(side, 0, self.p3[ring4(5), rows16(target(side, 3)), :] + got_p(side, 1))
            self.q3[...] = self.q2[rows_at(8 * d2, 8), :] + self.a_rs_in[par, rows_at(128 + 8 * d2, 8), :]
            self.b_rs_out[64:72, :] = self.q2[rows_at(8 * (1 - d2), 8), :] + self.a_rs_in[par, rows_at(128 + 8 * (1 - d2), 8), :]

        @pl.when((t >= 4) & (t < self.count + 4))
        def _stage4():
            for side in range(2):
                @pl.when(lead[side] <= 1)
                def _(side=side):
                    put_p(side, 1, self.p3[ring4(4), rows16(target(side, 2)), :] + got_p(side, 2))
            ring = ring4(4)

            def own_q(panel):
                first = self.q1[ring, rows_at(64 * panel + 16 * z, 16), :]
                spot = rows_at(16 + 16 * panel, 16)
                return first + z_in[0, par, spot, :] + z_in[1, par, spot, :]

            self.q2[...] = own_q(d1)
            self.a_rs_out[128:144, :] = own_q(1 - d1)

        @pl.when((t >= 3) & (t < self.count + 3))
        def _stage3():
            for side in range(2):
                @pl.when(lead[side] <= 2)
                def _(side=side):
                    for panel in range(2):
                        own = self.q1[ring4(3), rows_at(64 * panel + 16 * target(side, 3), 16), :]
                        put_q(side, 0, panel, own + got_q(side, 1, panel))
            ring = ring4(3)
            self.p3[ring] = self.p2[...] + self.b_rs_in[par, 0:64, :]
            for side in range(2):
                @pl.when(lead[side] == 0)
                def _(side=side, ring=ring):
                    put_p(side, 2, self.p3[ring, rows16(target(side, 1)), :])

        @pl.when((t >= 2) & (t < self.count + 2))
        def _stage2():
            for side in range(2):
                @pl.when(lead[side] <= 1)
                def _(side=side):
                    for panel in range(2):
                        own = self.q1[ring4(2), rows_at(64 * panel + 16 * target(side, 2), 16), :]
                        put_q(side, 1, panel, own + got_q(side, 2, panel))
            self.p2[...] = self.p1[rows_at(64 * d2, 64), :] + self.a_rs_in[par, rows_at(64 * d2, 64), :]
            self.b_rs_out[0:64, :] = self.p1[rows_at(64 * (1 - d2), 64), :] + self.a_rs_in[par, rows_at(64 * (1 - d2), 64), :]

        @pl.when((t >= 1) & (t < self.count + 1))
        def _stage1():
            slot, row = self.grad_rows(t - 1)
            mine = rows_at(row + 64 * place.c, 64)

            def summed(lane):
                spot = lanes_at(lane, 128)
                return self.grad_ref[slot, mine, spot] + self.sib_in[par, :, spot]

            for half in range(2):
                self.p1[64 * half:64 * half + 64, :] = summed(256 * d1 + 128 * half)
                self.a_rs_out[64 * half:64 * half + 64, :] = summed(256 * (1 - d1) + 128 * half)
            ring = ring4(1)
            for panel in range(2):
                self.q1[ring, 64 * panel:64 * panel + 64, :] = summed(512 + 128 * panel)
            for side in range(2):
                @pl.when(lead[side] == 0)
                def _(side=side, ring=ring):
                    for panel in range(2):
                        put_q(side, 2, panel, self.q1[ring, rows_at(64 * panel + 16 * target(side, 1), 16), :])


T0 = (((0,), (0,)), ((), ()))
NT = (((1,), (1,)), ((), ()))


def mm(left, right):
    return jnp.dot(left, right, preferred_element_type=F32)


def mm_nt(left, right):
    return lax.dot_general(left, right, NT, preferred_element_type=F32)


def mm_t(left, right):
    return lax.dot_general(left, right, T0, preferred_element_type=F32)


def row_of(ref):
    return ref[...].reshape(1, -1)


def normal_cdf(pre):
    return 0.5 + 0.5 * lax.erf(pre * 0.7071067811865476), jnp.exp(-0.5 * pre * pre)


G0, D0 = 0, 4
X, Q, K, V, O, Y1, DZ, DA, DO = 8, 9, 10, 11, 12, 13, 14, 15, 16
N_ACTS = 17
ROWS = 512
LATE = 8


class Net:
    def __init__(self, **refs):
        self.__dict__.update(refs)

    def project_q(self, i):
        rows = pl.ds(pl.multiple_of(i * ROWS, ROWS), ROWS)
        out = mm(self.acts[X, rows, :], self.w_q[...]) + row_of(self.query_bias)
        self.acts[Q, rows, :] = out.astype(BF) * BF(0.125)

    def project_k(self, i):
        rows = pl.ds(pl.multiple_of(i * ROWS, ROWS), ROWS)
        self.acts[K, rows, :] = mm(self.acts[X, rows, :], self.w_k[...]).astype(BF)

    def project_v(self, i):
        rows = pl.ds(pl.multiple_of(i * ROWS, ROWS), ROWS)
        self.acts[V, rows, :] = (mm(self.acts[X, rows, :], self.w_v[...]) + row_of(self.value_bias)).astype(BF)

    def masks(self):
        place = lax.broadcasted_iota(jnp.int32, (8, 512), 1)
        for s in range(2):
            self.key_row[s] = jnp.where(place < self.lengths[s], 0.0, -1e9)

    def attend(self, i):
        s, pair = i // 6, lax.rem(i, 6)
        rows = pl.ds(pl.multiple_of(s * 512, 512), 512)
        lanes = lanes_at(pair * 128, 128)
        acts = self.acts
        k = acts[K, rows, lanes]
        v = acts[V, rows, lanes]
        lane = lax.broadcasted_iota(jnp.int32, (1, 128), 1)
        v_ones = jnp.concatenate([v, jnp.ones((512, 128), BF)], axis=1)
        q = acts[Q, rows, lanes]
        boths, tops = [], []
        for head in range(2):
            live = (lane >= 64) if head else (lane < 64)
            score = mm_nt(jnp.where(live, q, BF(0)), k) + self.key_row[s, 0:1, :]
            top = jnp.max(score, axis=1, keepdims=True)
            boths.append(mm(jnp.exp(score - top).astype(BF), v_ones))
            tops.append(top)
        pick = lane < 64
        mixed = jnp.where(pick, boths[0][:, :128], boths[1][:, :128])
        total = jnp.where(pick, boths[0][:, 128:], boths[1][:, 128:])
        acts[O, rows, lanes] = (mixed * pl.reciprocal(total, approx=False)).astype(BF)
        one, two = lane == 2 * pair, lane == 2 * pair + 1
        self.logs[s] = jnp.where(one, tops[0], jnp.where(two, tops[1], self.logs[s]))
        self.sums[s] = jnp.where(one, boths[0][:, 128:], jnp.where(two, boths[1][:, 128:], self.sums[s]))

    def normed(self, rows):
        mean = jnp.sum(rows, axis=1, keepdims=True) * (1.0 / 768)
        centred = rows - mean
        spread = jnp.sum(centred * centred, axis=1, keepdims=True) * (1.0 / 768)
        inverse = lax.rsqrt(spread + 1e-6)
        return centred * inverse, inverse

    def feed(self, i):
        rows = pl.ds(pl.multiple_of(i * ROWS, ROWS), ROWS)
        acts = self.acts
        h1 = acts[X, rows, :].astype(F32) + mm(acts[O, rows, :], self.w_m[...]) + row_of(self.mixer_bias)
        n1, r1 = self.normed(h1)
        self.n1[rows, :] = n1.astype(self.n1.dtype)
        self.r1[rows, :] = jnp.broadcast_to(r1, (ROWS, 128))
        y1 = n1 * row_of(self.first_gain) + row_of(self.first_shift)
        self.z[...] = y1 + row_of(self.shrink_bias)
        acts[Y1, rows, :] = y1.astype(BF)
        for j in range(4):
            self.feed_block(rows, j)
        n2, r2 = self.normed(self.z[...])
        self.n2[rows, :] = n2
        self.r2[rows, :] = jnp.broadcast_to(r2, (ROWS, 128))
        each = 512 // ROWS
        s, part = i // each, lax.rem(i, each)
        at = lax.broadcasted_iota(jnp.int32, (ROWS, 1), 0) + part * ROWS
        live = jnp.where(at < self.lengths[s], n2, 0.0)
        some = jnp.sum(live, axis=0, keepdims=True)
        self.n2_sum[s, 0:1, :] = jnp.where(part == 0, some, self.n2_sum[s, 0:1, :] + some)

    def feed_block(self, rows, j):
        acts = self.acts
        cols = pl.ds(768 * j, 768)
        pre = mm(acts[Y1, rows, :], self.w_e[:, cols]) + self.expand_bias[cols].reshape(1, 768)
        cdf, bell = normal_cdf(pre)
        low = (pre * cdf).astype(BF)
        acts[G0 + j, rows, :] = low
        acts[D0 + j, rows, :] = (cdf + pre * bell * 0.3989422804014327).astype(BF)
        self.z[...] += mm(low, self.w_s[cols, :])

    def pool(self, s):
        count = self.lengths[s].astype(F32)
        return self.n2_sum[s, 0:1, :] * row_of(self.second_gain) / count + row_of(self.second_shift)


class Back(Net):
    def share_vectors(self, place, k):
        mine = rows_at(8 * place.c, 8)
        z = place.z
        target = (place.sibling, place.to_x, place.to_y, place.me + 8 - 16 * (z % 2), place.me + 16 - 32 * (z // 2),
                  place.sibling)[k]
        source = self.vec.at[rows_at(8 * (1 - place.c), 8)] if k == 0 else self.vec.at[mine]
        landing = self.vec.at[mine] if k == 5 else self.vec_in.at[k]
        return pltpu.make_async_remote_copy(
            src_ref=source, dst_ref=landing, send_sem=self.vec_sent.at[k], recv_sem=self.vec_came.at[k],
            device_id=(target,), device_id_type=MESH)

    def sum_vectors(self, place, turn):
        mine = rows_at(8 * place.c, 8)
        for k in range(6):
            @pl.when(turn == 76 + 3 * k)
            def _(k=k):
                self.share_vectors(place, k).start()

            @pl.when(turn == 79 + 3 * k)
            def _(k=k):
                copy = self.share_vectors(place, k)
                copy.wait_send()
                copy.wait_recv()
                if k < 5:
                    self.vec[mine, :] += self.vec_in[k]

    def turn_logs(self):
        for s in range(2):
            self.logs_t[s] = jnp.transpose(self.logs[s] + jnp.log(self.sums[s]))[0:16, :]

    def gather(self, place):
        c, chip = place.c, place.me // 2
        every = self.every
        for s in range(2):
            u = self.pool(s)
            for j in range(6):
                every[c, chip, 8 * s + j:8 * s + j + 1, :] = u[:, 128 * j:128 * j + 128]
            every[c, chip, 8 * s + 6:8 * s + 8, :] = jnp.full((2, 128), self.targets[s], F32)

        def copy(source, device):
            return pltpu.make_async_remote_copy(
                src_ref=every.at[c, source], dst_ref=every.at[c, source], send_sem=self.told.at[device // 2],
                recv_sem=self.heard.at[source], device_id=(device,), device_id_type=MESH)

        order = (12, 4, 13, 11, 3, 5, 14, 10, 2, 6, 15, 9, 1, 7, 8)
        for k in order:
            copy(chip, lax.rem(chip + k, 16) * 2 + c).start()
        for k in order:
            copy(lax.rem(chip + 16 - k, 16), place.me).wait_recv()
        share = pltpu.make_async_remote_copy(
            src_ref=every.at[c], dst_ref=every.at[c], send_sem=self.told.at[chip],
            recv_sem=self.heard.at[chip], device_id=(place.sibling,), device_id_type=MESH)
        share.start()
        for k in order:
            copy(chip, lax.rem(chip + k, 16) * 2 + c).wait_send()
        share.wait_send()
        share.wait_recv()

    def pair(self, place, s):
        here = place.me * 2 + s
        wanted = jnp.full((8, 128), self.partners[here], jnp.int32)
        mine = self.every[place.c, place.me // 2, 8 * s:8 * s + 8, :]

        def pick(i, found):
            far, near = found
            device = i // 2
            tile = self.every[lax.rem(device, 2), device // 2, rows_at(8 * lax.rem(i, 2), 8), :]
            far += jnp.where(wanted == i, tile, 0.0)
            near += jnp.where(jnp.full((8, 128), self.partners[i], jnp.int32) == here, tile, 0.0)
            return far, near

        nothing = jnp.zeros((8, 128), F32)
        far, near = lax.fori_loop(0, 64, pick, (nothing, nothing), unroll=8)
        live = lax.broadcasted_iota(jnp.int32, (8, 128), 0) < 6

        def inner(left, right):
            return jnp.sum(jnp.where(live, left * right, 0.0), axis=(0, 1), keepdims=True)

        length = jnp.sqrt(inner(mine, mine) + 1e-6)
        far_length = jnp.sqrt(inner(far, far) + 1e-6)
        near_length = jnp.sqrt(inner(near, near) + 1e-6)
        score = inner(mine, far) / (length * far_length)
        near_score = inner(near, mine) / (near_length * length)
        miss = score - mine[6:7, 0:1]
        near_miss = near_score - near[6:7, 0:1]
        own = mine / (length * length)
        grad = miss * (far / (length * far_length) - score * own)
        grad += near_miss * (near / (near_length * length) - near_score * own)
        for j in range(6):
            self.du[s, 0:1, 128 * j:128 * j + 128] = grad[j:j + 1, :]
        self.scores[s:s + 1, :] = jnp.broadcast_to(score, (1, 128))

    def clear(self):
        self.vec[...] = jnp.zeros_like(self.vec)
        self.logs[...] = jnp.zeros_like(self.logs)
        self.sums[...] = jnp.ones_like(self.sums)

    def add_vec(self, at, rows):
        self.vec[at:at + 1, :] += jnp.sum(rows.astype(F32), axis=0, keepdims=True)

    def second_vectors(self):
        gain = jnp.zeros((1, 768), F32)
        for s in range(2):
            gain += self.du[s, 0:1, :] * self.n2_sum[s, 0:1, :] / self.lengths[s].astype(F32)
        self.vec[6:7, :] = gain
        self.vec[7:8, :] = self.du[0, 0:1, :] + self.du[1, 0:1, :]

    def back_second(self, i):
        rows = pl.ds(pl.multiple_of(i * 256, 256), 256)
        s = i // 2
        up = self.du[s, 0:1, :] * row_of(self.second_gain) / self.lengths[s].astype(F32)
        mean = jnp.sum(up, axis=1, keepdims=True) * (1.0 / 768)
        n2 = self.n2[rows, :]
        along = jnp.sum(n2 * up, axis=1, keepdims=True) * (1.0 / 768)
        at = lax.broadcasted_iota(jnp.int32, (256, 1), 0) + lax.rem(i, 2) * 256
        dh2 = jnp.where(at < self.lengths[s], self.r2[rows, 0:1] * (up - mean - n2 * along), 0.0)
        self.n2[rows, :] = dh2
        dz = dh2.astype(BF)
        self.acts[DZ, rows, :] = dz
        self.add_vec(5, dz)

    def back_hidden(self, i):
        j, half = i // 2, lax.rem(i, 2)
        rows = pl.ds(pl.multiple_of(half * 512, 512), 512)
        units = pl.ds(pl.multiple_of(j * 768, 768), 768)
        df = (mm_nt(self.acts[DZ, rows, :], self.w_s[units, :]) * self.acts[D0 + j, rows, :].astype(F32)).astype(BF)
        self.acts[D0 + j, rows, :] = df
        part = jnp.sum(df.astype(F32), axis=0, keepdims=True)
        line = lax.broadcasted_iota(jnp.int32, (8, 768), 0) == j
        self.vec[8:16, :] += jnp.where(line, part, 0.0)

    def back_first(self, i):
        rows = pl.ds(pl.multiple_of(i * 256, 256), 256)
        acts = self.acts
        up = self.n2[rows, :]
        for j in range(4):
            up += mm_nt(acts[D0 + j, rows, :], self.w_e[:, 768 * j:768 * j + 768])
        n1 = self.n1[rows, :].astype(F32)
        self.add_vec(3, up * n1)
        self.add_vec(4, up)
        dn = up * row_of(self.first_gain)
        mean = jnp.sum(dn, axis=1, keepdims=True) * (1.0 / 768)
        along = jnp.sum(dn * n1, axis=1, keepdims=True) * (1.0 / 768)
        dh1 = self.r1[rows, 0:1] * (dn - mean - n1 * along)
        self.n2[rows, :] = dh1
        da = dh1.astype(BF)
        acts[DA, rows, :] = da
        self.add_vec(2, da)
        acts[DO, rows, :] = mm_nt(da, self.w_m[...]).astype(BF)

    def attend_back(self, i):
        s, head = i // 12, lax.rem(i, 12)
        rows = pl.ds(pl.multiple_of(s * 512, 512), 512)
        lanes = lanes_at((head // 2) * 128, 128)
        acts = self.acts
        lane = lax.broadcasted_iota(jnp.int32, (1, 128), 1)
        live = (lane // 64) == lax.rem(head, 2)
        q_all, k, v = acts[Q, rows, lanes], acts[K, rows, lanes], acts[V, rows, lanes]
        q = jnp.where(live, q_all, BF(0))
        up = jnp.where(live, acts[DO, rows, lanes], BF(0))
        place = lax.broadcasted_iota(jnp.int32, (512, 1), 0)
        off = jnp.where(place < self.lengths[s], 0.0, -1e9)
        probs = jnp.exp(mm_nt(k, q) + off - self.logs_t[s, pl.ds(head, 1), :])
        weighed = probs * mm_nt(v, up)
        delta = jnp.sum(weighed, axis=0, keepdims=True)
        ds = (weighed - probs * delta).astype(BF)
        dv = mm(probs.astype(BF), up)
        dk = mm(ds, q)
        dq = mm_t(ds, k) * 0.125
        acts[Q, rows, lanes] = jnp.where(live, dq.astype(BF), q_all)
        acts[K, rows, lanes] = jnp.where(live, dk.astype(BF), k)
        acts[V, rows, lanes] = jnp.where(live, dv.astype(BF), v)

    def back_tokens(self, i):
        rows = pl.ds(pl.multiple_of(i * 256, 256), 256)
        dq, dk, dv = self.acts[Q, rows, :], self.acts[K, rows, :], self.acts[V, rows, :]
        self.add_vec(0, dq)
        self.add_vec(1, dv)
        self.n2[rows, :] += mm_nt(dq, self.w_q[...]) + mm_nt(dk, self.w_k[...]) + mm_nt(dv, self.w_v[...])

    def back_task(self, i):
        pl.when(i < 8)(lambda: self.back_hidden(i))
        pl.when((i >= 8) & (i < 12))(lambda: self.back_first(i - 8))
        pl.when((i >= 12) & (i < 36))(lambda: self.attend_back(i - 12))
        pl.when((i >= 36) & (i < 40))(lambda: self.back_tokens(i - 36))

    def grad_piece(self, i):
        b = i // 3
        slot = lax.rem(i, 2)
        cols = pl.ds(pl.multiple_of(lax.rem(i, 3) * 256, 256), 256)
        left = jnp.where(b < 4, G0 + b, jnp.where(b < 8, Y1, jnp.where(b < 9, O, X)))
        right = jnp.where(b < 4, DZ, jnp.where(b < 8, D0 + b - 4, jnp.where(b < 9, DA, b)))
        self.ring[slot] = mm_t(self.acts[left, :, cols], self.acts[right])


N_IN = 19
VMEM_LIMIT = 54 << 20
VECTORS = ("query_bias", "value_bias", "mixer_bias", "first_gain", "first_shift", "shrink_bias", "second_gain",
           "second_shift")


def layer_kernel(*refs):
    (tokens, lengths, partners, targets, w_q, query_bias, w_k, w_v, value_bias, w_m, mixer_bias, first_gain,
     first_shift, w_e, expand_bias, w_s, shrink_bias, second_gain, second_shift) = refs[:N_IN]
    scores, late, vec, summed = refs[N_IN:N_IN + 4]
    rest = refs[N_IN + 4:]
    (acts, v_q, v_k, v_v, v_m, v_e, v_s, key_row, logs, sums, logs_t, r1, r2, n2_sum, every, du, vec_in, ring,
     loaded, told, heard, vec_sent, vec_came) = rest[:23]
    n2, n1, z = late.at[pl.ds(0, 1024)], late.at[pl.ds(1024, 1024)], late.at[pl.ds(2048, ROWS)]
    first, second = rest[23:23 + N_STREAM_SCRATCH], rest[23 + N_STREAM_SCRATCH:]
    place = Place()
    net = Back(
        acts=acts, w_q=v_q, w_k=v_k, w_v=v_v, w_m=v_m, w_e=v_e, w_s=v_s, query_bias=query_bias, value_bias=value_bias,
        mixer_bias=mixer_bias, first_gain=first_gain, first_shift=first_shift, expand_bias=expand_bias,
        shrink_bias=shrink_bias, second_gain=second_gain, second_shift=second_shift, lengths=lengths,
        partners=partners, targets=targets, scores=scores, key_row=key_row, logs=logs, sums=sums,
        logs_t=logs_t, n1=n1, r1=r1, n2=n2, r2=r2, z=z, n2_sum=n2_sum, every=every, du=du, vec=vec, ring=ring,
        told=told, heard=heard, vec_in=vec_in, vec_sent=vec_sent, vec_came=vec_came)
    loads = [pltpu.make_async_copy(src, dst, loaded.at[i]) for i, (src, dst) in enumerate([
        (tokens, acts.at[X]), (w_q, v_q), (w_k, v_k), (w_v, v_v), (w_m, v_m), (w_e, v_e), (w_s, v_s)])]
    for copy in loads[:4]:
        copy.start()

    def chunk_rows(t, shift):
        t = jnp.clip(t, 0, 36)
        return lax.rem(t, 2), shift

    def outs(m, shift):
        early = rows_at(jnp.clip(m, 0, 35 - LATE) * 256 + shift, 64)
        last = rows_at(1024 + (jnp.clip(m, 36 - LATE, 35) - (36 - LATE)) * 256 + shift, 64)
        return [(summed.at[early], m < 36 - LATE), (late.at[last], m >= 36 - LATE)]

    one = Stream(place, 0, 36, first, ring, lambda t: chunk_rows(t, 0), outs)
    two = Stream(place, 1, 36, second, ring, lambda t: chunk_rows(t, 128), lambda m, at: outs(m, 128 + at))
    one.prepare()
    two.prepare()
    greet_all(place)

    def each(count, task):
        def step(i, carry):
            task(i)
            return carry

        lax.fori_loop(0, count, step, 0)

    net.masks()
    net.clear()
    loads[0].wait()
    loads[1].wait()
    each(1024 // ROWS, net.project_q)
    loads[2].wait()
    loads[3].wait()
    for copy in loads[4:]:
        copy.start()
    each(1024 // ROWS, net.project_k)
    each(1024 // ROWS, net.project_v)
    each(12, net.attend)
    net.turn_logs()
    for copy in loads[4:]:
        copy.wait()
    each(1024 // ROWS, net.feed)
    await_all()
    net.gather(place)
    for s in range(2):
        net.pair(place, s)
    net.second_vectors()
    each(4, net.back_second)

    first_task = 12

    def step(turn, carry):
        t = turn // 2 - 1
        side = lax.rem(turn, 2)

        for i, stream in enumerate((one, two)):
            @pl.when((side == i) & (t >= 0))
            def _(stream=stream):
                stream.wait(t - 1)
                stream.work(t)
                stream.start(t)

        pl.when((side == 1) & (t + 1 < 36))(lambda: net.grad_piece(t + 1))
        task = turn - 2 - first_task
        pl.when((task >= 0) & (task < 40))(lambda: net.back_task(task))
        net.sum_vectors(place, turn)
        return carry

    lax.fori_loop(1, 2 * 48 + 2, step, 0)


def greet_all(place):
    bar = pltpu.get_barrier_semaphore()
    chip = place.me // 2

    def hail(k, carry):
        pl.semaphore_signal(bar, 1, device_id=(lax.rem(chip + k, 16) * 2 + place.c,), device_id_type=MESH)
        return carry

    pl.semaphore_signal(bar, 1, device_id=(place.sibling,), device_id_type=MESH)
    lax.fori_loop(1, 16, hail, 0)


def await_all():
    pl.semaphore_wait(pltpu.get_barrier_semaphore(), 16)


def whole_layer(*args):
    anywhere = pl.BlockSpec(memory_space=pltpu.HBM)
    vector = pl.BlockSpec(memory_space=pltpu.VMEM)
    scalars = pl.BlockSpec(memory_space=pltpu.SMEM)
    specs = [anywhere if a.dtype == BF else vector if a.shape[0] >= 768 else scalars for a in args]

    def low(*shape):
        return pltpu.VMEM(shape, BF)

    def full(*shape):
        return pltpu.VMEM(shape, F32)

    return pl.pallas_call(
        layer_kernel,
        out_shape=(
            pltpu.VMEM((8, 128), F32),
            pltpu.VMEM((1024 + max(1024 + ROWS, 256 * LATE), 768), F32),
            pltpu.VMEM((16, 768), F32),
            jax.ShapeDtypeStruct((256 * (36 - LATE), 768), F32),
        ),
        in_specs=specs,
        out_specs=(vector, vector, vector, pl.BlockSpec(memory_space=pltpu.HBM)),
        scratch_shapes=[
            low(N_ACTS, 1024, 768),
            low(768, 768), low(768, 768), low(768, 768), low(768, 768), low(768, 3072), low(3072, 768),
            full(2, 8, 512), full(2, 512, 128), full(2, 512, 128), full(2, 16, 512),
            full(1024, 128), full(1024, 128), full(2, 8, 768),
            full(2, 16, 16, 128), full(2, 8, 768), full(5, 8, 768), full(2, 256, 768),
            pltpu.SemaphoreType.DMA((7,)), pltpu.SemaphoreType.DMA((16,)), pltpu.SemaphoreType.DMA((16,)),
            pltpu.SemaphoreType.DMA((6,)), pltpu.SemaphoreType.DMA((6,)),
        ] + stream_scratch() + stream_scratch(),
        compiler_params=pltpu.CompilerParams(
            collective_id=0, has_side_effects=True, vmem_limit_bytes=VMEM_LIMIT),
    )(*args)


def deliver_kernel(count, height, summed, late, small, scores, *refs):
    (scores_out, tokens_out, w_q, query_bias, w_k, w_v, value_bias, w_m, mixer_bias, first_gain, first_shift, w_e,
     expand_bias, w_s, shrink_bias, second_gain, second_shift) = refs[:17]
    buffer, came, left, sent = refs[17:]

    def place(row, size):
        block, at = row // 768, row % 768
        if block < 4:
            return w_s.at[pl.ds(row, size)]
        if block < 8:
            return w_e.at[pl.ds(at, size), pl.ds(768 * (block - 4), 768)]
        return (w_m, w_q, w_k, w_v)[block - 8].at[pl.ds(at, size)]

    early = summed.shape[0]
    direct = [pltpu.make_async_copy(late.at[pl.ds(0, 1024)], tokens_out, sent.at[0])]
    row = early
    while row < 9216:
        size = min(768 - row % 768, 9216 - row)
        direct.append(pltpu.make_async_copy(
            late.at[pl.ds(1024 + row - early, size)], place(row, size), sent.at[len(direct)]))
        row += size
    jobs = []
    row = 0
    while row < early:
        size = min(height, 768 - row % 768, early - row)
        jobs.append((row, size))
        row += size

    def copies(i):
        row, size = jobs[i]
        spot = buffer.at[i % count, pl.ds(0, size)]
        return (pltpu.make_async_copy(summed.at[pl.ds(row, size)], spot, came.at[i % count]),
                pltpu.make_async_copy(spot, place(row, size), left.at[i % count]))

    total = len(jobs)
    ahead = count // 2
    for i in range(min(ahead, total)):
        copies(i)[0].start()
    for copy in direct:
        copy.start()
    for j, ref in enumerate((query_bias, value_bias, mixer_bias, first_gain, first_shift, shrink_bias,
                             second_gain, second_shift)):
        ref[...] = small[j, :]
    for j in range(4):
        expand_bias[768 * j:768 * j + 768] = small[8 + j, :]
    for s in range(2):
        scores_out[s] = jnp.sum(scores[s:s + 1, 0:1])
    for i in range(total):
        copies(i)[0].wait()
        copies(i)[1].start()
        later = i + ahead
        if later < total:
            if later >= count:
                copies(later - count)[1].wait()
            copies(later)[0].start()
    for i in range(max(0, total - count), total):
        copies(i)[1].wait()
    for copy in direct:
        copy.wait()


def fused(*args):
    pair_scores, late, small, summed = whole_layer(*args)
    hbm = pl.BlockSpec(memory_space=pltpu.HBM)
    vector = pl.BlockSpec(memory_space=pltpu.VMEM)
    scalars = pl.BlockSpec(memory_space=pltpu.SMEM)
    shapes = [(2,), (1024, 768), (768, 768), (768,), (768, 768), (768, 768), (768,), (768, 768), (768,), (768,), (768,),
              (768, 3072), (3072,), (3072, 768), (768,), (768,), (768,)]
    count, height = 14, 384
    return tuple(pl.pallas_call(
        partial(deliver_kernel, count, height),
        out_shape=[jax.ShapeDtypeStruct(shape, F32) for shape in shapes],
        in_specs=[hbm, vector, vector, vector],
        out_specs=[hbm if len(shape) == 2 else vector if shape[0] > 2 else scalars for shape in shapes],
        scratch_shapes=[pltpu.VMEM((count, height, 768), F32),
                        pltpu.SemaphoreType.DMA((count,)), pltpu.SemaphoreType.DMA((count,)),
                        pltpu.SemaphoreType.DMA((16,))],
        compiler_params=pltpu.CompilerParams(vmem_limit_bytes=36 << 20),
    )(summed, late, small, pair_scores))


def to_low(value):
    return value.astype(jnp.bfloat16)


def tdot(left, right):
    return lax.dot_general(
        left, right, (((0,), (0,)), ((), ())), preferred_element_type=jnp.float32
    )


def ndot(left, right):
    return lax.dot_general(
        left, right, (((1,), (1,)), ((), ())), preferred_element_type=jnp.float32
    )


def norm_rows(rows, gain, shift):
    mean = jnp.mean(rows, axis=-1, keepdims=True)
    centred = rows - mean
    spread = jnp.mean(centred * centred, axis=-1, keepdims=True)
    inverse = lax.rsqrt(spread + 1e-06)
    normed = centred * inverse
    return (normed * gain + shift, normed, inverse)


def norm_back(upstream, normed, inverse, gain):
    gain_grad = jnp.sum(upstream * normed, axis=0)
    shift_grad = jnp.sum(upstream, axis=0)
    dnormed = upstream * gain
    first_mean = jnp.mean(dnormed, axis=-1, keepdims=True)
    second_mean = jnp.mean(dnormed * normed, axis=-1, keepdims=True)
    return (inverse * (dnormed - first_mean - normed * second_mean), gain_grad, shift_grad)


def per_device(
    tokens,
    lengths,
    partners,
    targets,
    query_proj,
    query_bias,
    key_proj,
    value_proj,
    value_bias,
    mixer_proj,
    mixer_bias,
    first_gain,
    first_shift,
    expand_proj,
    expand_bias,
    shrink_proj,
    shrink_bias,
    second_gain,
    second_shift,
):
    sents = lengths.shape[0]
    rows_all = tokens.shape[0]
    slot = rows_all // sents
    width = tokens.shape[1]
    heads = H
    depth = width // heads
    scale = 1.0 / math.sqrt(depth)
    total = partners.shape[0]
    base = lax.axis_index("dp") * sents
    highest = lax.Precision.HIGHEST
    places = jnp.arange(slot, dtype=jnp.int32)
    valid = places[None, :] < lengths[:, None]
    row_mask = valid.reshape(rows_all, 1).astype(jnp.float32)
    shape4 = (sents, slot, heads, depth)
    queries = to_low(jnp.dot(tokens, query_proj, preferred_element_type=jnp.float32) + query_bias)
    keys = to_low(jnp.dot(tokens, key_proj, preferred_element_type=jnp.float32))
    values = to_low(jnp.dot(tokens, value_proj, preferred_element_type=jnp.float32) + value_bias)
    queries4 = queries.reshape(shape4)
    keys4 = keys.reshape(shape4)
    values4 = values.reshape(shape4)

    def masked_scores(query_rows, key_rows, live):
        raw = (
            jnp.einsum("qhd,khd->hqk", query_rows, key_rows, preferred_element_type=jnp.float32)
            * scale
        )
        return jnp.where(live[None, None, :], raw, -1000000000.0)

    def attend(item):
        query_rows, key_rows, value_rows, live = item
        raw = masked_scores(query_rows, key_rows, live)
        top = jnp.max(raw, axis=-1, keepdims=True)
        expd = jnp.exp(raw - top)
        summed = jnp.sum(expd, axis=-1, keepdims=True)
        probs = to_low(expd / summed)
        mixed = jnp.einsum("hqk,khd->qhd", probs, value_rows, preferred_element_type=jnp.float32)
        return (mixed, (top + jnp.log(summed))[..., 0])

    mixed, logsum = lax.map(attend, (queries4, keys4, values4, valid))
    mixed_low = to_low(mixed.reshape(rows_all, width))
    branch = jnp.dot(mixed_low, mixer_proj, preferred_element_type=jnp.float32) + mixer_bias
    first_out, first_normed, first_inverse = norm_rows(
        tokens.astype(jnp.float32) + branch, first_gain, first_shift
    )
    first_low = to_low(first_out)
    pre = jnp.dot(first_low, expand_proj, preferred_element_type=jnp.float32) + expand_bias
    act, gelu_back = jax.vjp(partial(jax.nn.gelu, approximate=False), pre)
    act_low = to_low(act)
    shrink = jnp.dot(act_low, shrink_proj, preferred_element_type=jnp.float32) + shrink_bias
    outputs, second_normed, second_inverse = norm_rows(
        first_out + shrink, second_gain, second_shift
    )
    counts = lengths.astype(jnp.float32)
    pooled = jnp.sum((outputs * row_mask).reshape(sents, slot, width), axis=1) / counts[:, None]
    mine = lax.dynamic_slice_in_dim(partners, base, sents)
    every = lax.all_gather(pooled, "dp", axis=0, tiled=True)
    partner_vec = jnp.take(every, mine, axis=0)
    inner = jnp.sum(pooled * partner_vec, axis=-1)
    own_len = jnp.sqrt(jnp.sum(pooled * pooled, axis=-1) + 1e-06)
    far_len = jnp.sqrt(jnp.sum(partner_vec * partner_vec, axis=-1) + 1e-06)
    pair_scores = inner / (own_len * far_len)
    miss = pair_scores - targets
    joint = (own_len * far_len)[:, None]
    dpooled = miss[:, None] * (
        partner_vec / joint - (pair_scores / (own_len * own_len))[:, None] * pooled
    )
    dpartner = miss[:, None] * (
        pooled / joint - (pair_scores / (far_len * far_len))[:, None] * partner_vec
    )
    owners = (mine[:, None] == jnp.arange(total, dtype=jnp.int32)[None, :]).astype(jnp.float32)
    spread = lax.dot_general(owners, dpartner, (((0,), (0,)), ((), ())), precision=highest)
    returned = lax.psum_scatter(spread, "dp", scatter_dimension=0, tiled=True)
    dpool_all = (dpooled + returned) / counts[:, None]
    doutputs = (dpool_all[:, None, :] * valid[:, :, None].astype(jnp.float32)).reshape(
        rows_all, width
    )
    dsecond, second_gain_grad, second_shift_grad = norm_back(
        doutputs, second_normed, second_inverse, second_gain
    )
    dshrink = to_low(dsecond)
    shrink_proj_grad = tdot(act_low, dshrink)
    shrink_bias_grad = jnp.sum(dshrink.astype(jnp.float32), axis=0)
    dact = ndot(dshrink, shrink_proj)
    dpre = to_low(gelu_back(dact)[0])
    expand_proj_grad = tdot(first_low, dpre)
    expand_bias_grad = jnp.sum(dpre.astype(jnp.float32), axis=0)
    dfirst_out = ndot(dpre, expand_proj) + dsecond
    dfirst, first_gain_grad, first_shift_grad = norm_back(
        dfirst_out, first_normed, first_inverse, first_gain
    )
    dbranch = to_low(dfirst)
    mixer_proj_grad = tdot(mixed_low, dbranch)
    mixer_bias_grad = jnp.sum(dbranch.astype(jnp.float32), axis=0)
    dmixed = to_low(ndot(dbranch, mixer_proj)).reshape(shape4)

    def attend_back(item):
        query_rows, key_rows, value_rows, live, row_logsum, dmix = item
        raw = masked_scores(query_rows, key_rows, live)
        probs = jnp.exp(raw - row_logsum[..., None])
        probs_low = to_low(probs)
        dprob = jnp.einsum("qhd,khd->hqk", dmix, value_rows, preferred_element_type=jnp.float32)
        delta = jnp.sum(dprob * probs, axis=-1, keepdims=True)
        dscore = to_low(probs * (dprob - delta))
        dquery = (
            jnp.einsum("hqk,khd->qhd", dscore, key_rows, preferred_element_type=jnp.float32) * scale
        )
        dkey = (
            jnp.einsum("hqk,qhd->khd", dscore, query_rows, preferred_element_type=jnp.float32)
            * scale
        )
        dvalue = jnp.einsum("hqk,qhd->khd", probs_low, dmix, preferred_element_type=jnp.float32)
        return (to_low(dquery), to_low(dkey), to_low(dvalue))

    dquery, dkey, dvalue = lax.map(attend_back, (queries4, keys4, values4, valid, logsum, dmixed))
    dquery = dquery.reshape(rows_all, width)
    dkey = dkey.reshape(rows_all, width)
    dvalue = dvalue.reshape(rows_all, width)
    query_proj_grad = tdot(tokens, dquery)
    query_bias_grad = jnp.sum(dquery.astype(jnp.float32), axis=0)
    key_proj_grad = tdot(tokens, dkey)
    value_proj_grad = tdot(tokens, dvalue)
    value_bias_grad = jnp.sum(dvalue.astype(jnp.float32), axis=0)
    tokens_grad = (
        ndot(dquery, query_proj) + ndot(dkey, key_proj) + ndot(dvalue, value_proj) + dfirst
    )
    (
        query_proj_grad,
        query_bias_grad,
        key_proj_grad,
        value_proj_grad,
        value_bias_grad,
        mixer_proj_grad,
        mixer_bias_grad,
        first_gain_grad,
        first_shift_grad,
        expand_proj_grad,
        expand_bias_grad,
        shrink_proj_grad,
        shrink_bias_grad,
        second_gain_grad,
        second_shift_grad,
    ) = lax.psum(
        (
            query_proj_grad,
            query_bias_grad,
            key_proj_grad,
            value_proj_grad,
            value_bias_grad,
            mixer_proj_grad,
            mixer_bias_grad,
            first_gain_grad,
            first_shift_grad,
            expand_proj_grad,
            expand_bias_grad,
            shrink_proj_grad,
            shrink_bias_grad,
            second_gain_grad,
            second_shift_grad,
        ),
        "dp",
    )
    return (
        pair_scores,
        tokens_grad,
        query_proj_grad,
        query_bias_grad,
        key_proj_grad,
        value_proj_grad,
        value_bias_grad,
        mixer_proj_grad,
        mixer_bias_grad,
        first_gain_grad,
        first_shift_grad,
        expand_proj_grad,
        expand_bias_grad,
        shrink_proj_grad,
        shrink_bias_grad,
        second_gain_grad,
        second_shift_grad,
    )


def solution(mesh):
    in_specs = (
        P("dp", None),
        P("dp"),
        P(),
        P("dp"),
        P(),
        P(),
        P(),
        P(),
        P(),
        P(),
        P(),
        P(),
        P(),
        P(),
        P(),
        P(),
        P(),
        P(),
        P(),
    )
    out_specs = (
        P("dp"),
        P("dp", None),
        P(),
        P(),
        P(),
        P(),
        P(),
        P(),
        P(),
        P(),
        P(),
        P(),
        P(),
        P(),
        P(),
        P(),
        P(),
    )
    plain = mesh.shape["dp"] != 32
    return jax.shard_map(
        per_device if plain else fused, mesh=mesh, in_specs=in_specs, out_specs=out_specs, check_vma=False
    )
```

```python
from functools import partial
import math

import jax
import jax.numpy as jnp
from jax import lax
from jax.sharding import PartitionSpec as P

from jax.experimental import pallas as pl
from jax.experimental.pallas import tpu as pltpu

H = 12

MESH = pl.DeviceIdType.MESH
F32 = jnp.float32
BF = jnp.bfloat16


def rows16(index):
    return pl.ds(pl.multiple_of(index * 16, 16), 16)


def rows_at(start, size):
    return pl.ds(pl.multiple_of(start, 8), size)


def lanes_at(start, size):
    return pl.ds(pl.multiple_of(start, 128), size)


class Place:
    def __init__(self):
        me = lax.axis_index("dp")
        self.me = me
        self.c = me % 2
        self.x = (me // 2) % 2
        self.y = (me // 4) % 2
        self.z = me // 8
        self.sibling = me + 1 - 2 * self.c
        self.to_x = me + 2 - 4 * self.x
        self.to_y = me + 4 - 8 * self.y
        self.up = me + 8
        self.down = me - 8


def stream_scratch():
    return [
        pltpu.VMEM((2, 64, 768), F32),
        pltpu.VMEM((144, 128), F32),
        pltpu.VMEM((2, 144, 128), F32),
        pltpu.VMEM((144, 128), F32),
        pltpu.VMEM((2, 144, 128), F32),
        pltpu.VMEM((80, 128), F32),
        pltpu.VMEM((2, 80, 128), F32),
        pltpu.VMEM((64, 128), F32),
        pltpu.VMEM((2, 64, 128), F32),
        pltpu.VMEM((2, 192, 128), F32),
        pltpu.VMEM((2, 2, 192, 128), F32),
        pltpu.VMEM((128, 128), F32),
        pltpu.VMEM((64, 128), F32),
        pltpu.VMEM((4, 64, 128), F32),
        pltpu.VMEM((4, 128, 128), F32),
        pltpu.VMEM((16, 128), F32),
        pltpu.VMEM((16, 128), F32),
        pltpu.VMEM((8, 64, 768), F32),
        pltpu.SemaphoreType.DMA((10, 2)),
        pltpu.SemaphoreType.DMA((10, 2)),
        pltpu.SemaphoreType.DMA((2,)),
    ]


N_STREAM_SCRATCH = 21


class Stream:
    def __init__(self, place, which, count, refs, grad_ref, grad_rows, outs):
        (self.sib_in, self.a_rs_out, self.a_rs_in, self.a_ag_out, self.a_ag_in, self.b_rs_out, self.b_rs_in,
         self.b_ag_out, self.b_ag_in, self.z_out, self.z_in, self.p1, self.p2, self.p3, self.q1, self.q2, self.q3,
         self.full, self.sent, self.came, self.kept) = refs
        self.place = place
        self.count = count
        self.grad_ref = grad_ref
        self.grad_rows = grad_rows
        self.outs = outs
        if which == 0:
            self.d1, self.d2, self.to_a, self.to_b = place.x, place.y, place.to_x, place.to_y
        else:
            self.d1, self.d2, self.to_a, self.to_b = place.y, place.x, place.to_y, place.to_x

    def prepare(self):
        zero = jnp.zeros((192, 128), F32)
        for side in range(2):
            for parity in range(2):
                self.z_in[side, parity] = zero

    def copies(self, t):
        place, n = self.place, self.count
        par = t % 2

        def remote(i, src, dst, target):
            return pltpu.make_async_remote_copy(
                src_ref=src, dst_ref=dst, send_sem=self.sent.at[i, par], recv_sem=self.came.at[i, par],
                device_id=(target,), device_id_type=MESH)

        def tail(i, src, dst, at, size, target):
            return remote(i, src.at[pl.ds(at, size)], dst.at[par, pl.ds(at, size)], target)

        slot, row = self.grad_rows(t)
        other = rows_at(row + 64 * (1 - place.c), 64)
        m = t - 10
        ring = lax.rem(t + 6, 8)
        outs = self.outs(m, 64 * place.c)
        lead = (place.z, 3 - place.z)
        zs = []
        for side, device in ((0, place.up), (1, place.down)):
            for half, when in ((0, (t >= 1) & (t < n + 6)), (1, (t >= 7) & (t < n + 9))):
                for k in range(3):
                    at, size = (0, 160 - 32 * k) if half == 0 else (160 - 32 * k, 32 + 32 * k)
                    spot = pl.ds(at, size)
                    copy = remote(5 + 2 * side + half, self.z_out.at[side, spot], self.z_in.at[side, par, spot], device)
                    zs.append((copy, when, lead[side] == k, lead[side] == k + 1))
        return [
            (remote(0, self.grad_ref.at[slot, other], self.sib_in.at[par], place.sibling), (t >= 0) & (t < n), True, True),
            (remote(1, self.a_rs_out, self.a_rs_in.at[par], self.to_a), (t >= 1) & (t < n + 1), True, True),
            (tail(1, self.a_rs_out, self.a_rs_in, 128, 16, self.to_a), (t >= n + 1) & (t < n + 4), True, True),
            (remote(2, self.a_ag_out, self.a_ag_in.at[par], self.to_a), (t >= 6) & (t < n + 7), True, True),
            (remote(3, self.b_rs_out, self.b_rs_in.at[par], self.to_b), (t >= 2) & (t < n + 2), True, True),
            (tail(3, self.b_rs_out, self.b_rs_in, 64, 16, self.to_b), (t >= n + 2) & (t < n + 5), True, True),
            (remote(4, self.b_ag_out, self.b_ag_in.at[par], self.to_b), (t >= 6) & (t < n + 6), True, True),
        ] + zs + [
            (remote(9, self.full.at[ring], spot, place.sibling), (t >= 10) & (t < n + 10) & when, True, True)
            for spot, when in outs
        ], [(pltpu.make_async_copy(self.full.at[ring], spot, self.kept.at[par]), (t >= 10) & (t < n + 10) & when)
            for spot, when in outs]

    def start(self, t):
        remote, local = self.copies(t)
        for copy, when, sends, _ in remote:
            pl.when(when if sends is True else when & sends)(copy.start)
        for copy, when in local:
            pl.when(when)(copy.start)

    def wait(self, t):
        remote, local = self.copies(t)
        for copy, when, sends, takes in remote:
            if sends is True:
                @pl.when(when)
                def _(copy=copy):
                    copy.wait_send()
                    copy.wait_recv()
            else:
                pl.when(when & sends)(copy.wait_send)
                pl.when(when & takes)(copy.wait_recv)
        for copy, when in local:
            pl.when(when)(copy.wait)

    def work(self, t):
        place = self.place
        z, d1, d2 = place.z, self.d1, self.d2
        par = (t + 1) % 2
        z_in, z_out = self.z_in, self.z_out
        lead = (z, 3 - z)

        def far(side, k):
            return z - k if side == 0 else z + k

        def target(side, step):
            return z + 4 - step if side == 0 else z - 4 + step

        def ring4(stage):
            return lax.rem(t + 16 - stage, 4)

        def ring8(stage):
            return lax.rem(t + 16 - stage, 8)

        def got_p(side):
            return z_in[side, par, 0:64, :]

        def got_q(side, pos, panel):
            at = 64 + 32 * pos + 16 * panel
            return z_in[side, par, at:at + 16, :]

        def put_p(side, value):
            z_out[side, 0:64, :] = value

        def put_q(side, pos, panel, value):
            at = 64 + 32 * pos + 16 * panel
            z_out[side, at:at + 16, :] = value

        def full_p(ring, value):
            self.full[ring, :, lanes_at((2 * d1 + d2) * 128, 128)] = value

        def full_q(ring, block, panel, value):
            self.full[ring, rows16(block), 512 + 128 * panel:640 + 128 * panel] = value

        def live(stage):
            return (t >= stage) & (t < self.count + stage)

        @pl.when(live(10))
        def _stage10():
            ring = ring8(10)
            for side in range(2):
                @pl.when(lead[side] == 3)
                def _(side=side):
                    for panel in range(2):
                        full_q(ring, far(side, 3), panel, got_q(side, 1, panel))

        @pl.when(live(9))
        def _stage9():
            ring = ring8(9)
            for side in range(2):
                @pl.when(lead[side] >= 2)
                def _(side=side):
                    for panel in range(2):
                        value = got_q(side, 2, panel)
                        full_q(ring, far(side, 2), panel, value)
                        put_q(side, 1, panel, value)

        @pl.when(live(8))
        def _stage8():
            ring = ring8(8)
            self.full[ring, :, lanes_at((1 - d1) * 256, 128)] = self.a_ag_in[par, 0:64, :]
            self.full[ring, :, lanes_at((1 - d1) * 256 + 128, 128)] = self.a_ag_in[par, 64:128, :]
            for side in range(2):
                @pl.when(lead[side] >= 1)
                def _(side=side):
                    for panel in range(2):
                        value = got_q(side, 3, panel)
                        full_q(ring, far(side, 1), panel, value)
                        put_q(side, 2, panel, value)

        @pl.when(live(7))
        def _stage7():
            ring = ring8(7)
            other = self.b_ag_in[par]
            self.full[ring, :, lanes_at((2 * d1 + 1 - d2) * 128, 128)] = other
            self.a_ag_out[rows_at(64 * (1 - d2), 64), :] = other
            self.a_ag_out[rows_at(64 * d2, 64), :] = self.full[ring, :, lanes_at((2 * d1 + d2) * 128, 128)]
            self.full[ring, rows16(z), lanes_at(512 + 128 * (1 - d1), 128)] = self.a_ag_in[par, 128:144, :]
            for panel in range(2):
                value = self.full[ring, rows16(z), 512 + 128 * panel:640 + 128 * panel]
                for side in range(2):
                    put_q(side, 3, panel, value)

        @pl.when(live(6))
        def _stage6():
            ring = ring8(6)
            for side in range(2):
                @pl.when(lead[side] == 3)
                def _(side=side):
                    full_p(ring, got_p(side))
            self.b_ag_out[...] = self.full[ring, :, lanes_at((2 * d1 + d2) * 128, 128)]
            value = self.q3[...] + self.b_rs_in[par, 64:80, :]
            self.full[ring, rows16(z), lanes_at(512 + 128 * d1, 128)] = value
            self.a_ag_out[128:144, :] = value

        @pl.when(live(5))
        def _stage5():
            ring = ring8(5)
            for side in range(2):
                @pl.when(lead[side] == 2)
                def _(side=side):
                    value = self.p3[ring4(5)] + got_p(side)
                    full_p(ring, value)
                    put_p(side, value)
            value = self.q2[...] + self.a_rs_in[par, 128:144, :]
            self.q3[...] = value
            self.b_rs_out[64:80, :] = value

        @pl.when(live(4))
        def _stage4():
            ring = ring4(4)
            for side in range(2):
                @pl.when(lead[side] == 1)
                def _(side=side):
                    value = self.p3[ring] + got_p(side)
                    self.p3[ring] = value
                    put_p(side, value)

            def own_q(panel):
                first = self.q1[ring, rows_at(64 * panel + 16 * z, 16), :]
                spot = rows_at(64 + 16 * panel, 16)
                return first + z_in[0, par, spot, :] + z_in[1, par, spot, :]

            self.q2[...] = own_q(d1)
            self.a_rs_out[128:144, :] = own_q(1 - d1)

        @pl.when(live(3))
        def _stage3():
            ring = ring4(3)
            for side in range(2):
                @pl.when(lead[side] <= 2)
                def _(side=side):
                    for panel in range(2):
                        own = self.q1[ring, rows_at(64 * panel + 16 * target(side, 3), 16), :]
                        put_q(side, 0, panel, own + got_q(side, 1, panel))
            value = self.p2[...] + self.b_rs_in[par, 0:64, :]
            self.p3[ring] = value
            for side in range(2):
                @pl.when(lead[side] == 0)
                def _(side=side):
                    put_p(side, value)

        @pl.when((t >= 2) & (t < self.count + 2))
        def _stage2():
            for side in range(2):
                @pl.when(lead[side] <= 1)
                def _(side=side):
                    for panel in range(2):
                        own = self.q1[ring4(2), rows_at(64 * panel + 16 * target(side, 2), 16), :]
                        put_q(side, 1, panel, own + got_q(side, 2, panel))
            self.p2[...] = self.p1[rows_at(64 * d2, 64), :] + self.a_rs_in[par, rows_at(64 * d2, 64), :]
            self.b_rs_out[0:64, :] = self.p1[rows_at(64 * (1 - d2), 64), :] + self.a_rs_in[par, rows_at(64 * (1 - d2), 64), :]

        @pl.when((t >= 1) & (t < self.count + 1))
        def _stage1():
            slot, row = self.grad_rows(t - 1)
            mine = rows_at(row + 64 * place.c, 64)

            def summed(lane):
                spot = lanes_at(lane, 128)
                return self.grad_ref[slot, mine, spot] + self.sib_in[par, :, spot]

            for half in range(2):
                self.p1[64 * half:64 * half + 64, :] = summed(256 * d1 + 128 * half)
                self.a_rs_out[64 * half:64 * half + 64, :] = summed(256 * (1 - d1) + 128 * half)
            ring = ring4(1)
            for panel in range(2):
                self.q1[ring, 64 * panel:64 * panel + 64, :] = summed(512 + 128 * panel)
            for side in range(2):
                @pl.when(lead[side] == 0)
                def _(side=side, ring=ring):
                    for panel in range(2):
                        put_q(side, 2, panel, self.q1[ring, rows_at(64 * panel + 16 * target(side, 1), 16), :])


T0 = (((0,), (0,)), ((), ()))
NT = (((1,), (1,)), ((), ()))


def mm(left, right):
    return jnp.dot(left, right, preferred_element_type=F32)


def mm_nt(left, right):
    return lax.dot_general(left, right, NT, preferred_element_type=F32)


def mm_t(left, right):
    return lax.dot_general(left, right, T0, preferred_element_type=F32)


def row_of(ref):
    return ref[...].reshape(1, -1)


def normal_cdf(pre):
    return 0.5 + 0.5 * lax.erf(pre * 0.7071067811865476), jnp.exp(-0.5 * pre * pre)


G0, D0 = 0, 4
X, Q, K, V, O, Y1, DZ, DA, DO = 8, 9, 10, 11, 12, 13, 14, 15, 16
N_ACTS = 17
ROWS = 512
LATE = 8


class Net:
    def __init__(self, **refs):
        self.__dict__.update(refs)

    def project_q(self, i):
        rows = pl.ds(pl.multiple_of(i * ROWS, ROWS), ROWS)
        out = mm(self.acts[X, rows, :], self.w_q[...]) + row_of(self.query_bias)
        self.acts[Q, rows, :] = out.astype(BF) * BF(0.125)

    def project_k(self, i):
        rows = pl.ds(pl.multiple_of(i * ROWS, ROWS), ROWS)
        self.acts[K, rows, :] = mm(self.acts[X, rows, :], self.w_k[...]).astype(BF)

    def project_v(self, i):
        rows = pl.ds(pl.multiple_of(i * ROWS, ROWS), ROWS)
        self.acts[V, rows, :] = (mm(self.acts[X, rows, :], self.w_v[...]) + row_of(self.value_bias)).astype(BF)

    def masks(self):
        place = lax.broadcasted_iota(jnp.int32, (8, 512), 1)
        for s in range(2):
            self.key_row[s] = jnp.where(place < self.lengths[s], 0.0, -1e9)

    def attend(self, i):
        s, pair = i // 6, lax.rem(i, 6)
        rows = pl.ds(pl.multiple_of(s * 512, 512), 512)
        lanes = lanes_at(pair * 128, 128)
        acts = self.acts
        k = acts[K, rows, lanes]
        v = acts[V, rows, lanes]
        lane = lax.broadcasted_iota(jnp.int32, (1, 128), 1)
        v_ones = jnp.concatenate([v, jnp.ones((512, 128), BF)], axis=1)
        q = acts[Q, rows, lanes]
        boths, tops = [], []
        for head in range(2):
            live = (lane >= 64) if head else (lane < 64)
            score = mm_nt(jnp.where(live, q, BF(0)), k) + self.key_row[s, 0:1, :]
            top = jnp.max(score, axis=1, keepdims=True)
            boths.append(mm(jnp.exp(score - top).astype(BF), v_ones))
            tops.append(top)
        pick = lane < 64
        mixed = jnp.where(pick, boths[0][:, :128], boths[1][:, :128])
        total = jnp.where(pick, boths[0][:, 128:], boths[1][:, 128:])
        acts[O, rows, lanes] = (mixed * pl.reciprocal(total, approx=False)).astype(BF)
        one, two = lane == 2 * pair, lane == 2 * pair + 1
        self.logs[s] = jnp.where(one, tops[0], jnp.where(two, tops[1], self.logs[s]))
        self.sums[s] = jnp.where(one, boths[0][:, 128:], jnp.where(two, boths[1][:, 128:], self.sums[s]))

    def normed(self, rows):
        mean = jnp.sum(rows, axis=1, keepdims=True) * (1.0 / 768)
        centred = rows - mean
        spread = jnp.sum(centred * centred, axis=1, keepdims=True) * (1.0 / 768)
        inverse = lax.rsqrt(spread + 1e-6)
        return centred * inverse, inverse

    def feed(self, i):
        rows = pl.ds(pl.multiple_of(i * ROWS, ROWS), ROWS)
        acts = self.acts
        h1 = acts[X, rows, :].astype(F32) + mm(acts[O, rows, :], self.w_m[...]) + row_of(self.mixer_bias)
        n1, r1 = self.normed(h1)
        self.n1[rows, :] = n1.astype(self.n1.dtype)
        self.r1[rows, :] = jnp.broadcast_to(r1, (ROWS, 128))
        y1 = n1 * row_of(self.first_gain) + row_of(self.first_shift)
        self.z[...] = y1 + row_of(self.shrink_bias)
        acts[Y1, rows, :] = y1.astype(BF)
        for j in range(4):
            self.feed_block(rows, j)
        n2, r2 = self.normed(self.z[...])
        self.n2[rows, :] = n2
        self.r2[rows, :] = jnp.broadcast_to(r2, (ROWS, 128))
        each = 512 // ROWS
        s, part = i // each, lax.rem(i, each)
        at = lax.broadcasted_iota(jnp.int32, (ROWS, 1), 0) + part * ROWS
        live = jnp.where(at < self.lengths[s], n2, 0.0)
        some = jnp.sum(live, axis=0, keepdims=True)
        self.n2_sum[s, 0:1, :] = jnp.where(part == 0, some, self.n2_sum[s, 0:1, :] + some)

    def feed_block(self, rows, j):
        acts = self.acts
        cols = pl.ds(768 * j, 768)
        pre = mm(acts[Y1, rows, :], self.w_e[:, cols]) + self.expand_bias[cols].reshape(1, 768)
        cdf, bell = normal_cdf(pre)
        low = (pre * cdf).astype(BF)
        acts[G0 + j, rows, :] = low
        acts[D0 + j, rows, :] = (cdf + pre * bell * 0.3989422804014327).astype(BF)
        self.z[...] += mm(low, self.w_s[cols, :])

    def pool(self, s):
        count = self.lengths[s].astype(F32)
        return self.n2_sum[s, 0:1, :] * row_of(self.second_gain) / count + row_of(self.second_shift)


class Back(Net):
    def share_vectors(self, place, k):
        mine = rows_at(8 * place.c, 8)
        z = place.z
        target = (place.sibling, place.to_x, place.to_y, place.me + 8 - 16 * (z % 2), place.me + 16 - 32 * (z // 2),
                  place.sibling)[k]
        source = self.vec.at[rows_at(8 * (1 - place.c), 8)] if k == 0 else self.vec.at[mine]
        landing = self.vec.at[mine] if k == 5 else self.vec_in.at[k]
        return pltpu.make_async_remote_copy(
            src_ref=source, dst_ref=landing, send_sem=self.vec_sent.at[k], recv_sem=self.vec_came.at[k],
            device_id=(target,), device_id_type=MESH)

    def sum_vectors(self, place, turn):
        mine = rows_at(8 * place.c, 8)
        for k in range(6):
            @pl.when(turn == 76 + 3 * k)
            def _(k=k):
                self.share_vectors(place, k).start()

            @pl.when(turn == 79 + 3 * k)
            def _(k=k):
                copy = self.share_vectors(place, k)
                copy.wait_send()
                copy.wait_recv()
                if k < 5:
                    self.vec[mine, :] += self.vec_in[k]

    def turn_logs(self):
        for s in range(2):
            self.logs_t[s] = jnp.transpose(self.logs[s] + jnp.log(self.sums[s]))[0:16, :]

    def gather(self, place):
        c, chip = place.c, place.me // 2
        every = self.every
        for s in range(2):
            u = self.pool(s)
            for j in range(6):
                every[c, chip, 8 * s + j:8 * s + j + 1, :] = u[:, 128 * j:128 * j + 128]
            every[c, chip, 8 * s + 6:8 * s + 8, :] = jnp.full((2, 128), self.targets[s], F32)

        def copy(source, device):
            return pltpu.make_async_remote_copy(
                src_ref=every.at[c, source], dst_ref=every.at[c, source], send_sem=self.told.at[device // 2],
                recv_sem=self.heard.at[source], device_id=(device,), device_id_type=MESH)

        order = (12, 4, 13, 11, 3, 5, 14, 10, 2, 6, 15, 9, 1, 7, 8)
        for k in order:
            copy(chip, lax.rem(chip + k, 16) * 2 + c).start()
        for k in order:
            copy(lax.rem(chip + 16 - k, 16), place.me).wait_recv()
        share = pltpu.make_async_remote_copy(
            src_ref=every.at[c], dst_ref=every.at[c], send_sem=self.told.at[chip],
            recv_sem=self.heard.at[chip], device_id=(place.sibling,), device_id_type=MESH)
        share.start()
        for k in order:
            copy(chip, lax.rem(chip + k, 16) * 2 + c).wait_send()
        share.wait_send()
        share.wait_recv()

    def partners_of(self, place):
        first = place.me * 2
        wanted = [jnp.full((8, 128), self.partners[first + s], jnp.int32) for s in range(2)]

        def pick(i, found):
            device = i // 2
            tile = self.every[lax.rem(device, 2), device // 2, rows_at(8 * lax.rem(i, 2), 8), :]
            chosen = jnp.full((8, 128), self.partners[i], jnp.int32)
            return tuple(
                old + jnp.where(hit, tile, 0.0)
                for old, hit in zip(found, (wanted[0] == i, chosen == first, wanted[1] == i, chosen == first + 1)))

        return lax.fori_loop(0, 64, pick, (jnp.zeros((8, 128), F32),) * 4, unroll=8)

    def pair(self, place, s, far, near):
        mine = self.every[place.c, place.me // 2, 8 * s:8 * s + 8, :]
        live = lax.broadcasted_iota(jnp.int32, (8, 128), 0) < 6

        def inner(left, right):
            return jnp.sum(jnp.where(live, left * right, 0.0), axis=(0, 1), keepdims=True)

        length = jnp.sqrt(inner(mine, mine) + 1e-6)
        far_length = jnp.sqrt(inner(far, far) + 1e-6)
        near_length = jnp.sqrt(inner(near, near) + 1e-6)
        score = inner(mine, far) / (length * far_length)
        near_score = inner(near, mine) / (near_length * length)
        miss = score - mine[6:7, 0:1]
        near_miss = near_score - near[6:7, 0:1]
        own = mine / (length * length)
        grad = miss * (far / (length * far_length) - score * own)
        grad += near_miss * (near / (near_length * length) - near_score * own)
        for j in range(6):
            self.du[s, 0:1, 128 * j:128 * j + 128] = grad[j:j + 1, :]
        self.scores[s:s + 1, :] = jnp.broadcast_to(score, (1, 128))

    def clear(self):
        self.vec[...] = jnp.zeros_like(self.vec)
        self.logs[...] = jnp.zeros_like(self.logs)
        self.sums[...] = jnp.ones_like(self.sums)

    def add_vec(self, at, rows):
        self.vec[at:at + 1, :] += jnp.sum(rows.astype(F32), axis=0, keepdims=True)

    def second_vectors(self):
        gain = jnp.zeros((1, 768), F32)
        for s in range(2):
            gain += self.du[s, 0:1, :] * self.n2_sum[s, 0:1, :] / self.lengths[s].astype(F32)
        self.vec[6:7, :] = gain
        self.vec[7:8, :] = self.du[0, 0:1, :] + self.du[1, 0:1, :]

    def back_second(self, i):
        rows = pl.ds(pl.multiple_of(i * 256, 256), 256)
        s = i // 2
        up = self.du[s, 0:1, :] * row_of(self.second_gain) / self.lengths[s].astype(F32)
        mean = jnp.sum(up, axis=1, keepdims=True) * (1.0 / 768)
        n2 = self.n2[rows, :]
        along = jnp.sum(n2 * up, axis=1, keepdims=True) * (1.0 / 768)
        at = lax.broadcasted_iota(jnp.int32, (256, 1), 0) + lax.rem(i, 2) * 256
        dh2 = jnp.where(at < self.lengths[s], self.r2[rows, 0:1] * (up - mean - n2 * along), 0.0)
        self.n2[rows, :] = dh2
        dz = dh2.astype(BF)
        self.acts[DZ, rows, :] = dz
        self.add_vec(5, dz)

    def back_hidden(self, i):
        j, half = i // 2, lax.rem(i, 2)
        rows = pl.ds(pl.multiple_of(half * 512, 512), 512)
        units = pl.ds(pl.multiple_of(j * 768, 768), 768)
        df = (mm_nt(self.acts[DZ, rows, :], self.w_s[units, :]) * self.acts[D0 + j, rows, :].astype(F32)).astype(BF)
        self.acts[D0 + j, rows, :] = df
        part = jnp.sum(df.astype(F32), axis=0, keepdims=True)
        line = lax.broadcasted_iota(jnp.int32, (8, 768), 0) == j
        self.vec[8:16, :] += jnp.where(line, part, 0.0)

    def back_first(self, i):
        rows = pl.ds(pl.multiple_of(i * 256, 256), 256)
        acts = self.acts
        up = self.n2[rows, :]
        for j in range(4):
            up += mm_nt(acts[D0 + j, rows, :], self.w_e[:, 768 * j:768 * j + 768])
        n1 = self.n1[rows, :].astype(F32)
        self.add_vec(3, up * n1)
        self.add_vec(4, up)
        dn = up * row_of(self.first_gain)
        mean = jnp.sum(dn, axis=1, keepdims=True) * (1.0 / 768)
        along = jnp.sum(dn * n1, axis=1, keepdims=True) * (1.0 / 768)
        dh1 = self.r1[rows, 0:1] * (dn - mean - n1 * along)
        self.n2[rows, :] = dh1
        da = dh1.astype(BF)
        acts[DA, rows, :] = da
        self.add_vec(2, da)
        acts[DO, rows, :] = mm_nt(da, self.w_m[...]).astype(BF)

    def attend_back(self, i):
        s, head = i // 12, lax.rem(i, 12)
        rows = pl.ds(pl.multiple_of(s * 512, 512), 512)
        lanes = lanes_at((head // 2) * 128, 128)
        acts = self.acts
        lane = lax.broadcasted_iota(jnp.int32, (1, 128), 1)
        live = (lane // 64) == lax.rem(head, 2)
        q_all, k, v = acts[Q, rows, lanes], acts[K, rows, lanes], acts[V, rows, lanes]
        q = jnp.where(live, q_all, BF(0))
        up = jnp.where(live, acts[DO, rows, lanes], BF(0))
        place = lax.broadcasted_iota(jnp.int32, (512, 1), 0)
        off = jnp.where(place < self.lengths[s], 0.0, -1e9)
        probs = jnp.exp(mm_nt(k, q) + off - self.logs_t[s, pl.ds(head, 1), :])
        weighed = probs * mm_nt(v, up)
        delta = jnp.sum(weighed, axis=0, keepdims=True)
        ds = (weighed - probs * delta).astype(BF)
        dv = mm(probs.astype(BF), up)
        dk = mm(ds, q)
        dq = mm_t(ds, k) * 0.125
        acts[Q, rows, lanes] = jnp.where(live, dq.astype(BF), q_all)
        acts[K, rows, lanes] = jnp.where(live, dk.astype(BF), k)
        acts[V, rows, lanes] = jnp.where(live, dv.astype(BF), v)

    def back_tokens(self, i):
        rows = pl.ds(pl.multiple_of(i * 256, 256), 256)
        dq, dk, dv = self.acts[Q, rows, :], self.acts[K, rows, :], self.acts[V, rows, :]
        self.add_vec(0, dq)
        self.add_vec(1, dv)
        self.n2[rows, :] += mm_nt(dq, self.w_q[...]) + mm_nt(dk, self.w_k[...]) + mm_nt(dv, self.w_v[...])

    def back_task(self, i):
        pl.when(i < 8)(lambda: self.back_hidden(i))
        pl.when((i >= 8) & (i < 12))(lambda: self.back_first(i - 8))
        pl.when((i >= 12) & (i < 36))(lambda: self.attend_back(i - 12))
        pl.when((i >= 36) & (i < 40))(lambda: self.back_tokens(i - 36))

    def grad_piece(self, i):
        b = i // 3
        slot = lax.rem(i, 2)
        cols = pl.ds(pl.multiple_of(lax.rem(i, 3) * 256, 256), 256)
        left = jnp.where(b < 4, G0 + b, jnp.where(b < 8, Y1, jnp.where(b < 9, O, X)))
        right = jnp.where(b < 4, DZ, jnp.where(b < 8, D0 + b - 4, jnp.where(b < 9, DA, b)))
        self.ring[slot] = mm_t(self.acts[left, :, cols], self.acts[right])


N_IN = 19
VMEM_LIMIT = 54 << 20
VECTORS = ("query_bias", "value_bias", "mixer_bias", "first_gain", "first_shift", "shrink_bias", "second_gain",
           "second_shift")


def layer_kernel(*refs):
    (tokens, lengths, partners, targets, w_q, query_bias, w_k, w_v, value_bias, w_m, mixer_bias, first_gain,
     first_shift, w_e, expand_bias, w_s, shrink_bias, second_gain, second_shift) = refs[:N_IN]
    scores, late, vec, summed = refs[N_IN:N_IN + 4]
    rest = refs[N_IN + 4:]
    (acts, v_q, v_k, v_v, v_m, v_e, v_s, key_row, logs, sums, logs_t, r1, r2, n2_sum, every, du, vec_in, ring,
     loaded, told, heard, vec_sent, vec_came) = rest[:23]
    n2, n1, z = late.at[pl.ds(0, 1024)], late.at[pl.ds(1024, 1024)], late.at[pl.ds(2048, ROWS)]
    first, second = rest[23:23 + N_STREAM_SCRATCH], rest[23 + N_STREAM_SCRATCH:]
    place = Place()
    net = Back(
        acts=acts, w_q=v_q, w_k=v_k, w_v=v_v, w_m=v_m, w_e=v_e, w_s=v_s, query_bias=query_bias, value_bias=value_bias,
        mixer_bias=mixer_bias, first_gain=first_gain, first_shift=first_shift, expand_bias=expand_bias,
        shrink_bias=shrink_bias, second_gain=second_gain, second_shift=second_shift, lengths=lengths,
        partners=partners, targets=targets, scores=scores, key_row=key_row, logs=logs, sums=sums,
        logs_t=logs_t, n1=n1, r1=r1, n2=n2, r2=r2, z=z, n2_sum=n2_sum, every=every, du=du, vec=vec, ring=ring,
        told=told, heard=heard, vec_in=vec_in, vec_sent=vec_sent, vec_came=vec_came)
    loads = [pltpu.make_async_copy(src, dst, loaded.at[i]) for i, (src, dst) in enumerate([
        (tokens, acts.at[X]), (w_q, v_q), (w_k, v_k), (w_v, v_v), (w_m, v_m), (w_e, v_e), (w_s, v_s)])]
    for copy in loads[:4]:
        copy.start()

    def chunk_rows(t, shift):
        t = jnp.clip(t, 0, 36)
        return lax.rem(t, 2), shift

    def outs(m, shift):
        early = rows_at(jnp.clip(m, 0, 35 - LATE) * 256 + shift, 64)
        last = rows_at(1024 + (jnp.clip(m, 36 - LATE, 35) - (36 - LATE)) * 256 + shift, 64)
        return [(summed.at[early], m < 36 - LATE), (late.at[last], m >= 36 - LATE)]

    one = Stream(place, 0, 36, first, ring, lambda t: chunk_rows(t, 0), outs)
    two = Stream(place, 1, 36, second, ring, lambda t: chunk_rows(t, 128), lambda m, at: outs(m, 128 + at))
    one.prepare()
    two.prepare()
    greet_all(place)

    def each(count, task):
        def step(i, carry):
            task(i)
            return carry

        lax.fori_loop(0, count, step, 0)

    net.masks()
    net.clear()
    loads[0].wait()
    loads[1].wait()
    each(1024 // ROWS, net.project_q)
    loads[2].wait()
    loads[3].wait()
    for copy in loads[4:]:
        copy.start()
    each(1024 // ROWS, net.project_k)
    each(1024 // ROWS, net.project_v)
    each(12, net.attend)
    net.turn_logs()
    for copy in loads[4:]:
        copy.wait()
    each(1024 // ROWS, net.feed)
    await_all()
    net.gather(place)
    tiles = net.partners_of(place)
    for s in range(2):
        net.pair(place, s, tiles[2 * s], tiles[2 * s + 1])
    net.second_vectors()
    each(4, net.back_second)

    first_task = 12

    def step(turn, carry):
        t = turn // 2 - 1
        side = lax.rem(turn, 2)

        for i, stream in enumerate((one, two)):
            @pl.when((side == i) & (t >= 0))
            def _(stream=stream):
                stream.wait(t - 1)
                stream.work(t)
                stream.start(t)

        pl.when((side == 1) & (t + 1 < 36))(lambda: net.grad_piece(t + 1))
        task = turn - 2 - first_task
        pl.when((task >= 0) & (task < 40))(lambda: net.back_task(task))
        net.sum_vectors(place, turn)
        return carry

    lax.fori_loop(1, 2 * 47 + 2, step, 0)


def greet_all(place):
    bar = pltpu.get_barrier_semaphore()
    chip = place.me // 2

    def hail(k, carry):
        pl.semaphore_signal(bar, 1, device_id=(lax.rem(chip + k, 16) * 2 + place.c,), device_id_type=MESH)
        return carry

    pl.semaphore_signal(bar, 1, device_id=(place.sibling,), device_id_type=MESH)
    lax.fori_loop(1, 16, hail, 0)


def await_all():
    pl.semaphore_wait(pltpu.get_barrier_semaphore(), 16)


def whole_layer(*args):
    anywhere = pl.BlockSpec(memory_space=pltpu.HBM)
    vector = pl.BlockSpec(memory_space=pltpu.VMEM)
    scalars = pl.BlockSpec(memory_space=pltpu.SMEM)
    specs = [anywhere if a.dtype == BF else vector if a.shape[0] >= 768 else scalars for a in args]

    def low(*shape):
        return pltpu.VMEM(shape, BF)

    def full(*shape):
        return pltpu.VMEM(shape, F32)

    return pl.pallas_call(
        layer_kernel,
        out_shape=(
            pltpu.VMEM((8, 128), F32),
            pltpu.VMEM((1024 + max(1024 + ROWS, 256 * LATE), 768), F32),
            pltpu.VMEM((16, 768), F32),
            jax.ShapeDtypeStruct((256 * (36 - LATE), 768), F32),
        ),
        in_specs=specs,
        out_specs=(vector, vector, vector, pl.BlockSpec(memory_space=pltpu.HBM)),
        scratch_shapes=[
            low(N_ACTS, 1024, 768),
            low(768, 768), low(768, 768), low(768, 768), low(768, 768), low(768, 3072), low(3072, 768),
            full(2, 8, 512), full(2, 512, 128), full(2, 512, 128), full(2, 16, 512),
            full(1024, 128), full(1024, 128), full(2, 8, 768),
            full(2, 16, 16, 128), full(2, 8, 768), full(5, 8, 768), full(2, 256, 768),
            pltpu.SemaphoreType.DMA((7,)), pltpu.SemaphoreType.DMA((16,)), pltpu.SemaphoreType.DMA((16,)),
            pltpu.SemaphoreType.DMA((6,)), pltpu.SemaphoreType.DMA((6,)),
        ] + stream_scratch() + stream_scratch(),
        compiler_params=pltpu.CompilerParams(
            collective_id=0, has_side_effects=True, vmem_limit_bytes=VMEM_LIMIT),
    )(*args)


def deliver_kernel(count, height, summed, late, small, scores, *refs):
    (scores_out, tokens_out, w_q, query_bias, w_k, w_v, value_bias, w_m, mixer_bias, first_gain, first_shift, w_e,
     expand_bias, w_s, shrink_bias, second_gain, second_shift) = refs[:17]
    buffer, came, left, sent = refs[17:]

    def place(row, size):
        block, at = row // 768, row % 768
        if block < 4:
            return w_s.at[pl.ds(row, size)]
        if block < 8:
            return w_e.at[pl.ds(at, size), pl.ds(768 * (block - 4), 768)]
        return (w_m, w_q, w_k, w_v)[block - 8].at[pl.ds(at, size)]

    early = summed.shape[0]
    direct = [pltpu.make_async_copy(late.at[pl.ds(0, 1024)], tokens_out, sent.at[0])]
    row = early
    while row < 9216:
        size = min(768 - row % 768, 9216 - row)
        direct.append(pltpu.make_async_copy(
            late.at[pl.ds(1024 + row - early, size)], place(row, size), sent.at[len(direct)]))
        row += size
    jobs = []
    row = 0
    while row < early:
        size = min(height, 768 - row % 768, early - row)
        jobs.append((row, size))
        row += size

    def copies(i):
        row, size = jobs[i]
        spot = buffer.at[i % count, pl.ds(0, size)]
        return (pltpu.make_async_copy(summed.at[pl.ds(row, size)], spot, came.at[i % count]),
                pltpu.make_async_copy(spot, place(row, size), left.at[i % count]))

    total = len(jobs)
    ahead = count // 2
    for i in range(min(ahead, total)):
        copies(i)[0].start()
    for copy in direct:
        copy.start()
    for j, ref in enumerate((query_bias, value_bias, mixer_bias, first_gain, first_shift, shrink_bias,
                             second_gain, second_shift)):
        ref[...] = small[j, :]
    for j in range(4):
        expand_bias[768 * j:768 * j + 768] = small[8 + j, :]
    for s in range(2):
        scores_out[s] = jnp.sum(scores[s:s + 1, 0:1])
    for i in range(total):
        copies(i)[0].wait()
        copies(i)[1].start()
        later = i + ahead
        if later < total:
            if later >= count:
                copies(later - count)[1].wait()
            copies(later)[0].start()
    for i in range(max(0, total - count), total):
        copies(i)[1].wait()
    for copy in direct:
        copy.wait()


def fused(*args):
    pair_scores, late, small, summed = whole_layer(*args)
    hbm = pl.BlockSpec(memory_space=pltpu.HBM)
    vector = pl.BlockSpec(memory_space=pltpu.VMEM)
    scalars = pl.BlockSpec(memory_space=pltpu.SMEM)
    shapes = [(2,), (1024, 768), (768, 768), (768,), (768, 768), (768, 768), (768,), (768, 768), (768,), (768,), (768,),
              (768, 3072), (3072,), (3072, 768), (768,), (768,), (768,)]
    count, height = 14, 384
    return tuple(pl.pallas_call(
        partial(deliver_kernel, count, height),
        out_shape=[jax.ShapeDtypeStruct(shape, F32) for shape in shapes],
        in_specs=[hbm, vector, vector, vector],
        out_specs=[hbm if len(shape) == 2 else vector if shape[0] > 2 else scalars for shape in shapes],
        scratch_shapes=[pltpu.VMEM((count, height, 768), F32),
                        pltpu.SemaphoreType.DMA((count,)), pltpu.SemaphoreType.DMA((count,)),
                        pltpu.SemaphoreType.DMA((16,))],
        compiler_params=pltpu.CompilerParams(vmem_limit_bytes=36 << 20),
    )(summed, late, small, pair_scores))


def to_low(value):
    return value.astype(jnp.bfloat16)


def tdot(left, right):
    return lax.dot_general(
        left, right, (((0,), (0,)), ((), ())), preferred_element_type=jnp.float32
    )


def ndot(left, right):
    return lax.dot_general(
        left, right, (((1,), (1,)), ((), ())), preferred_element_type=jnp.float32
    )


def norm_rows(rows, gain, shift):
    mean = jnp.mean(rows, axis=-1, keepdims=True)
    centred = rows - mean
    spread = jnp.mean(centred * centred, axis=-1, keepdims=True)
    inverse = lax.rsqrt(spread + 1e-06)
    normed = centred * inverse
    return (normed * gain + shift, normed, inverse)


def norm_back(upstream, normed, inverse, gain):
    gain_grad = jnp.sum(upstream * normed, axis=0)
    shift_grad = jnp.sum(upstream, axis=0)
    dnormed = upstream * gain
    first_mean = jnp.mean(dnormed, axis=-1, keepdims=True)
    second_mean = jnp.mean(dnormed * normed, axis=-1, keepdims=True)
    return (inverse * (dnormed - first_mean - normed * second_mean), gain_grad, shift_grad)


def per_device(
    tokens,
    lengths,
    partners,
    targets,
    query_proj,
    query_bias,
    key_proj,
    value_proj,
    value_bias,
    mixer_proj,
    mixer_bias,
    first_gain,
    first_shift,
    expand_proj,
    expand_bias,
    shrink_proj,
    shrink_bias,
    second_gain,
    second_shift,
):
    sents = lengths.shape[0]
    rows_all = tokens.shape[0]
    slot = rows_all // sents
    width = tokens.shape[1]
    heads = H
    depth = width // heads
    scale = 1.0 / math.sqrt(depth)
    total = partners.shape[0]
    base = lax.axis_index("dp") * sents
    highest = lax.Precision.HIGHEST
    places = jnp.arange(slot, dtype=jnp.int32)
    valid = places[None, :] < lengths[:, None]
    row_mask = valid.reshape(rows_all, 1).astype(jnp.float32)
    shape4 = (sents, slot, heads, depth)
    queries = to_low(jnp.dot(tokens, query_proj, preferred_element_type=jnp.float32) + query_bias)
    keys = to_low(jnp.dot(tokens, key_proj, preferred_element_type=jnp.float32))
    values = to_low(jnp.dot(tokens, value_proj, preferred_element_type=jnp.float32) + value_bias)
    queries4 = queries.reshape(shape4)
    keys4 = keys.reshape(shape4)
    values4 = values.reshape(shape4)

    def masked_scores(query_rows, key_rows, live):
        raw = (
            jnp.einsum("qhd,khd->hqk", query_rows, key_rows, preferred_element_type=jnp.float32)
            * scale
        )
        return jnp.where(live[None, None, :], raw, -1000000000.0)

    def attend(item):
        query_rows, key_rows, value_rows, live = item
        raw = masked_scores(query_rows, key_rows, live)
        top = jnp.max(raw, axis=-1, keepdims=True)
        expd = jnp.exp(raw - top)
        summed = jnp.sum(expd, axis=-1, keepdims=True)
        probs = to_low(expd / summed)
        mixed = jnp.einsum("hqk,khd->qhd", probs, value_rows, preferred_element_type=jnp.float32)
        return (mixed, (top + jnp.log(summed))[..., 0])

    mixed, logsum = lax.map(attend, (queries4, keys4, values4, valid))
    mixed_low = to_low(mixed.reshape(rows_all, width))
    branch = jnp.dot(mixed_low, mixer_proj, preferred_element_type=jnp.float32) + mixer_bias
    first_out, first_normed, first_inverse = norm_rows(
        tokens.astype(jnp.float32) + branch, first_gain, first_shift
    )
    first_low = to_low(first_out)
    pre = jnp.dot(first_low, expand_proj, preferred_element_type=jnp.float32) + expand_bias
    act, gelu_back = jax.vjp(partial(jax.nn.gelu, approximate=False), pre)
    act_low = to_low(act)
    shrink = jnp.dot(act_low, shrink_proj, preferred_element_type=jnp.float32) + shrink_bias
    outputs, second_normed, second_inverse = norm_rows(
        first_out + shrink, second_gain, second_shift
    )
    counts = lengths.astype(jnp.float32)
    pooled = jnp.sum((outputs * row_mask).reshape(sents, slot, width), axis=1) / counts[:, None]
    mine = lax.dynamic_slice_in_dim(partners, base, sents)
    every = lax.all_gather(pooled, "dp", axis=0, tiled=True)
    partner_vec = jnp.take(every, mine, axis=0)
    inner = jnp.sum(pooled * partner_vec, axis=-1)
    own_len = jnp.sqrt(jnp.sum(pooled * pooled, axis=-1) + 1e-06)
    far_len = jnp.sqrt(jnp.sum(partner_vec * partner_vec, axis=-1) + 1e-06)
    pair_scores = inner / (own_len * far_len)
    miss = pair_scores - targets
    joint = (own_len * far_len)[:, None]
    dpooled = miss[:, None] * (
        partner_vec / joint - (pair_scores / (own_len * own_len))[:, None] * pooled
    )
    dpartner = miss[:, None] * (
        pooled / joint - (pair_scores / (far_len * far_len))[:, None] * partner_vec
    )
    owners = (mine[:, None] == jnp.arange(total, dtype=jnp.int32)[None, :]).astype(jnp.float32)
    spread = lax.dot_general(owners, dpartner, (((0,), (0,)), ((), ())), precision=highest)
    returned = lax.psum_scatter(spread, "dp", scatter_dimension=0, tiled=True)
    dpool_all = (dpooled + returned) / counts[:, None]
    doutputs = (dpool_all[:, None, :] * valid[:, :, None].astype(jnp.float32)).reshape(
        rows_all, width
    )
    dsecond, second_gain_grad, second_shift_grad = norm_back(
        doutputs, second_normed, second_inverse, second_gain
    )
    dshrink = to_low(dsecond)
    shrink_proj_grad = tdot(act_low, dshrink)
    shrink_bias_grad = jnp.sum(dshrink.astype(jnp.float32), axis=0)
    dact = ndot(dshrink, shrink_proj)
    dpre = to_low(gelu_back(dact)[0])
    expand_proj_grad = tdot(first_low, dpre)
    expand_bias_grad = jnp.sum(dpre.astype(jnp.float32), axis=0)
    dfirst_out = ndot(dpre, expand_proj) + dsecond
    dfirst, first_gain_grad, first_shift_grad = norm_back(
        dfirst_out, first_normed, first_inverse, first_gain
    )
    dbranch = to_low(dfirst)
    mixer_proj_grad = tdot(mixed_low, dbranch)
    mixer_bias_grad = jnp.sum(dbranch.astype(jnp.float32), axis=0)
    dmixed = to_low(ndot(dbranch, mixer_proj)).reshape(shape4)

    def attend_back(item):
        query_rows, key_rows, value_rows, live, row_logsum, dmix = item
        raw = masked_scores(query_rows, key_rows, live)
        probs = jnp.exp(raw - row_logsum[..., None])
        probs_low = to_low(probs)
        dprob = jnp.einsum("qhd,khd->hqk", dmix, value_rows, preferred_element_type=jnp.float32)
        delta = jnp.sum(dprob * probs, axis=-1, keepdims=True)
        dscore = to_low(probs * (dprob - delta))
        dquery = (
            jnp.einsum("hqk,khd->qhd", dscore, key_rows, preferred_element_type=jnp.float32) * scale
        )
        dkey = (
            jnp.einsum("hqk,qhd->khd", dscore, query_rows, preferred_element_type=jnp.float32)
            * scale
        )
        dvalue = jnp.einsum("hqk,qhd->khd", probs_low, dmix, preferred_element_type=jnp.float32)
        return (to_low(dquery), to_low(dkey), to_low(dvalue))

    dquery, dkey, dvalue = lax.map(attend_back, (queries4, keys4, values4, valid, logsum, dmixed))
    dquery = dquery.reshape(rows_all, width)
    dkey = dkey.reshape(rows_all, width)
    dvalue = dvalue.reshape(rows_all, width)
    query_proj_grad = tdot(tokens, dquery)
    query_bias_grad = jnp.sum(dquery.astype(jnp.float32), axis=0)
    key_proj_grad = tdot(tokens, dkey)
    value_proj_grad = tdot(tokens, dvalue)
    value_bias_grad = jnp.sum(dvalue.astype(jnp.float32), axis=0)
    tokens_grad = (
        ndot(dquery, query_proj) + ndot(dkey, key_proj) + ndot(dvalue, value_proj) + dfirst
    )
    (
        query_proj_grad,
        query_bias_grad,
        key_proj_grad,
        value_proj_grad,
        value_bias_grad,
        mixer_proj_grad,
        mixer_bias_grad,
        first_gain_grad,
        first_shift_grad,
        expand_proj_grad,
        expand_bias_grad,
        shrink_proj_grad,
        shrink_bias_grad,
        second_gain_grad,
        second_shift_grad,
    ) = lax.psum(
        (
            query_proj_grad,
            query_bias_grad,
            key_proj_grad,
            value_proj_grad,
            value_bias_grad,
            mixer_proj_grad,
            mixer_bias_grad,
            first_gain_grad,
            first_shift_grad,
            expand_proj_grad,
            expand_bias_grad,
            shrink_proj_grad,
            shrink_bias_grad,
            second_gain_grad,
            second_shift_grad,
        ),
        "dp",
    )
    return (
        pair_scores,
        tokens_grad,
        query_proj_grad,
        query_bias_grad,
        key_proj_grad,
        value_proj_grad,
        value_bias_grad,
        mixer_proj_grad,
        mixer_bias_grad,
        first_gain_grad,
        first_shift_grad,
        expand_proj_grad,
        expand_bias_grad,
        shrink_proj_grad,
        shrink_bias_grad,
        second_gain_grad,
        second_shift_grad,
    )


def solution(mesh):
    in_specs = (
        P("dp", None),
        P("dp"),
        P(),
        P("dp"),
        P(),
        P(),
        P(),
        P(),
        P(),
        P(),
        P(),
        P(),
        P(),
        P(),
        P(),
        P(),
        P(),
        P(),
        P(),
    )
    out_specs = (
        P("dp"),
        P("dp", None),
        P(),
        P(),
        P(),
        P(),
        P(),
        P(),
        P(),
        P(),
        P(),
        P(),
        P(),
        P(),
        P(),
        P(),
        P(),
    )
    plain = mesh.shape["dp"] != 32
    return jax.shard_map(
        per_device if plain else fused, mesh=mesh, in_specs=in_specs, out_specs=out_specs, check_vma=False
    )
```

```python
from functools import partial
import math

import jax
import jax.numpy as jnp
from jax import lax
from jax.sharding import PartitionSpec as P

from jax.experimental import pallas as pl
from jax.experimental.pallas import tpu as pltpu

H = 12

MESH = pl.DeviceIdType.MESH
F32 = jnp.float32
BF = jnp.bfloat16


def rows16(index):
    return pl.ds(pl.multiple_of(index * 16, 16), 16)


def rows_at(start, size):
    return pl.ds(pl.multiple_of(start, 8), size)


def lanes_at(start, size):
    return pl.ds(pl.multiple_of(start, 128), size)


class Place:
    def __init__(self):
        me = lax.axis_index("dp")
        self.me = me
        self.c = me % 2
        self.x = (me // 2) % 2
        self.y = (me // 4) % 2
        self.z = me // 8
        self.sibling = me + 1 - 2 * self.c
        self.to_x = me + 2 - 4 * self.x
        self.to_y = me + 4 - 8 * self.y
        self.up = me + 8
        self.down = me - 8


def stream_scratch():
    return [
        pltpu.VMEM((2, 64, 768), F32),
        pltpu.VMEM((144, 128), F32),
        pltpu.VMEM((2, 144, 128), F32),
        pltpu.VMEM((144, 128), F32),
        pltpu.VMEM((2, 144, 128), F32),
        pltpu.VMEM((80, 128), F32),
        pltpu.VMEM((2, 80, 128), F32),
        pltpu.VMEM((64, 128), F32),
        pltpu.VMEM((2, 64, 128), F32),
        pltpu.VMEM((2, 192, 128), F32),
        pltpu.VMEM((2, 2, 192, 128), F32),
        pltpu.VMEM((128, 128), F32),
        pltpu.VMEM((64, 128), F32),
        pltpu.VMEM((4, 64, 128), F32),
        pltpu.VMEM((4, 128, 128), F32),
        pltpu.VMEM((16, 128), F32),
        pltpu.VMEM((16, 128), F32),
        pltpu.VMEM((8, 64, 768), F32),
        pltpu.SemaphoreType.DMA((10, 2)),
        pltpu.SemaphoreType.DMA((10, 2)),
        pltpu.SemaphoreType.DMA((2,)),
    ]


N_STREAM_SCRATCH = 21


class Stream:
    def __init__(self, place, which, count, refs, grad_ref, grad_rows, outs):
        (self.sib_in, self.a_rs_out, self.a_rs_in, self.a_ag_out, self.a_ag_in, self.b_rs_out, self.b_rs_in,
         self.b_ag_out, self.b_ag_in, self.z_out, self.z_in, self.p1, self.p2, self.p3, self.q1, self.q2, self.q3,
         self.full, self.sent, self.came, self.kept) = refs
        self.place = place
        self.count = count
        self.grad_ref = grad_ref
        self.grad_rows = grad_rows
        self.outs = outs
        if which == 0:
            self.d1, self.d2, self.to_a, self.to_b = place.x, place.y, place.to_x, place.to_y
        else:
            self.d1, self.d2, self.to_a, self.to_b = place.y, place.x, place.to_y, place.to_x

    def prepare(self):
        zero = jnp.zeros((192, 128), F32)
        for side in range(2):
            for parity in range(2):
                self.z_in[side, parity] = zero

    def copies(self, t):
        place, n = self.place, self.count
        par = t % 2

        def remote(i, src, dst, target):
            return pltpu.make_async_remote_copy(
                src_ref=src, dst_ref=dst, send_sem=self.sent.at[i, par], recv_sem=self.came.at[i, par],
                device_id=(target,), device_id_type=MESH)

        def tail(i, src, dst, at, size, target):
            return remote(i, src.at[pl.ds(at, size)], dst.at[par, pl.ds(at, size)], target)

        slot, row = self.grad_rows(t)
        other = rows_at(row + 64 * (1 - place.c), 64)
        m = t - 10
        ring = lax.rem(t + 6, 8)
        outs = self.outs(m, 64 * place.c)
        lead = (place.z, 3 - place.z)
        zs = []
        for side, device in ((0, place.up), (1, place.down)):
            for half, when in ((0, (t >= 1) & (t < n + 6)), (1, (t >= 7) & (t < n + 9))):
                for k in range(3):
                    at, size = (0, 160 - 32 * k) if half == 0 else (160 - 32 * k, 32 + 32 * k)
                    spot = pl.ds(at, size)
                    copy = remote(5 + 2 * side + half, self.z_out.at[side, spot], self.z_in.at[side, par, spot], device)
                    zs.append((copy, when, lead[side] == k, lead[side] == k + 1))
        return [
            (remote(0, self.grad_ref.at[slot, other], self.sib_in.at[par], place.sibling), (t >= 0) & (t < n), True, True),
            (remote(1, self.a_rs_out, self.a_rs_in.at[par], self.to_a), (t >= 1) & (t < n + 1), True, True),
            (tail(1, self.a_rs_out, self.a_rs_in, 128, 16, self.to_a), (t >= n + 1) & (t < n + 4), True, True),
            (remote(2, self.a_ag_out, self.a_ag_in.at[par], self.to_a), (t >= 6) & (t < n + 7), True, True),
            (remote(3, self.b_rs_out, self.b_rs_in.at[par], self.to_b), (t >= 2) & (t < n + 2), True, True),
            (tail(3, self.b_rs_out, self.b_rs_in, 64, 16, self.to_b), (t >= n + 2) & (t < n + 5), True, True),
            (remote(4, self.b_ag_out, self.b_ag_in.at[par], self.to_b), (t >= 6) & (t < n + 6), True, True),
        ] + zs + [
            (remote(9, self.full.at[ring], spot, place.sibling), (t >= 10) & (t < n + 10) & when, True, True)
            for spot, when in outs
        ], [(pltpu.make_async_copy(self.full.at[ring], spot, self.kept.at[par]), (t >= 10) & (t < n + 10) & when)
            for spot, when in outs]

    def start(self, t):
        remote, local = self.copies(t)
        for copy, when, sends, _ in remote:
            pl.when(when if sends is True else when & sends)(copy.start)
        for copy, when in local:
            pl.when(when)(copy.start)

    def wait(self, t):
        remote, local = self.copies(t)
        for copy, when, sends, takes in remote:
            if sends is True:
                @pl.when(when)
                def _(copy=copy):
                    copy.wait_send()
                    copy.wait_recv()
            else:
                pl.when(when & sends)(copy.wait_send)
                pl.when(when & takes)(copy.wait_recv)
        for copy, when in local:
            pl.when(when)(copy.wait)

    def work(self, t):
        place = self.place
        z, d1, d2 = place.z, self.d1, self.d2
        par = (t + 1) % 2
        z_in, z_out = self.z_in, self.z_out
        lead = (z, 3 - z)

        def far(side, k):
            return z - k if side == 0 else z + k

        def target(side, step):
            return z + 4 - step if side == 0 else z - 4 + step

        def ring4(stage):
            return lax.rem(t + 16 - stage, 4)

        def ring8(stage):
            return lax.rem(t + 16 - stage, 8)

        def got_p(side):
            return z_in[side, par, 0:64, :]

        def got_q(side, pos, panel):
            at = 64 + 32 * pos + 16 * panel
            return z_in[side, par, at:at + 16, :]

        def put_p(side, value):
            z_out[side, 0:64, :] = value

        def put_q(side, pos, panel, value):
            at = 64 + 32 * pos + 16 * panel
            z_out[side, at:at + 16, :] = value

        def full_p(ring, value):
            self.full[ring, :, lanes_at((2 * d1 + d2) * 128, 128)] = value

        def full_q(ring, block, panel, value):
            self.full[ring, rows16(block), 512 + 128 * panel:640 + 128 * panel] = value

        def live(stage):
            return (t >= stage) & (t < self.count + stage)

        @pl.when(live(10))
        def _stage10():
            ring = ring8(10)
            for side in range(2):
                @pl.when(lead[side] == 3)
                def _(side=side):
                    for panel in range(2):
                        full_q(ring, far(side, 3), panel, got_q(side, 1, panel))

        @pl.when(live(9))
        def _stage9():
            ring = ring8(9)
            for side in range(2):
                @pl.when(lead[side] >= 2)
                def _(side=side):
                    for panel in range(2):
                        value = got_q(side, 2, panel)
                        full_q(ring, far(side, 2), panel, value)
                        put_q(side, 1, panel, value)

        @pl.when(live(8))
        def _stage8():
            ring = ring8(8)
            self.full[ring, :, lanes_at((1 - d1) * 256, 128)] = self.a_ag_in[par, 0:64, :]
            self.full[ring, :, lanes_at((1 - d1) * 256 + 128, 128)] = self.a_ag_in[par, 64:128, :]
            for side in range(2):
                @pl.when(lead[side] >= 1)
                def _(side=side):
                    for panel in range(2):
                        value = got_q(side, 3, panel)
                        full_q(ring, far(side, 1), panel, value)
                        put_q(side, 2, panel, value)

        @pl.when(live(7))
        def _stage7():
            ring = ring8(7)
            other = self.b_ag_in[par]
            self.full[ring, :, lanes_at((2 * d1 + 1 - d2) * 128, 128)] = other
            self.a_ag_out[rows_at(64 * (1 - d2), 64), :] = other
            self.a_ag_out[rows_at(64 * d2, 64), :] = self.full[ring, :, lanes_at((2 * d1 + d2) * 128, 128)]
            self.full[ring, rows16(z), lanes_at(512 + 128 * (1 - d1), 128)] = self.a_ag_in[par, 128:144, :]
            for panel in range(2):
                value = self.full[ring, rows16(z), 512 + 128 * panel:640 + 128 * panel]
                for side in range(2):
                    put_q(side, 3, panel, value)

        @pl.when(live(6))
        def _stage6():
            ring = ring8(6)
            for side in range(2):
                @pl.when(lead[side] == 3)
                def _(side=side):
                    full_p(ring, got_p(side))
            self.b_ag_out[...] = self.full[ring, :, lanes_at((2 * d1 + d2) * 128, 128)]
            value = self.q3[...] + self.b_rs_in[par, 64:80, :]
            self.full[ring, rows16(z), lanes_at(512 + 128 * d1, 128)] = value
            self.a_ag_out[128:144, :] = value

        @pl.when(live(5))
        def _stage5():
            ring = ring8(5)
            for side in range(2):
                @pl.when(lead[side] == 2)
                def _(side=side):
                    value = self.p3[ring4(5)] + got_p(side)
                    full_p(ring, value)
                    put_p(side, value)
            value = self.q2[...] + self.a_rs_in[par, 128:144, :]
            self.q3[...] = value
            self.b_rs_out[64:80, :] = value

        @pl.when(live(4))
        def _stage4():
            ring = ring4(4)
            for side in range(2):
                @pl.when(lead[side] == 1)
                def _(side=side):
                    value = self.p3[ring] + got_p(side)
                    self.p3[ring] = value
                    put_p(side, value)

            def own_q(panel):
                first = self.q1[ring, rows_at(64 * panel + 16 * z, 16), :]
                spot = rows_at(64 + 16 * panel, 16)
                return first + z_in[0, par, spot, :] + z_in[1, par, spot, :]

            self.q2[...] = own_q(d1)
            self.a_rs_out[128:144, :] = own_q(1 - d1)

        @pl.when(live(3))
        def _stage3():
            ring = ring4(3)
            for side in range(2):
                @pl.when(lead[side] <= 2)
                def _(side=side):
                    for panel in range(2):
                        own = self.q1[ring, rows_at(64 * panel + 16 * target(side, 3), 16), :]
                        put_q(side, 0, panel, own + got_q(side, 1, panel))
            value = self.p2[...] + self.b_rs_in[par, 0:64, :]
            self.p3[ring] = value
            for side in range(2):
                @pl.when(lead[side] == 0)
                def _(side=side):
                    put_p(side, value)

        @pl.when((t >= 2) & (t < self.count + 2))
        def _stage2():
            for side in range(2):
                @pl.when(lead[side] <= 1)
                def _(side=side):
                    for panel in range(2):
                        own = self.q1[ring4(2), rows_at(64 * panel + 16 * target(side, 2), 16), :]
                        put_q(side, 1, panel, own + got_q(side, 2, panel))
            self.p2[...] = self.p1[rows_at(64 * d2, 64), :] + self.a_rs_in[par, rows_at(64 * d2, 64), :]
            self.b_rs_out[0:64, :] = self.p1[rows_at(64 * (1 - d2), 64), :] + self.a_rs_in[par, rows_at(64 * (1 - d2), 64), :]

        @pl.when((t >= 1) & (t < self.count + 1))
        def _stage1():
            slot, row = self.grad_rows(t - 1)
            mine = rows_at(row + 64 * place.c, 64)

            def summed(lane):
                spot = lanes_at(lane, 128)
                return self.grad_ref[slot, mine, spot] + self.sib_in[par, :, spot]

            for half in range(2):
                self.p1[64 * half:64 * half + 64, :] = summed(256 * d1 + 128 * half)
                self.a_rs_out[64 * half:64 * half + 64, :] = summed(256 * (1 - d1) + 128 * half)
            ring = ring4(1)
            for panel in range(2):
                self.q1[ring, 64 * panel:64 * panel + 64, :] = summed(512 + 128 * panel)
            for side in range(2):
                @pl.when(lead[side] == 0)
                def _(side=side, ring=ring):
                    for panel in range(2):
                        put_q(side, 2, panel, self.q1[ring, rows_at(64 * panel + 16 * target(side, 1), 16), :])


T0 = (((0,), (0,)), ((), ()))
NT = (((1,), (1,)), ((), ()))


def mm(left, right):
    return jnp.dot(left, right, preferred_element_type=F32)


def mm_nt(left, right):
    return lax.dot_general(left, right, NT, preferred_element_type=F32)


def mm_t(left, right):
    return lax.dot_general(left, right, T0, preferred_element_type=F32)


def row_of(ref):
    return ref[...].reshape(1, -1)


def normal_cdf(pre):
    return 0.5 + 0.5 * lax.erf(pre * 0.7071067811865476), jnp.exp(-0.5 * pre * pre)


G0, D0 = 0, 4
X, Q, K, V, O, Y1, DZ, DA, DO = 8, 9, 10, 11, 12, 13, 14, 15, 16
N_ACTS = 17
ROWS = 512
LATE = 8


class Net:
    def __init__(self, **refs):
        self.__dict__.update(refs)

    def project_q(self, i):
        rows = pl.ds(pl.multiple_of(i * ROWS, ROWS), ROWS)
        out = mm(self.acts[X, rows, :], self.w_q[...]) + row_of(self.query_bias)
        self.acts[Q, rows, :] = out.astype(BF) * BF(0.125)

    def project_k(self, i):
        rows = pl.ds(pl.multiple_of(i * ROWS, ROWS), ROWS)
        self.acts[K, rows, :] = mm(self.acts[X, rows, :], self.w_k[...]).astype(BF)

    def project_v(self, i):
        rows = pl.ds(pl.multiple_of(i * ROWS, ROWS), ROWS)
        self.acts[V, rows, :] = (mm(self.acts[X, rows, :], self.w_v[...]) + row_of(self.value_bias)).astype(BF)

    def masks(self):
        place = lax.broadcasted_iota(jnp.int32, (8, 512), 1)
        for s in range(2):
            self.key_row[s] = jnp.where(place < self.lengths[s], 0.0, -1e9)

    def attend(self, i):
        s, pair = i // 6, lax.rem(i, 6)
        rows = pl.ds(pl.multiple_of(s * 512, 512), 512)
        lanes = lanes_at(pair * 128, 128)
        acts = self.acts
        k = acts[K, rows, lanes]
        v = acts[V, rows, lanes]
        lane = lax.broadcasted_iota(jnp.int32, (1, 128), 1)
        v_ones = jnp.concatenate([v, jnp.ones((512, 128), BF)], axis=1)
        q = acts[Q, rows, lanes]
        boths, tops = [], []
        for head in range(2):
            live = (lane >= 64) if head else (lane < 64)
            score = mm_nt(jnp.where(live, q, BF(0)), k) + self.key_row[s, 0:1, :]
            top = jnp.max(score, axis=1, keepdims=True)
            boths.append(mm(jnp.exp(score - top).astype(BF), v_ones))
            tops.append(top)
        pick = lane < 64
        mixed = jnp.where(pick, boths[0][:, :128], boths[1][:, :128])
        total = jnp.where(pick, boths[0][:, 128:], boths[1][:, 128:])
        acts[O, rows, lanes] = (mixed * pl.reciprocal(total, approx=False)).astype(BF)
        one, two = lane == 2 * pair, lane == 2 * pair + 1
        self.logs[s] = jnp.where(one, tops[0], jnp.where(two, tops[1], self.logs[s]))
        self.sums[s] = jnp.where(one, boths[0][:, 128:], jnp.where(two, boths[1][:, 128:], self.sums[s]))

    def normed(self, rows):
        mean = jnp.sum(rows, axis=1, keepdims=True) * (1.0 / 768)
        centred = rows - mean
        spread = jnp.sum(centred * centred, axis=1, keepdims=True) * (1.0 / 768)
        inverse = lax.rsqrt(spread + 1e-6)
        return centred * inverse, inverse

    def feed(self, i):
        rows = pl.ds(pl.multiple_of(i * ROWS, ROWS), ROWS)
        acts = self.acts
        h1 = acts[X, rows, :].astype(F32) + mm(acts[O, rows, :], self.w_m[...]) + row_of(self.mixer_bias)
        n1, r1 = self.normed(h1)
        self.n1[rows, :] = n1.astype(self.n1.dtype)
        self.r1[rows, :] = jnp.broadcast_to(r1, (ROWS, 128))
        y1 = n1 * row_of(self.first_gain) + row_of(self.first_shift)
        self.z[...] = y1 + row_of(self.shrink_bias)
        acts[Y1, rows, :] = y1.astype(BF)
        for j in range(4):
            self.feed_block(rows, j)
        n2, r2 = self.normed(self.z[...])
        self.n2[rows, :] = n2
        self.r2[rows, :] = jnp.broadcast_to(r2, (ROWS, 128))
        each = 512 // ROWS
        s, part = i // each, lax.rem(i, each)
        at = lax.broadcasted_iota(jnp.int32, (ROWS, 1), 0) + part * ROWS
        live = jnp.where(at < self.lengths[s], n2, 0.0)
        some = jnp.sum(live, axis=0, keepdims=True)
        self.n2_sum[s, 0:1, :] = jnp.where(part == 0, some, self.n2_sum[s, 0:1, :] + some)

    def feed_block(self, rows, j):
        acts = self.acts
        cols = pl.ds(768 * j, 768)
        pre = mm(acts[Y1, rows, :], self.w_e[:, cols]) + self.expand_bias[cols].reshape(1, 768)
        cdf, bell = normal_cdf(pre)
        low = (pre * cdf).astype(BF)
        acts[G0 + j, rows, :] = low
        acts[D0 + j, rows, :] = (cdf + pre * bell * 0.3989422804014327).astype(BF)
        self.z[...] += mm(low, self.w_s[cols, :])

    def pool(self, s):
        count = self.lengths[s].astype(F32)
        return self.n2_sum[s, 0:1, :] * row_of(self.second_gain) / count + row_of(self.second_shift)


class Back(Net):
    def share_vectors(self, place, k):
        mine = rows_at(8 * place.c, 8)
        z = place.z
        target = (place.sibling, place.to_x, place.to_y, place.me + 8 - 16 * (z % 2), place.me + 16 - 32 * (z // 2),
                  place.sibling)[k]
        source = self.vec.at[rows_at(8 * (1 - place.c), 8)] if k == 0 else self.vec.at[mine]
        landing = self.vec.at[mine] if k == 5 else self.vec_in.at[k]
        return pltpu.make_async_remote_copy(
            src_ref=source, dst_ref=landing, send_sem=self.vec_sent.at[k], recv_sem=self.vec_came.at[k],
            device_id=(target,), device_id_type=MESH)

    def sum_vectors(self, place, turn):
        mine = rows_at(8 * place.c, 8)
        for k in range(6):
            @pl.when(turn == 76 + 3 * k)
            def _(k=k):
                self.share_vectors(place, k).start()

            @pl.when(turn == 79 + 3 * k)
            def _(k=k):
                copy = self.share_vectors(place, k)
                copy.wait_send()
                copy.wait_recv()
                if k < 5:
                    self.vec[mine, :] += self.vec_in[k]

    def turn_logs(self):
        for s in range(2):
            self.logs_t[s] = jnp.transpose(self.logs[s] + jnp.log(self.sums[s]))[0:16, :]

    ORDER = (12, 4, 13, 11, 3, 5, 14, 10, 2, 6, 15, 9, 1, 7, 8)

    def tell_copy(self, place, s, source, device):
        spot = self.every.at[place.c, source, pl.ds(8 * s, 8)]
        return pltpu.make_async_remote_copy(
            src_ref=spot, dst_ref=spot, send_sem=self.told.at[s, device // 2], recv_sem=self.heard.at[s, source],
            device_id=(device,), device_id_type=MESH)

    def tell(self, place, s):
        c, chip = place.c, place.me // 2
        u = self.pool(s)
        for j in range(6):
            self.every[c, chip, 8 * s + j:8 * s + j + 1, :] = u[:, 128 * j:128 * j + 128]
        self.every[c, chip, 8 * s + 6:8 * s + 8, :] = jnp.full((2, 128), self.targets[s], F32)
        for k in self.ORDER:
            self.tell_copy(place, s, chip, lax.rem(chip + k, 16) * 2 + c).start()

    def gather(self, place):
        c, chip = place.c, place.me // 2
        for s in range(2):
            for k in self.ORDER:
                self.tell_copy(place, s, lax.rem(chip + 16 - k, 16), place.me).wait_recv()
        share = pltpu.make_async_remote_copy(
            src_ref=self.every.at[c], dst_ref=self.every.at[c], send_sem=self.told.at[0, chip],
            recv_sem=self.heard.at[0, chip], device_id=(place.sibling,), device_id_type=MESH)
        share.start()
        for s in range(2):
            for k in self.ORDER:
                self.tell_copy(place, s, chip, lax.rem(chip + k, 16) * 2 + c).wait_send()
        share.wait_send()
        share.wait_recv()

    def partners_of(self, place):
        first = place.me * 2
        wanted = [jnp.full((8, 128), self.partners[first + s], jnp.int32) for s in range(2)]

        def pick(i, found):
            device = i // 2
            tile = self.every[lax.rem(device, 2), device // 2, rows_at(8 * lax.rem(i, 2), 8), :]
            chosen = jnp.full((8, 128), self.partners[i], jnp.int32)
            return tuple(
                old + jnp.where(hit, tile, 0.0)
                for old, hit in zip(found, (wanted[0] == i, chosen == first, wanted[1] == i, chosen == first + 1)))

        return lax.fori_loop(0, 64, pick, (jnp.zeros((8, 128), F32),) * 4, unroll=8)

    def pair(self, place, s, far, near):
        mine = self.every[place.c, place.me // 2, 8 * s:8 * s + 8, :]
        live = lax.broadcasted_iota(jnp.int32, (8, 128), 0) < 6

        def inner(left, right):
            return jnp.sum(jnp.where(live, left * right, 0.0), axis=(0, 1), keepdims=True)

        length = jnp.sqrt(inner(mine, mine) + 1e-6)
        far_length = jnp.sqrt(inner(far, far) + 1e-6)
        near_length = jnp.sqrt(inner(near, near) + 1e-6)
        score = inner(mine, far) / (length * far_length)
        near_score = inner(near, mine) / (near_length * length)
        miss = score - mine[6:7, 0:1]
        near_miss = near_score - near[6:7, 0:1]
        own = mine / (length * length)
        grad = miss * (far / (length * far_length) - score * own)
        grad += near_miss * (near / (near_length * length) - near_score * own)
        for j in range(6):
            self.du[s, 0:1, 128 * j:128 * j + 128] = grad[j:j + 1, :]
        self.scores[s:s + 1, :] = jnp.broadcast_to(score, (1, 128))

    def clear(self):
        self.vec[...] = jnp.zeros_like(self.vec)
        self.logs[...] = jnp.zeros_like(self.logs)
        self.sums[...] = jnp.ones_like(self.sums)

    def add_vec(self, at, rows):
        self.vec[at:at + 1, :] += jnp.sum(rows.astype(F32), axis=0, keepdims=True)

    def second_vectors(self):
        gain = jnp.zeros((1, 768), F32)
        for s in range(2):
            gain += self.du[s, 0:1, :] * self.n2_sum[s, 0:1, :] / self.lengths[s].astype(F32)
        self.vec[6:7, :] = gain
        self.vec[7:8, :] = self.du[0, 0:1, :] + self.du[1, 0:1, :]

    def back_second(self, i):
        rows = pl.ds(pl.multiple_of(i * 256, 256), 256)
        s = i // 2
        up = self.du[s, 0:1, :] * row_of(self.second_gain) / self.lengths[s].astype(F32)
        mean = jnp.sum(up, axis=1, keepdims=True) * (1.0 / 768)
        n2 = self.n2[rows, :]
        along = jnp.sum(n2 * up, axis=1, keepdims=True) * (1.0 / 768)
        at = lax.broadcasted_iota(jnp.int32, (256, 1), 0) + lax.rem(i, 2) * 256
        dh2 = jnp.where(at < self.lengths[s], self.r2[rows, 0:1] * (up - mean - n2 * along), 0.0)
        self.n2[rows, :] = dh2
        dz = dh2.astype(BF)
        self.acts[DZ, rows, :] = dz
        self.add_vec(5, dz)

    def back_hidden(self, i):
        j, half = i // 2, lax.rem(i, 2)
        rows = pl.ds(pl.multiple_of(half * 512, 512), 512)
        units = pl.ds(pl.multiple_of(j * 768, 768), 768)
        df = (mm_nt(self.acts[DZ, rows, :], self.w_s[units, :]) * self.acts[D0 + j, rows, :].astype(F32)).astype(BF)
        self.acts[D0 + j, rows, :] = df
        part = jnp.sum(df.astype(F32), axis=0, keepdims=True)
        line = lax.broadcasted_iota(jnp.int32, (8, 768), 0) == j
        self.vec[8:16, :] += jnp.where(line, part, 0.0)

    def back_first(self, i):
        rows = pl.ds(pl.multiple_of(i * 256, 256), 256)
        acts = self.acts
        up = self.n2[rows, :]
        for j in range(4):
            up += mm_nt(acts[D0 + j, rows, :], self.w_e[:, 768 * j:768 * j + 768])
        n1 = self.n1[rows, :].astype(F32)
        self.add_vec(3, up * n1)
        self.add_vec(4, up)
        dn = up * row_of(self.first_gain)
        mean = jnp.sum(dn, axis=1, keepdims=True) * (1.0 / 768)
        along = jnp.sum(dn * n1, axis=1, keepdims=True) * (1.0 / 768)
        dh1 = self.r1[rows, 0:1] * (dn - mean - n1 * along)
        self.n2[rows, :] = dh1
        da = dh1.astype(BF)
        acts[DA, rows, :] = da
        self.add_vec(2, da)
        acts[DO, rows, :] = mm_nt(da, self.w_m[...]).astype(BF)

    def attend_back(self, i):
        s, head = i // 12, lax.rem(i, 12)
        rows = pl.ds(pl.multiple_of(s * 512, 512), 512)
        lanes = lanes_at((head // 2) * 128, 128)
        acts = self.acts
        lane = lax.broadcasted_iota(jnp.int32, (1, 128), 1)
        live = (lane // 64) == lax.rem(head, 2)
        q_all, k, v = acts[Q, rows, lanes], acts[K, rows, lanes], acts[V, rows, lanes]
        q = jnp.where(live, q_all, BF(0))
        up = jnp.where(live, acts[DO, rows, lanes], BF(0))
        place = lax.broadcasted_iota(jnp.int32, (512, 1), 0)
        off = jnp.where(place < self.lengths[s], 0.0, -1e9)
        probs = jnp.exp(mm_nt(k, q) + off - self.logs_t[s, pl.ds(head, 1), :])
        weighed = probs * mm_nt(v, up)
        delta = jnp.sum(weighed, axis=0, keepdims=True)
        ds = (weighed - probs * delta).astype(BF)
        dv = mm(probs.astype(BF), up)
        dk = mm(ds, q)
        dq = mm_t(ds, k) * 0.125
        acts[Q, rows, lanes] = jnp.where(live, dq.astype(BF), q_all)
        acts[K, rows, lanes] = jnp.where(live, dk.astype(BF), k)
        acts[V, rows, lanes] = jnp.where(live, dv.astype(BF), v)

    def back_tokens(self, i):
        rows = pl.ds(pl.multiple_of(i * 256, 256), 256)
        dq, dk, dv = self.acts[Q, rows, :], self.acts[K, rows, :], self.acts[V, rows, :]
        self.add_vec(0, dq)
        self.add_vec(1, dv)
        self.n2[rows, :] += mm_nt(dq, self.w_q[...]) + mm_nt(dk, self.w_k[...]) + mm_nt(dv, self.w_v[...])

    def back_task(self, i):
        pl.when(i < 8)(lambda: self.back_hidden(i))
        pl.when((i >= 8) & (i < 12))(lambda: self.back_first(i - 8))
        pl.when((i >= 12) & (i < 36))(lambda: self.attend_back(i - 12))
        pl.when((i >= 36) & (i < 40))(lambda: self.back_tokens(i - 36))

    def grad_piece(self, i):
        b = i // 3
        slot = lax.rem(i, 2)
        cols = pl.ds(pl.multiple_of(lax.rem(i, 3) * 256, 256), 256)
        left = jnp.where(b < 4, G0 + b, jnp.where(b < 8, Y1, jnp.where(b < 9, O, X)))
        right = jnp.where(b < 4, DZ, jnp.where(b < 8, D0 + b - 4, jnp.where(b < 9, DA, b)))
        self.ring[slot] = mm_t(self.acts[left, :, cols], self.acts[right])


N_IN = 19
VMEM_LIMIT = 54 << 20
VECTORS = ("query_bias", "value_bias", "mixer_bias", "first_gain", "first_shift", "shrink_bias", "second_gain",
           "second_shift")


def layer_kernel(*refs):
    (tokens, lengths, partners, targets, w_q, query_bias, w_k, w_v, value_bias, w_m, mixer_bias, first_gain,
     first_shift, w_e, expand_bias, w_s, shrink_bias, second_gain, second_shift) = refs[:N_IN]
    scores, late, vec, summed = refs[N_IN:N_IN + 4]
    rest = refs[N_IN + 4:]
    (acts, v_q, v_k, v_v, v_m, v_e, v_s, key_row, logs, sums, logs_t, r1, r2, n2_sum, every, du, vec_in, ring,
     loaded, told, heard, vec_sent, vec_came) = rest[:23]
    n2, n1, z = late.at[pl.ds(0, 1024)], late.at[pl.ds(1024, 1024)], late.at[pl.ds(2048, ROWS)]
    first, second = rest[23:23 + N_STREAM_SCRATCH], rest[23 + N_STREAM_SCRATCH:]
    place = Place()
    net = Back(
        acts=acts, w_q=v_q, w_k=v_k, w_v=v_v, w_m=v_m, w_e=v_e, w_s=v_s, query_bias=query_bias, value_bias=value_bias,
        mixer_bias=mixer_bias, first_gain=first_gain, first_shift=first_shift, expand_bias=expand_bias,
        shrink_bias=shrink_bias, second_gain=second_gain, second_shift=second_shift, lengths=lengths,
        partners=partners, targets=targets, scores=scores, key_row=key_row, logs=logs, sums=sums,
        logs_t=logs_t, n1=n1, r1=r1, n2=n2, r2=r2, z=z, n2_sum=n2_sum, every=every, du=du, vec=vec, ring=ring,
        told=told, heard=heard, vec_in=vec_in, vec_sent=vec_sent, vec_came=vec_came)
    loads = [pltpu.make_async_copy(src, dst, loaded.at[i]) for i, (src, dst) in enumerate([
        (tokens, acts.at[X]), (w_q, v_q), (w_k, v_k), (w_v, v_v), (w_m, v_m), (w_e, v_e), (w_s, v_s)])]
    for copy in loads[:4]:
        copy.start()

    def chunk_rows(t, shift):
        t = jnp.clip(t, 0, 36)
        return lax.rem(t, 2), shift

    def outs(m, shift):
        early = rows_at(jnp.clip(m, 0, 35 - LATE) * 256 + shift, 64)
        last = rows_at(1024 + (jnp.clip(m, 36 - LATE, 35) - (36 - LATE)) * 256 + shift, 64)
        return [(summed.at[early], m < 36 - LATE), (late.at[last], m >= 36 - LATE)]

    one = Stream(place, 0, 36, first, ring, lambda t: chunk_rows(t, 0), outs)
    two = Stream(place, 1, 36, second, ring, lambda t: chunk_rows(t, 128), lambda m, at: outs(m, 128 + at))
    one.prepare()
    two.prepare()
    greet_all(place)

    def each(count, task):
        def step(i, carry):
            task(i)
            return carry

        lax.fori_loop(0, count, step, 0)

    net.masks()
    net.clear()
    loads[0].wait()
    loads[1].wait()
    each(1024 // ROWS, net.project_q)
    loads[2].wait()
    loads[3].wait()
    for copy in loads[4:]:
        copy.start()
    each(1024 // ROWS, net.project_k)
    each(1024 // ROWS, net.project_v)
    each(12, net.attend)
    net.turn_logs()
    for copy in loads[4:]:
        copy.wait()
    await_all()

    def feed_and_tell(i):
        net.feed(i)
        for s in range(2):
            pl.when(i == s)(lambda s=s: net.tell(place, s))

    each(1024 // ROWS, feed_and_tell)
    net.gather(place)
    tiles = net.partners_of(place)
    for s in range(2):
        net.pair(place, s, tiles[2 * s], tiles[2 * s + 1])
    net.second_vectors()
    each(4, net.back_second)

    first_task = 12

    def step(turn, carry):
        t = turn // 2 - 1
        side = lax.rem(turn, 2)

        for i, stream in enumerate((one, two)):
            @pl.when((side == i) & (t >= 0))
            def _(stream=stream):
                stream.wait(t - 1)
                stream.work(t)
                stream.start(t)

        pl.when((side == 1) & (t + 1 < 36))(lambda: net.grad_piece(t + 1))
        task = turn - 2 - first_task
        pl.when((task >= 0) & (task < 40))(lambda: net.back_task(task))
        net.sum_vectors(place, turn)
        return carry

    lax.fori_loop(1, 2 * 47 + 2, step, 0)


def greet_all(place):
    bar = pltpu.get_barrier_semaphore()
    chip = place.me // 2

    def hail(k, carry):
        pl.semaphore_signal(bar, 1, device_id=(lax.rem(chip + k, 16) * 2 + place.c,), device_id_type=MESH)
        return carry

    pl.semaphore_signal(bar, 1, device_id=(place.sibling,), device_id_type=MESH)
    lax.fori_loop(1, 16, hail, 0)


def await_all():
    pl.semaphore_wait(pltpu.get_barrier_semaphore(), 16)


def whole_layer(*args):
    anywhere = pl.BlockSpec(memory_space=pltpu.HBM)
    vector = pl.BlockSpec(memory_space=pltpu.VMEM)
    scalars = pl.BlockSpec(memory_space=pltpu.SMEM)
    specs = [anywhere if a.dtype == BF else vector if a.shape[0] >= 768 else scalars for a in args]

    def low(*shape):
        return pltpu.VMEM(shape, BF)

    def full(*shape):
        return pltpu.VMEM(shape, F32)

    return pl.pallas_call(
        layer_kernel,
        out_shape=(
            pltpu.VMEM((8, 128), F32),
            pltpu.VMEM((1024 + max(1024 + ROWS, 256 * LATE), 768), F32),
            pltpu.VMEM((16, 768), F32),
            jax.ShapeDtypeStruct((256 * (36 - LATE), 768), F32),
        ),
        in_specs=specs,
        out_specs=(vector, vector, vector, pl.BlockSpec(memory_space=pltpu.HBM)),
        scratch_shapes=[
            low(N_ACTS, 1024, 768),
            low(768, 768), low(768, 768), low(768, 768), low(768, 768), low(768, 3072), low(3072, 768),
            full(2, 8, 512), full(2, 512, 128), full(2, 512, 128), full(2, 16, 512),
            full(1024, 128), full(1024, 128), full(2, 8, 768),
            full(2, 16, 16, 128), full(2, 8, 768), full(5, 8, 768), full(2, 256, 768),
            pltpu.SemaphoreType.DMA((7,)), pltpu.SemaphoreType.DMA((2, 16)), pltpu.SemaphoreType.DMA((2, 16)),
            pltpu.SemaphoreType.DMA((6,)), pltpu.SemaphoreType.DMA((6,)),
        ] + stream_scratch() + stream_scratch(),
        compiler_params=pltpu.CompilerParams(
            collective_id=0, has_side_effects=True, vmem_limit_bytes=VMEM_LIMIT),
    )(*args)


def deliver_kernel(count, height, summed, late, small, scores, *refs):
    (scores_out, tokens_out, w_q, query_bias, w_k, w_v, value_bias, w_m, mixer_bias, first_gain, first_shift, w_e,
     expand_bias, w_s, shrink_bias, second_gain, second_shift) = refs[:17]
    buffer, came, left, sent = refs[17:]

    def place(row, size):
        block, at = row // 768, row % 768
        if block < 4:
            return w_s.at[pl.ds(row, size)]
        if block < 8:
            return w_e.at[pl.ds(at, size), pl.ds(768 * (block - 4), 768)]
        return (w_m, w_q, w_k, w_v)[block - 8].at[pl.ds(at, size)]

    early = summed.shape[0]
    direct = [pltpu.make_async_copy(late.at[pl.ds(0, 1024)], tokens_out, sent.at[0])]
    row = early
    while row < 9216:
        size = min(768 - row % 768, 9216 - row)
        direct.append(pltpu.make_async_copy(
            late.at[pl.ds(1024 + row - early, size)], place(row, size), sent.at[len(direct)]))
        row += size
    jobs = []
    row = 0
    while row < early:
        size = min(height, 768 - row % 768, early - row)
        jobs.append((row, size))
        row += size

    def copies(i):
        row, size = jobs[i]
        spot = buffer.at[i % count, pl.ds(0, size)]
        return (pltpu.make_async_copy(summed.at[pl.ds(row, size)], spot, came.at[i % count]),
                pltpu.make_async_copy(spot, place(row, size), left.at[i % count]))

    total = len(jobs)
    ahead = count // 2
    for i in range(min(ahead, total)):
        copies(i)[0].start()
    for copy in direct:
        copy.start()
    for j, ref in enumerate((query_bias, value_bias, mixer_bias, first_gain, first_shift, shrink_bias,
                             second_gain, second_shift)):
        ref[...] = small[j, :]
    for j in range(4):
        expand_bias[768 * j:768 * j + 768] = small[8 + j, :]
    for s in range(2):
        scores_out[s] = jnp.sum(scores[s:s + 1, 0:1])
    for i in range(total):
        copies(i)[0].wait()
        copies(i)[1].start()
        later = i + ahead
        if later < total:
            if later >= count:
                copies(later - count)[1].wait()
            copies(later)[0].start()
    for i in range(max(0, total - count), total):
        copies(i)[1].wait()
    for copy in direct:
        copy.wait()


def fused(*args):
    pair_scores, late, small, summed = whole_layer(*args)
    hbm = pl.BlockSpec(memory_space=pltpu.HBM)
    vector = pl.BlockSpec(memory_space=pltpu.VMEM)
    scalars = pl.BlockSpec(memory_space=pltpu.SMEM)
    shapes = [(2,), (1024, 768), (768, 768), (768,), (768, 768), (768, 768), (768,), (768, 768), (768,), (768,), (768,),
              (768, 3072), (3072,), (3072, 768), (768,), (768,), (768,)]
    count, height = 14, 384
    return tuple(pl.pallas_call(
        partial(deliver_kernel, count, height),
        out_shape=[jax.ShapeDtypeStruct(shape, F32) for shape in shapes],
        in_specs=[hbm, vector, vector, vector],
        out_specs=[hbm if len(shape) == 2 else vector if shape[0] > 2 else scalars for shape in shapes],
        scratch_shapes=[pltpu.VMEM((count, height, 768), F32),
                        pltpu.SemaphoreType.DMA((count,)), pltpu.SemaphoreType.DMA((count,)),
                        pltpu.SemaphoreType.DMA((16,))],
        compiler_params=pltpu.CompilerParams(vmem_limit_bytes=36 << 20),
    )(summed, late, small, pair_scores))


def to_low(value):
    return value.astype(jnp.bfloat16)


def tdot(left, right):
    return lax.dot_general(
        left, right, (((0,), (0,)), ((), ())), preferred_element_type=jnp.float32
    )


def ndot(left, right):
    return lax.dot_general(
        left, right, (((1,), (1,)), ((), ())), preferred_element_type=jnp.float32
    )


def norm_rows(rows, gain, shift):
    mean = jnp.mean(rows, axis=-1, keepdims=True)
    centred = rows - mean
    spread = jnp.mean(centred * centred, axis=-1, keepdims=True)
    inverse = lax.rsqrt(spread + 1e-06)
    normed = centred * inverse
    return (normed * gain + shift, normed, inverse)


def norm_back(upstream, normed, inverse, gain):
    gain_grad = jnp.sum(upstream * normed, axis=0)
    shift_grad = jnp.sum(upstream, axis=0)
    dnormed = upstream * gain
    first_mean = jnp.mean(dnormed, axis=-1, keepdims=True)
    second_mean = jnp.mean(dnormed * normed, axis=-1, keepdims=True)
    return (inverse * (dnormed - first_mean - normed * second_mean), gain_grad, shift_grad)


def per_device(
    tokens,
    lengths,
    partners,
    targets,
    query_proj,
    query_bias,
    key_proj,
    value_proj,
    value_bias,
    mixer_proj,
    mixer_bias,
    first_gain,
    first_shift,
    expand_proj,
    expand_bias,
    shrink_proj,
    shrink_bias,
    second_gain,
    second_shift,
):
    sents = lengths.shape[0]
    rows_all = tokens.shape[0]
    slot = rows_all // sents
    width = tokens.shape[1]
    heads = H
    depth = width // heads
    scale = 1.0 / math.sqrt(depth)
    total = partners.shape[0]
    base = lax.axis_index("dp") * sents
    highest = lax.Precision.HIGHEST
    places = jnp.arange(slot, dtype=jnp.int32)
    valid = places[None, :] < lengths[:, None]
    row_mask = valid.reshape(rows_all, 1).astype(jnp.float32)
    shape4 = (sents, slot, heads, depth)
    queries = to_low(jnp.dot(tokens, query_proj, preferred_element_type=jnp.float32) + query_bias)
    keys = to_low(jnp.dot(tokens, key_proj, preferred_element_type=jnp.float32))
    values = to_low(jnp.dot(tokens, value_proj, preferred_element_type=jnp.float32) + value_bias)
    queries4 = queries.reshape(shape4)
    keys4 = keys.reshape(shape4)
    values4 = values.reshape(shape4)

    def masked_scores(query_rows, key_rows, live):
        raw = (
            jnp.einsum("qhd,khd->hqk", query_rows, key_rows, preferred_element_type=jnp.float32)
            * scale
        )
        return jnp.where(live[None, None, :], raw, -1000000000.0)

    def attend(item):
        query_rows, key_rows, value_rows, live = item
        raw = masked_scores(query_rows, key_rows, live)
        top = jnp.max(raw, axis=-1, keepdims=True)
        expd = jnp.exp(raw - top)
        summed = jnp.sum(expd, axis=-1, keepdims=True)
        probs = to_low(expd / summed)
        mixed = jnp.einsum("hqk,khd->qhd", probs, value_rows, preferred_element_type=jnp.float32)
        return (mixed, (top + jnp.log(summed))[..., 0])

    mixed, logsum = lax.map(attend, (queries4, keys4, values4, valid))
    mixed_low = to_low(mixed.reshape(rows_all, width))
    branch = jnp.dot(mixed_low, mixer_proj, preferred_element_type=jnp.float32) + mixer_bias
    first_out, first_normed, first_inverse = norm_rows(
        tokens.astype(jnp.float32) + branch, first_gain, first_shift
    )
    first_low = to_low(first_out)
    pre = jnp.dot(first_low, expand_proj, preferred_element_type=jnp.float32) + expand_bias
    act, gelu_back = jax.vjp(partial(jax.nn.gelu, approximate=False), pre)
    act_low = to_low(act)
    shrink = jnp.dot(act_low, shrink_proj, preferred_element_type=jnp.float32) + shrink_bias
    outputs, second_normed, second_inverse = norm_rows(
        first_out + shrink, second_gain, second_shift
    )
    counts = lengths.astype(jnp.float32)
    pooled = jnp.sum((outputs * row_mask).reshape(sents, slot, width), axis=1) / counts[:, None]
    mine = lax.dynamic_slice_in_dim(partners, base, sents)
    every = lax.all_gather(pooled, "dp", axis=0, tiled=True)
    partner_vec = jnp.take(every, mine, axis=0)
    inner = jnp.sum(pooled * partner_vec, axis=-1)
    own_len = jnp.sqrt(jnp.sum(pooled * pooled, axis=-1) + 1e-06)
    far_len = jnp.sqrt(jnp.sum(partner_vec * partner_vec, axis=-1) + 1e-06)
    pair_scores = inner / (own_len * far_len)
    miss = pair_scores - targets
    joint = (own_len * far_len)[:, None]
    dpooled = miss[:, None] * (
        partner_vec / joint - (pair_scores / (own_len * own_len))[:, None] * pooled
    )
    dpartner = miss[:, None] * (
        pooled / joint - (pair_scores / (far_len * far_len))[:, None] * partner_vec
    )
    owners = (mine[:, None] == jnp.arange(total, dtype=jnp.int32)[None, :]).astype(jnp.float32)
    spread = lax.dot_general(owners, dpartner, (((0,), (0,)), ((), ())), precision=highest)
    returned = lax.psum_scatter(spread, "dp", scatter_dimension=0, tiled=True)
    dpool_all = (dpooled + returned) / counts[:, None]
    doutputs = (dpool_all[:, None, :] * valid[:, :, None].astype(jnp.float32)).reshape(
        rows_all, width
    )
    dsecond, second_gain_grad, second_shift_grad = norm_back(
        doutputs, second_normed, second_inverse, second_gain
    )
    dshrink = to_low(dsecond)
    shrink_proj_grad = tdot(act_low, dshrink)
    shrink_bias_grad = jnp.sum(dshrink.astype(jnp.float32), axis=0)
    dact = ndot(dshrink, shrink_proj)
    dpre = to_low(gelu_back(dact)[0])
    expand_proj_grad = tdot(first_low, dpre)
    expand_bias_grad = jnp.sum(dpre.astype(jnp.float32), axis=0)
    dfirst_out = ndot(dpre, expand_proj) + dsecond
    dfirst, first_gain_grad, first_shift_grad = norm_back(
        dfirst_out, first_normed, first_inverse, first_gain
    )
    dbranch = to_low(dfirst)
    mixer_proj_grad = tdot(mixed_low, dbranch)
    mixer_bias_grad = jnp.sum(dbranch.astype(jnp.float32), axis=0)
    dmixed = to_low(ndot(dbranch, mixer_proj)).reshape(shape4)

    def attend_back(item):
        query_rows, key_rows, value_rows, live, row_logsum, dmix = item
        raw = masked_scores(query_rows, key_rows, live)
        probs = jnp.exp(raw - row_logsum[..., None])
        probs_low = to_low(probs)
        dprob = jnp.einsum("qhd,khd->hqk", dmix, value_rows, preferred_element_type=jnp.float32)
        delta = jnp.sum(dprob * probs, axis=-1, keepdims=True)
        dscore = to_low(probs * (dprob - delta))
        dquery = (
            jnp.einsum("hqk,khd->qhd", dscore, key_rows, preferred_element_type=jnp.float32) * scale
        )
        dkey = (
            jnp.einsum("hqk,qhd->khd", dscore, query_rows, preferred_element_type=jnp.float32)
            * scale
        )
        dvalue = jnp.einsum("hqk,qhd->khd", probs_low, dmix, preferred_element_type=jnp.float32)
        return (to_low(dquery), to_low(dkey), to_low(dvalue))

    dquery, dkey, dvalue = lax.map(attend_back, (queries4, keys4, values4, valid, logsum, dmixed))
    dquery = dquery.reshape(rows_all, width)
    dkey = dkey.reshape(rows_all, width)
    dvalue = dvalue.reshape(rows_all, width)
    query_proj_grad = tdot(tokens, dquery)
    query_bias_grad = jnp.sum(dquery.astype(jnp.float32), axis=0)
    key_proj_grad = tdot(tokens, dkey)
    value_proj_grad = tdot(tokens, dvalue)
    value_bias_grad = jnp.sum(dvalue.astype(jnp.float32), axis=0)
    tokens_grad = (
        ndot(dquery, query_proj) + ndot(dkey, key_proj) + ndot(dvalue, value_proj) + dfirst
    )
    (
        query_proj_grad,
        query_bias_grad,
        key_proj_grad,
        value_proj_grad,
        value_bias_grad,
        mixer_proj_grad,
        mixer_bias_grad,
        first_gain_grad,
        first_shift_grad,
        expand_proj_grad,
        expand_bias_grad,
        shrink_proj_grad,
        shrink_bias_grad,
        second_gain_grad,
        second_shift_grad,
    ) = lax.psum(
        (
            query_proj_grad,
            query_bias_grad,
            key_proj_grad,
            value_proj_grad,
            value_bias_grad,
            mixer_proj_grad,
            mixer_bias_grad,
            first_gain_grad,
            first_shift_grad,
            expand_proj_grad,
            expand_bias_grad,
            shrink_proj_grad,
            shrink_bias_grad,
            second_gain_grad,
            second_shift_grad,
        ),
        "dp",
    )
    return (
        pair_scores,
        tokens_grad,
        query_proj_grad,
        query_bias_grad,
        key_proj_grad,
        value_proj_grad,
        value_bias_grad,
        mixer_proj_grad,
        mixer_bias_grad,
        first_gain_grad,
        first_shift_grad,
        expand_proj_grad,
        expand_bias_grad,
        shrink_proj_grad,
        shrink_bias_grad,
        second_gain_grad,
        second_shift_grad,
    )


def solution(mesh):
    in_specs = (
        P("dp", None),
        P("dp"),
        P(),
        P("dp"),
        P(),
        P(),
        P(),
        P(),
        P(),
        P(),
        P(),
        P(),
        P(),
        P(),
        P(),
        P(),
        P(),
        P(),
        P(),
    )
    out_specs = (
        P("dp"),
        P("dp", None),
        P(),
        P(),
        P(),
        P(),
        P(),
        P(),
        P(),
        P(),
        P(),
        P(),
        P(),
        P(),
        P(),
        P(),
        P(),
    )
    plain = mesh.shape["dp"] != 32
    return jax.shard_map(
        per_device if plain else fused, mesh=mesh, in_specs=in_specs, out_specs=out_specs, check_vma=False
    )
```
